32 devices in a mesh: mem: 8 (over y, x, core), lat: 4 (over z).
Axes of the slice: x: 2, y: 2, z: 4, core: 2. Of those that a mesh axis runs over, the one named last changes fastest.
Arguments:
- ensemble: float32 [256, 4, 16, 1024], P('mem', None, 'lat'), may hold values from -6 to 6
- obs_value: float32 [1, 32, 16], P(None, ('mem', 'lat')), may hold values from -9 to 9
- obs_var: float32 [1, 32, 16], P(None, ('mem', 'lat')), may hold values from 0.5 to 4
- obs_cell: int32 [1, 32, 16], P(None, ('mem', 'lat')), may hold values from 0 to 2047
- obs_loop: int32 [1, 32, 16], P(None, ('mem', 'lat')), may hold values from 0 to 3
- obs_count: int32 [1, 32], P(None, ('mem', 'lat')), may hold values from 8 to 16, as said below
Outputs:
- analysis: float32 [256, 4, 16, 1024], P('mem', None, 'lat')
The draws below stay inside these ranges and needn't reach their ends.
Inputs may be any that keep to these rules, and one draw needn't show every extreme that they name: `obs_count`: at least 8 and at most 16 slots live per patch; in each cycle some patch has all 16 slots live and another exactly 8.
All inputs are finite; a program needn't handle non-finite values.
Results may differ from the reference program's by a relative error of at most 0.0003.
Values sent between devices are 32-bit elements; how exact they have to be, the bound alone decides.
No kernel may reach another device: no remote copies, remote signals or barrier semaphores. Data moves between devices by JAX's collectives and lax.ppermute only.
A program may use at most 64 MiB of HBM per device.

```python
import math
import jax
import jax.numpy as jnp
from jax import lax

K = 256
F = 4
NX = 1024
ROWS = 4
NOBS = 16
NCYC = 1
STEPS = 1
NSI = 5
NY = 16
NPATCH = 32
CELLS = 2048
N_MEM = 8
N_LAT = 4


def draw_obs_count(key, part):
    key_base, key_top, key_offset = jax.random.split(jax.random.fold_in(key, 7), 3)
    base = jax.random.randint(key_base, (NCYC, NPATCH), NOBS // 2, NOBS + 1)
    top_patch = jax.random.randint(key_top, (NCYC,), 0, NPATCH)
    offset = jax.random.randint(key_offset, (NCYC,), 1, NPATCH)
    low_patch = (top_patch + offset) % NPATCH
    patch_index = jnp.arange(NPATCH)[None, :]
    base = jnp.where(patch_index == top_patch[:, None], NOBS, base)
    base = jnp.where(patch_index == low_patch[:, None], NOBS // 2, base)
    return base.astype(jnp.int32)


def with_ends(values, stream_key, least, largest):
    shape = values.shape
    place = [jax.random.randint(jax.random.fold_in(stream_key, axis), (), 0, shape[axis]) for axis in range(len(shape))]
    values = values.at[tuple(place)].set(least)
    longest = shape.index(max(shape))
    place[longest] = (place[longest] + 1) % shape[longest]
    return values.at[tuple(place)].set(largest)


def level_of(own_key, extent, cuts, least, top_value):
    level = 1.0
    for position, blocks in cuts:
        heights = jax.random.uniform(jax.random.fold_in(jax.random.fold_in(own_key, 6), position), (blocks,), jnp.float32, least / len(cuts), top_value / len(cuts))
        level = level * jnp.repeat(jnp.exp(heights), extent[position] // blocks).reshape((-1,) + (1,) * (len(extent) - 1 - position))
    return level


def normal_values(rng, dims, deviation, most, pieces=(), held_as=jnp.bfloat16):
    values = deviation * jax.random.normal(rng, dims, jnp.float32)
    if pieces:
        values = values * level_of(rng, dims, pieces, -0.22, 0.18)
    return jnp.clip(values, -most, most).astype(held_as)


def setup_inputs(seed: int = 0) -> dict:
    splits = jax.random.split(jax.random.key(seed), 7)
    return {
        "ensemble": normal_values(splits[0], (K, F, NY, NX), 1.0, 6.0, ((0, 8), (2, 4)), jnp.float32),
        "obs_value": normal_values(splits[1], (NCYC, NPATCH, NOBS), 1.5, 9.0, ((1, 32),), jnp.float32),
        "obs_var": jnp.clip(jnp.exp(math.log(4.0) - 2.0794415 * jax.random.uniform(splits[2], (NCYC, NPATCH, NOBS), jnp.float32) ** level_of(splits[2], (NCYC, NPATCH, NOBS), ((1, 32),), -0.2, 0.2)), 0.5, 4.0),
        "obs_cell": with_ends(jax.random.randint(splits[3], (NCYC, NPATCH, NOBS), 0, CELLS), jax.random.fold_in(splits[3], 1), 0, CELLS - 1).astype(jnp.int32),
        "obs_loop": with_ends(jax.random.randint(splits[4], (NCYC, NPATCH, NOBS), 0, 4), jax.random.fold_in(splits[4], 1), 0, 3).astype(jnp.int32),
        "obs_count": draw_obs_count(jax.random.fold_in(splits[6], 71), 0),
    }


time_step = 0.15
viscosity = 0.1
third_part = 1.0 / 3.0
two_thirds = 2.0 / 3.0

def tendency(padded):
    centre = padded[:, :, 1:-1, 1:-1]
    to_north = padded[:, :, 2:, 1:-1]
    to_south = padded[:, :, :-2, 1:-1]
    to_east = padded[:, :, 1:-1, 2:]
    to_west = padded[:, :, 1:-1, :-2]
    zonal_wind = centre[:, 0:1]
    meridional = centre[:, 1:2]
    moved = zonal_wind * (to_east - to_west) * 0.5 + meridional * (to_north - to_south) * 0.5
    return -moved + viscosity * (to_north + to_south + to_east + to_west - 4.0 * centre)

def extend_fixed(state):
    padded = jnp.pad(state, ((0, 0), (0, 0), (1, 1), (0, 0)))
    return jnp.concatenate([padded[..., -1:], padded, padded[..., :1]], axis=3)

def advance(state):
    first = state + time_step * tendency(extend_fixed(state))
    second = 0.75 * state + 0.25 * (first + time_step * tendency(extend_fixed(first)))
    return third_part * state + two_thirds * (second + time_step * tendency(extend_fixed(second)))

def analyse(cells, values, variance, slot_cell, slot_loop, count):
    members = cells.shape[0]
    highest = lax.Precision.HIGHEST
    centre_mean = lax.optimization_barrier(jnp.mean(cells, axis=0))
    perturb = cells - centre_mean
    seen = jnp.take(cells, slot_cell, axis=1)
    seen_mean = lax.optimization_barrier(jnp.mean(seen, axis=0))
    seen_pert = seen - seen_mean
    slots = jnp.arange(slot_cell.shape[0], dtype=jnp.int32)
    weight = jnp.where(slots < count, jnp.exp(-0.35 * slot_loop.astype(cells.dtype)) / variance, 0.0)
    scaled = seen_pert * weight
    gram = jnp.dot(scaled, seen_pert.T, precision=highest)
    drive = jnp.dot(scaled, values - seen_mean, precision=highest)
    identity = jnp.eye(members, dtype=cells.dtype)
    bound = members - 1.0 + 0.5 * jnp.trace(gram)
    root_up = ((members - 1.0) * identity + gram) / bound
    root_down = identity
    for repeat in range(NSI):
        factor = 1.5 * identity - 0.5 * jnp.dot(root_down, root_up, precision=highest)
        root_up = jnp.dot(root_up, factor, precision=highest)
        root_down = jnp.dot(factor, root_down, precision=highest)
    spread = root_down * jnp.sqrt((members - 1.0) / bound)
    centre_shift = jnp.dot(root_down, jnp.dot(root_down, drive, precision=highest), precision=highest) / bound
    transform = spread + centre_shift[:, None]
    return centre_mean + jnp.dot(transform.T, perturb, precision=highest)

def reference(ensemble, obs_value, obs_var, obs_cell, obs_loop, obs_count):
    state = ensemble
    members, fields, rows_all, columns = state.shape
    lon_part = columns // N_MEM

    def one_patch(packed):
        return analyse(*packed)
    for cycle_index in range(NCYC):
        for repeat in range(STEPS):
            state = advance(state)
        blocks = state.reshape(members, fields, N_LAT, ROWS, N_MEM, lon_part)
        blocks = blocks.transpose(4, 2, 0, 1, 3, 5).reshape(N_MEM * N_LAT, members, fields * ROWS * lon_part)
        result = lax.map(one_patch, (blocks, obs_value[cycle_index], obs_var[cycle_index], obs_cell[cycle_index], obs_loop[cycle_index], obs_count[cycle_index]))
        result = result.reshape(N_MEM, N_LAT, members, fields, ROWS, lon_part)
        state = result.transpose(2, 3, 1, 4, 0, 5).reshape(members, fields, rows_all, columns)
    return state
```

```python
import functools

import jax
import jax.numpy as jnp
from jax import lax
from jax.experimental import pallas as pl
from jax.experimental.pallas import tpu as pltpu
from jax.sharding import PartitionSpec as P

NSI = 5
HALO = 3
LANES = 128
SUB = 8

time_step = 0.15
viscosity = 0.1
third_part = 1.0 / 3.0
two_thirds = 2.0 / 3.0

HIGHEST = lax.Precision.HIGHEST
VMEM = pl.BlockSpec(memory_space=pltpu.VMEM)
SMEM = pl.BlockSpec(memory_space=pltpu.SMEM)
KERNEL_VMEM = 24 << 20


def call(kernel, out_shape, in_specs, scratch=(), cost=(1 << 20, 1 << 20), name=None):
    flops, nbytes = cost
    return pl.pallas_call(
        kernel,
        out_shape=out_shape,
        in_specs=in_specs,
        out_specs=jax.tree.map(lambda _: VMEM, out_shape),
        scratch_shapes=list(scratch),
        compiler_params=pltpu.CompilerParams(vmem_limit_bytes=KERNEL_VMEM),
        cost_estimate=pl.CostEstimate(flops=flops, bytes_accessed=nbytes, transcendentals=0),
        name=name,
    )


class Plan:
    def __init__(self, ensemble, slots, groups):
        self.members, self.fields, self.rows, self.columns = ensemble.shape
        self.total = self.members * groups
        self.slots = slots
        self.groups = groups
        self.width = self.columns // groups
        self.tiles = self.columns // LANES
        chunks = min(4, self.tiles)
        while self.tiles % chunks or (self.columns // chunks) % self.width:
            chunks -= 1
        self.chunks = chunks
        self.nt = self.tiles // chunks
        self.np = self.columns // chunks // self.width
        self.halves = 2
        self.hrows = self.rows // self.halves
        self.hrf = self.hrows * self.fields
        self.edge_groups = HALO * self.fields
        self.per_edge = LANES // (2 * HALO)
        self.edge_tiles = -(-self.edge_groups // self.per_edge)
        self.message = self.nt * self.edge_groups + self.edge_tiles
        self.q = max(1, LANES // self.width)
        self.plain = -(-self.hrf // SUB) * SUB
        self.block = self.hrf * slots + self.plain
        self.total_rows = self.nt * self.block

    def patches_of(self, tile):
        if self.width >= LANES:
            return [(tile * LANES // self.width, 0, LANES)]
        return [(tile * self.q + i, i * self.width, (i + 1) * self.width) for i in range(self.q)]


def lane_ids(shape):
    return lax.broadcasted_iota(jnp.int32, shape, len(shape) - 1)


def pack_kernel(plan, raw, state, *messages):
    p = plan
    lane = lane_ids((SUB, LANES))

    def body(kk, carry):
        mem = pl.ds(pl.multiple_of(kk * SUB, SUB), SUB)
        for t in range(p.tiles):
            c, i = divmod(t, p.nt)
            up, down = messages[2 * c], messages[2 * c + 1]
            for f in range(p.fields):
                for r in range(p.rows):
                    x = raw[mem, f, r, t * LANES : (t + 1) * LANES]
                    state[t, r, f, mem, :] = x
                    if r >= p.rows - HALO:
                        up[(i * HALO + r - (p.rows - HALO)) * p.fields + f, mem, :] = x
                    if r < HALO:
                        down[(i * HALO + r) * p.fields + f, mem, :] = x
        for c in range(p.chunks):
            after = (c + 1) * p.nt % p.tiles
            before = (c * p.nt - 1) % p.tiles
            for d in range(2):
                out = messages[2 * c + d]
                for e in range(p.edge_tiles):
                    packed = jnp.zeros((SUB, LANES), jnp.float32)
                    for g in range(e * p.per_edge, min((e + 1) * p.per_edge, p.edge_groups)):
                        i, f = divmod(g, p.fields)
                        r = i + (p.rows - HALO if d == 0 else 0)
                        edge = jnp.where(lane < LANES // 2, state[after, r, f, mem, :], state[before, r, f, mem, :])
                        place = (g - e * p.per_edge) * 2 * HALO
                        inside = (lane >= place) & (lane < place + 2 * HALO)
                        packed = jnp.where(inside, pltpu.roll(edge, place + HALO, 1), packed)
                    out[p.nt * p.edge_groups + e, mem, :] = packed
        return carry

    lax.fori_loop(0, p.members // SUB, body, 0)


def step_once(p, rows_in, load, store, last):
    lane = lane_ids((SUB, LANES))
    ring = p.nt + 1
    out_tiles = p.nt if last else ring
    for row in range(1, rows_in - 1):
        coef = []
        for t in range(out_tiles):
            u = load(row, 0, t) * (time_step * 0.5)
            v = load(row, 1, t) * (time_step * 0.5)
            k = time_step * viscosity
            coef.append((k - u, k + u, k - v, k + v))
        for f in range(p.fields):
            x = [load(row, f, t) for t in range(ring)]
            right = [pltpu.roll(a, 1, 1) for a in x]
            left = [pltpu.roll(a, LANES - 1, 1) for a in x]
            for t in range(out_tiles):
                west = jnp.where(lane == 0, right[(t - 1) % ring], right[t])
                east = jnp.where(lane == LANES - 1, left[(t + 1) % ring], left[t])
                ce, cw, cn, cs = coef[t]
                moved = (ce * east + cw * west) + (cn * load(row + 1, f, t) + cs * load(row - 1, f, t))
                store(row, f, t, x[t], (1.0 - 4.0 * time_step * viscosity) * x[t] + moved)


def forecast_kernel(plan, chunk, obs_cell, flags, state, low, high, ahead, seen, keep, send, s0, s1, s2):
    p = plan
    ring = p.nt + 1
    full = p.rows + 2 * HALO
    after = (chunk + 1) * p.nt % p.tiles
    before = (chunk * p.nt - 1) % p.tiles
    has_low = flags[0].astype(jnp.float32)
    has_high = flags[1].astype(jnp.float32)
    core = flags[2]
    lane = lane_ids((SUB, LANES))

    def body(kk, carry):
        mem = pl.ds(pl.multiple_of(kk * SUB, SUB), SUB)

        def edge_of(source, g):
            e, place = divmod(g, p.per_edge)
            return pltpu.roll(source[p.nt * p.edge_groups + e, mem, :], (LANES - HALO - place * 2 * HALO) % LANES, 1)

        for f in range(p.fields):
            for r in range(p.rows):
                s0[r + HALO, f, p.nt] = jnp.where(lane < LANES // 2, state[after, r, f, mem, :], state[before, r, f, mem, :])
            for i in range(HALO):
                s0[i, f, p.nt] = edge_of(low, i * p.fields + f)
                s0[HALO + p.rows + i, f, p.nt] = edge_of(high, i * p.fields + f)

        def load0(row, f, t):
            if t == p.nt:
                return s0[row, f, t]
            if row < HALO:
                return low[(t * HALO + row) * p.fields + f, mem, :]
            if row >= HALO + p.rows:
                return high[(t * HALO + row - HALO - p.rows) * p.fields + f, mem, :]
            return state[chunk * p.nt + t, row - HALO, f, mem, :]

        def keep_zero(row, value):
            if row < HALO:
                return value * has_low
            if row >= HALO + p.rows:
                return value * has_high
            return value

        def load1(row, f, t):
            return s1[row, f, t]

        def load2(row, f, t):
            return s2[row, f, t]

        def store1(row, f, t, x, stepped):
            s1[row, f, t] = keep_zero(row, stepped)

        def store2(row, f, t, x, stepped):
            row = row + 1
            s2[row, f, t] = keep_zero(row, 0.75 * load0(row, f, t) + 0.25 * stepped)

        def store3(row, f, t, x, stepped):
            row = row + 2
            ahead[t, row - HALO, f, mem, :] = third_part * load0(row, f, t) + two_thirds * stepped

        step_once(p, full, load0, store1, False)
        step_once(p, full - 2, lambda row, f, t: s1[row + 1, f, t], store2, False)
        step_once(p, full - 4, lambda row, f, t: s2[row + 2, f, t], store3, True)
        return carry

    lax.fori_loop(0, p.members // SUB, body, 0)

    wide = lane_ids((p.members, LANES))
    for j in range(p.np):
        found = jnp.zeros((p.members, LANES), jnp.float32)
        for o in range(p.slots):
            cell = obs_cell[(chunk * p.np + j) * p.slots + o]
            f = cell // (p.rows * p.width)
            r = cell // p.width % p.rows
            column = cell % p.width + j * p.width
            tile = ahead[column // LANES, r, f]
            shift = (o - column % LANES + LANES) % LANES
            found = jnp.where(wide == o, pltpu.roll(tile, shift, 1), found)
        seen[j] = found

    last = lax.broadcasted_iota(jnp.int32, (SUB, p.members), 0)
    ones = jnp.where(last == 0, 1.0, 0.0).astype(jnp.float32)
    sides = [jnp.concatenate([jnp.transpose(seen[j])[: p.slots], ones], axis=0) for j in range(p.np)]
    for side in range(p.halves):
        out = keep if side == 0 else send
        half = core if side == 0 else 1 - core
        for t in range(p.nt):
            base = t * p.block
            tiles = [ahead[t, half * p.hrows + i // p.fields, i % p.fields] for i in range(p.hrf)]
            joined = jnp.concatenate(tiles, axis=1)
            result = None
            for j, first, stop in p.patches_of(t):
                part = jnp.dot(sides[j], joined, precision=HIGHEST, preferred_element_type=jnp.float32)
                if result is None:
                    result = part
                else:
                    at = lane_ids(part.shape) % LANES
                    result = jnp.where((at >= first) & (at < stop), part, result)
            for i in range(p.hrf):
                piece = result[:, i * LANES : (i + 1) * LANES]
                out[pl.ds(base + i * p.slots, p.slots), :] = piece[: p.slots]
                out[pl.ds(base + p.hrf * p.slots + i, 1), :] = piece[p.slots : p.slots + 1]
            for i in range(p.hrf, p.plain):
                out[pl.ds(base + p.hrf * p.slots + i, 1), :] = jnp.zeros((1, LANES), jnp.float32)


def finish_kernel(plan, chunk, obs_cell, flags, obs, ahead, seen, own, other, new):
    p = plan
    n = p.slots
    core = flags[2]
    free = p.total - 1.0
    row_of = lax.broadcasted_iota(jnp.int32, (n, n), 0)
    col_of = lax.broadcasted_iota(jnp.int32, (n, n), 1)
    eye = jnp.where(row_of == col_of, 1.0, 0.0).astype(jnp.float32)
    lane_row = lane_ids((1, LANES))
    lane_mat = lane_ids((n, LANES))

    def column(row):
        return jnp.sum(eye * row, axis=1, keepdims=True)

    def dot(a, b):
        return jnp.dot(a, b, precision=HIGHEST, preferred_element_type=jnp.float32)

    factors = []
    for j in range(p.np):
        moments = jnp.zeros((n, LANES), jnp.float32)
        sums = jnp.zeros((1, LANES), jnp.float32)
        for o in range(n):
            cell = obs_cell[(chunk * p.np + j) * n + o]
            f = cell // (p.rows * p.width)
            r = cell // p.width % p.rows
            col = cell % p.width + j * p.width
            base = col // LANES * p.block
            index = r % p.hrows * p.fields + f
            half = r // p.hrows
            shift = (o - col % LANES + LANES) % LANES
            at = pl.multiple_of(base + index * n, SUB)
            a = own[pl.ds(at, n), :]
            b = other[pl.ds(at, n), :]
            value = jnp.where(half == core, a, b)
            moments = jnp.where(lane_mat == o, pltpu.roll(value, shift, 1), moments)
            plain = base + p.hrf * n + index
            value = jnp.where(half == core, own[pl.ds(plain, 1), :], other[pl.ds(plain, 1), :])
            sums = jnp.where(lane_row == o, pltpu.roll(jnp.broadcast_to(value, (SUB, LANES)), shift, 1)[:1], sums)
        mean = sums[:, :n] * (1.0 / p.total)
        mean_col = column(mean)
        gram = moments[:, :n] - p.total * mean_col * mean
        patch = chunk * p.np + j
        value, variance, loop, count = (obs[patch, i : i + 1, :n] for i in range(4))
        slot = lax.broadcasted_iota(jnp.int32, (1, n), 1).astype(jnp.float32)
        weight = jnp.where(slot < count, jnp.exp(-0.35 * loop) / variance, 0.0)
        root = jnp.sqrt(weight)
        root_col = column(root)
        scaled = root_col * gram * root
        bound = free + 0.5 * jnp.sum(jnp.sum(scaled * eye, axis=1, keepdims=True), axis=0, keepdims=True)
        inverse = 1.0 / bound
        y0 = free * inverse
        yg = eye * inverse
        yf = y0 * eye + scaled * inverse
        z0 = jnp.ones((1, 1), jnp.float32)
        zg = jnp.zeros((n, n), jnp.float32)
        zf = eye
        for repeat in range(NSI):
            if repeat == 0:
                tf, tg = yf, yg
            else:
                both = dot(jnp.concatenate([zf, zg], axis=0), yf)
                tf, tg = both[:n], z0 * yg + both[n:]
            f0 = 1.5 - 0.5 * z0 * y0
            fg = -0.5 * tg
            ff = 1.5 * eye - 0.5 * tf
            if repeat == 0:
                both = dot(jnp.concatenate([yf, yg], axis=0), ff)
                yf, yg = both[:n], y0 * fg + both[n:]
                zf, zg = ff, fg
            elif repeat < NSI - 1:
                both = dot(jnp.concatenate([yf, yg, zf, zg], axis=0), ff)
                yf, yg = both[:n], y0 * fg + both[n : 2 * n]
                zf, zg = both[2 * n : 3 * n], z0 * fg + both[3 * n :]
            else:
                both = dot(jnp.concatenate([zf, zg], axis=0), ff)
                zf, zg = both[:n], z0 * fg + both[n:]
            y0 = y0 * f0
            z0 = z0 * f0
        scale = jnp.sqrt(free * inverse)
        spread = scale * root_col * zg * root
        drive = root * (value - mean)
        down = jnp.sum(zf * column(drive), axis=0, keepdims=True)
        down = jnp.sum(zf * column(down), axis=0, keepdims=True)
        shift_row = root * down * inverse
        pert = seen[j][:, :n] - mean
        weights = dot(pert, spread) + shift_row
        factors.append((weights, mean_col, scale * z0))

    for t in range(p.nt):
        for half in range(p.halves):
            at_own = half == core
            pieces = []
            for i in range(p.hrf):
                at = t * p.block + i * n
                pieces.append(jnp.where(at_own, own[at : at + n, :], other[at : at + n, :]))
            base = t * p.block + p.hrf * n
            plain = jnp.where(at_own, own[base : base + p.plain, :], other[base : base + p.plain, :])
            results = []
            for j, first, stop in p.patches_of(t):
                weights, mean_col, spread0 = factors[j]
                centred = [pieces[i] - mean_col * plain[i : i + 1, :] for i in range(p.hrf)]
                update = dot(weights, jnp.concatenate(centred, axis=1))
                results.append((update, spread0, first, stop))
            for i in range(p.hrf):
                r, f = half * p.hrows + i // p.fields, i % p.fields
                x = ahead[t, r, f]
                mean = plain[i : i + 1, :] * (1.0 / p.total)
                final = None
                for update, spread0, first, stop in results:
                    part = mean + spread0 * (x - mean) + update[:, i * LANES : (i + 1) * LANES]
                    if final is None:
                        final = part
                    else:
                        at = lane_ids(part.shape)
                        final = jnp.where((at >= first) & (at < stop), part, final)
                new[t, r, f] = final


def total_over_members(plan, keep, send):
    p = plan
    pairs = [(i, i ^ 1) for i in range(p.groups)]
    chip = keep + lax.ppermute(send, "mem", pairs)
    chips = p.groups // 2
    if chips <= 4 and chips & (chips - 1) == 0:
        total = chip
        for step in range(chips - 1, 0, -1):
            total = total + lax.ppermute(chip, "mem", [(i, i ^ (2 * step)) for i in range(p.groups)])
    else:
        same = [[2 * i + core for i in range(chips)] for core in range(2)]
        total = lax.psum(chip, "mem", axis_index_groups=same)
    return total, lax.ppermute(total, "mem", pairs)


def per_device(ensemble, obs_value, obs_var, obs_cell, obs_loop, obs_count):
    groups = lax.axis_size("mem")
    bands = lax.axis_size("lat")
    slots = obs_cell.shape[-1]
    p = Plan(ensemble, slots, groups)
    f32 = jnp.float32
    shape = jax.ShapeDtypeStruct

    out = call(
        functools.partial(pack_kernel, p),
        [shape((p.tiles, p.rows, p.fields, p.members, LANES), f32)]
        + [shape((p.message, p.members, LANES), f32)] * (2 * p.chunks),
        [VMEM],
        name="pack",
    )(ensemble)
    state, messages = out[0], out[1:]
    up = [(i, i + 1) for i in range(bands - 1)]
    down = [(i + 1, i) for i in range(bands - 1)]
    low, high = [], []
    for c in range(p.chunks):
        low.append(lax.ppermute(messages[2 * c], "lat", up))
        high.append(lax.ppermute(messages[2 * c + 1], "lat", down))

    mine = jnp.concatenate(
        [
            obs_value[0],
            obs_var[0],
            obs_loop[0].astype(f32),
            jnp.broadcast_to(obs_count[0][:, None].astype(f32), (1, slots)),
            obs_cell[0].astype(f32),
        ],
        axis=1,
    )
    every = lax.all_gather(mine, "mem", axis=0, tiled=True).reshape(groups, 5, slots)
    cells = every[:, 4].astype(jnp.int32).reshape(groups * slots)
    obs = jnp.pad(every[:, :4], ((0, 0), (0, SUB - 4), (0, LANES - slots)))

    band = lax.axis_index("lat")
    core = lax.rem(lax.axis_index("mem"), 2)
    flags = jnp.stack([(band > 0).astype(jnp.int32), (band < bands - 1).astype(jnp.int32), core.astype(jnp.int32)])

    new = []
    for c in range(p.chunks):
        stage = (p.rows + 2 * HALO, p.fields, p.nt + 1, SUB, LANES)
        ahead, seen, keep, send = call(
            functools.partial(forecast_kernel, p, c),
            [
                shape((p.nt, p.rows, p.fields, p.members, LANES), f32),
                shape((p.np, p.members, LANES), f32),
                shape((p.total_rows, LANES), f32),
                shape((p.total_rows, LANES), f32),
            ],
            [SMEM, SMEM, VMEM, VMEM, VMEM],
            [pltpu.VMEM(stage, f32)] * 3,
            name="forecast",
        )(cells, flags, state, low[c], high[c])
        own, other = total_over_members(p, keep, send)
        new.append(
            call(
                functools.partial(finish_kernel, p, c),
                shape((p.nt, p.rows, p.fields, p.members, LANES), f32),
                [SMEM, SMEM, VMEM, VMEM, VMEM, VMEM, VMEM],
                name="finish",
            )(cells, flags, obs, ahead, seen, own, other)
        )
    joined = jnp.concatenate(new, axis=0)
    return joined.transpose(3, 2, 1, 0, 4).reshape(p.members, p.fields, p.rows, p.columns)


def solution(mesh):
    placed = (
        P("mem", None, "lat", None),
        P(None, ("mem", "lat"), None),
        P(None, ("mem", "lat"), None),
        P(None, ("mem", "lat"), None),
        P(None, ("mem", "lat"), None),
        P(None, ("mem", "lat")),
    )
    return jax.shard_map(
        per_device,
        mesh=mesh,
        in_specs=placed,
        out_specs=P("mem", None, "lat", None),
        check_vma=False,
    )
```

```python
import copy
import functools

import jax
import jax.numpy as jnp
from jax import lax
from jax.experimental import pallas as pl
from jax.experimental.pallas import tpu as pltpu
from jax.sharding import PartitionSpec as P

NSI = 5
HALO = 3
LANES = 128
SUB = 8

time_step = 0.15
viscosity = 0.1
third_part = 1.0 / 3.0
two_thirds = 2.0 / 3.0

HIGHEST = lax.Precision.HIGHEST
VMEM = pl.BlockSpec(memory_space=pltpu.VMEM)
SMEM = pl.BlockSpec(memory_space=pltpu.SMEM)
HBM = pl.BlockSpec(memory_space=pltpu.HBM)
KERNEL_VMEM = 10 << 20


def call(kernel, out_shape, in_specs, scratch=(), cost=(1 << 20, 1 << 20), name=None, out_spec=VMEM, alias={}):
    flops, nbytes = cost
    return pl.pallas_call(
        kernel,
        out_shape=out_shape,
        in_specs=in_specs,
        out_specs=jax.tree.map(lambda _: out_spec, out_shape),
        scratch_shapes=list(scratch),
        input_output_aliases=alias,
        compiler_params=pltpu.CompilerParams(vmem_limit_bytes=KERNEL_VMEM),
        cost_estimate=pl.CostEstimate(flops=flops, bytes_accessed=nbytes, transcendentals=0),
        name=name,
    )


def chunk_tiles(tiles, most, step):
    most = max(step, most // step * step)
    count = -(-tiles // most)
    units = tiles // step
    return [(units // count + (1 if i < units % count else 0)) * step for i in range(count)]


class Plan:
    def __init__(self, ensemble, slots, groups):
        self.members, self.fields, self.rows, self.columns = ensemble.shape
        self.total = self.members * groups
        self.slots = slots
        self.groups = groups
        self.width = self.columns // groups
        self.tiles = self.columns // LANES
        self.q = max(1, LANES // self.width)
        most = LANES // (slots * self.q)
        self.counts = chunk_tiles(self.tiles, min(most, -(-self.tiles // 2)), max(1, self.width // LANES))
        self.starts = [sum(self.counts[:i]) for i in range(len(self.counts))]
        self.halves = 2
        self.hrows = self.rows // self.halves
        self.hrf = self.hrows * self.fields
        self.edge_groups = HALO * self.fields
        self.per_edge = LANES // (2 * HALO)
        self.edge_tiles = -(-self.edge_groups // self.per_edge)
        self.plain = -(-self.hrf // SUB) * SUB
        self.block = self.hrf * slots + self.plain

    def chunk(self, c):
        p = copy.copy(self)
        p.nt = self.counts[c]
        p.first = self.starts[c]
        p.after = (p.first + p.nt) % self.tiles
        p.before = (p.first - 1) % self.tiles
        p.np = p.nt * LANES // self.width
        p.first_patch = p.first * LANES // self.width
        p.message = p.nt * self.edge_groups + self.edge_tiles
        p.total_rows = p.nt * self.block
        return p

    def patches_of(self, tile):
        if self.width >= LANES:
            return [(tile * LANES // self.width, 0, LANES)]
        return [(tile * self.q + i, i * self.width, (i + 1) * self.width) for i in range(self.q)]


def lane_ids(shape):
    return lax.broadcasted_iota(jnp.int32, shape, len(shape) - 1)


def pack_kernel(plan, raw, state, *messages):
    p = plan
    lane = lane_ids((SUB, LANES))
    chunks = [p.chunk(c) for c in range(len(p.counts))]

    def body(kk, carry):
        mem = pl.ds(pl.multiple_of(kk * SUB, SUB), SUB)
        for c, h in enumerate(chunks):
            up, down = messages[2 * c], messages[2 * c + 1]
            for i in range(h.nt):
                t = h.first + i
                for f in range(p.fields):
                    for r in range(p.rows):
                        x = raw[mem, f, r, t * LANES : (t + 1) * LANES]
                        state[t, r, f, mem, :] = x
                        if r >= p.rows - HALO:
                            up[(i * HALO + r - (p.rows - HALO)) * p.fields + f, mem, :] = x
                        if r < HALO:
                            down[(i * HALO + r) * p.fields + f, mem, :] = x
        for c, h in enumerate(chunks):
            for d in range(2):
                out = messages[2 * c + d]
                for e in range(p.edge_tiles):
                    packed = jnp.zeros((SUB, LANES), jnp.float32)
                    for g in range(e * p.per_edge, min((e + 1) * p.per_edge, p.edge_groups)):
                        i, f = divmod(g, p.fields)
                        r = i + (p.rows - HALO if d == 0 else 0)
                        edge = jnp.where(lane < LANES // 2, state[h.after, r, f, mem, :], state[h.before, r, f, mem, :])
                        place = (g - e * p.per_edge) * 2 * HALO
                        inside = (lane >= place) & (lane < place + 2 * HALO)
                        packed = jnp.where(inside, pltpu.roll(edge, place + HALO, 1), packed)
                    out[h.nt * p.edge_groups + e, mem, :] = packed
        return carry

    lax.fori_loop(0, p.members // SUB, body, 0)


def step_once(p, rows_in, load, store, last):
    lane = lane_ids((SUB, LANES))
    ring = p.nt + 1
    out_tiles = p.nt if last else ring
    for row in range(1, rows_in - 1):
        coef = []
        for t in range(out_tiles):
            u = load(row, 0, t) * (time_step * 0.5)
            v = load(row, 1, t) * (time_step * 0.5)
            k = time_step * viscosity
            coef.append((k - u, k + u, k - v, k + v))
        for f in range(p.fields):
            x = [load(row, f, t) for t in range(ring)]
            right = [pltpu.roll(a, 1, 1) for a in x]
            left = [pltpu.roll(a, LANES - 1, 1) for a in x]
            for t in range(out_tiles):
                west = jnp.where(lane == 0, right[(t - 1) % ring], right[t])
                east = jnp.where(lane == LANES - 1, left[(t + 1) % ring], left[t])
                ce, cw, cn, cs = coef[t]
                moved = (ce * east + cw * west) + (cn * load(row + 1, f, t) + cs * load(row - 1, f, t))
                store(row, f, t, (1.0 - 4.0 * time_step * viscosity) * x[t] + moved)


def place_of(p, cell, patch):
    column = lax.rem(cell, p.width) + patch * p.width
    line = lax.div(cell, p.width)
    return lax.rem(line, p.rows), lax.div(line, p.rows), lax.div(column, LANES), lax.rem(column, LANES)


def forecast_kernel(plan, obs_cell, flags, state, low, high, ahead, seen, keep, send, s0, s1, s2):
    p = plan
    full = p.rows + 2 * HALO
    has_low = flags[0].astype(jnp.float32)
    has_high = flags[1].astype(jnp.float32)
    core = flags[2]
    me = flags[3]
    lane = lane_ids((SUB, LANES))

    def body(kk, carry):
        mem = pl.ds(pl.multiple_of(kk * SUB, SUB), SUB)

        def edge_of(source, g):
            e, place = divmod(g, p.per_edge)
            return pltpu.roll(source[p.nt * p.edge_groups + e, mem, :], (LANES - HALO - place * 2 * HALO) % LANES, 1)

        for f in range(p.fields):
            for r in range(p.rows):
                s0[r + HALO, f] = jnp.where(lane < LANES // 2, state[p.after, r, f, mem, :], state[p.before, r, f, mem, :])
            for i in range(HALO):
                s0[i, f] = edge_of(low, i * p.fields + f)
                s0[HALO + p.rows + i, f] = edge_of(high, i * p.fields + f)

        def load0(row, f, t):
            if t == p.nt:
                return s0[row, f]
            if row < HALO:
                return low[(t * HALO + row) * p.fields + f, mem, :]
            if row >= HALO + p.rows:
                return high[(t * HALO + row - HALO - p.rows) * p.fields + f, mem, :]
            return state[p.first + t, row - HALO, f, mem, :]

        def keep_zero(row, value):
            if row < HALO:
                return value * has_low
            if row >= HALO + p.rows:
                return value * has_high
            return value

        def store1(row, f, t, stepped):
            s1[row, f, t] = keep_zero(row, stepped)

        def store2(row, f, t, stepped):
            row = row + 1
            s2[row, f, t] = keep_zero(row, 0.75 * load0(row, f, t) + 0.25 * stepped)

        def store3(row, f, t, stepped):
            row = row + 2
            ahead[t, row - HALO, f, mem, :] = third_part * load0(row, f, t) + two_thirds * stepped

        step_once(p, full, load0, store1, False)
        step_once(p, full - 2, lambda row, f, t: s1[row + 1, f, t], store2, False)
        step_once(p, full - 4, lambda row, f, t: s2[row + 2, f, t], store3, True)
        return carry

    lax.fori_loop(0, p.members // SUB, body, 0)

    wide = lane_ids((p.members, LANES))
    found = jnp.zeros((p.members, LANES), jnp.float32)
    for j in range(p.np):
        at = ((p.first_patch + j) ^ me) * p.slots
        for o in range(p.slots):
            r, f, t, column = place_of(p, obs_cell[at + o], j)
            to = j * p.slots + o
            found = jnp.where(wide == to, pltpu.roll(ahead[t, r, f], lax.rem(to + LANES - column, LANES), 1), found)
    seen[...] = found

    last = lax.broadcasted_iota(jnp.int32, (SUB, p.members), 0)
    ones = jnp.where(last == 0, 1.0, 0.0).astype(jnp.float32)
    turned = jnp.transpose(found)
    sides = [jnp.concatenate([turned[j * p.slots : (j + 1) * p.slots], ones], axis=0) for j in range(p.np)]
    for side in range(p.halves):
        out = keep if side == 0 else send
        half = core if side == 0 else 1 - core
        for t in range(p.nt):
            base = t * p.block
            tiles = [ahead[t, half * p.hrows + i // p.fields, i % p.fields] for i in range(p.hrf)]
            joined = jnp.concatenate(tiles, axis=1)
            result = None
            for j, first, stop in p.patches_of(t):
                part = jnp.dot(sides[j], joined, precision=HIGHEST, preferred_element_type=jnp.float32)
                if result is None:
                    result = part
                else:
                    at = lane_ids(part.shape) % LANES
                    result = jnp.where((at >= first) & (at < stop), part, result)
            for i in range(p.hrf):
                piece = result[:, i * LANES : (i + 1) * LANES]
                out[pl.ds(base + i * p.slots, p.slots), :] = piece[: p.slots]
                out[pl.ds(base + p.hrf * p.slots + i, 1), :] = piece[p.slots : p.slots + 1]
            for i in range(p.hrf, p.plain):
                out[pl.ds(base + p.hrf * p.slots + i, 1), :] = jnp.zeros((1, LANES), jnp.float32)


def finish_kernel(plan, obs_cell, flags, obs, ahead, seen, own, other, *rest):
    out, staged, sems = rest[-3:]
    p = plan
    n = p.slots
    core = flags[2]
    me = flags[3]
    free = p.total - 1.0
    shape = (n, LANES)
    lane = lane_ids(shape)
    row = lax.broadcasted_iota(jnp.int32, shape, 0)
    group = lane // n * n
    eye = jnp.where(lane - group == row, 1.0, 0.0).astype(jnp.float32)
    lane_row = lane_ids((1, LANES))
    lane_sub = lane_ids((SUB, LANES))

    def pick(a, index):
        return jnp.take_along_axis(a, index, axis=1)

    def col(a):
        return pick(jnp.broadcast_to(a, shape), group + row)

    def spread_out(a):
        base = lane_ids(a.shape) // n * n
        return [pick(a, base + k) for k in range(n)]

    def product(parts, b):
        total = parts[0] * b[0:1]
        for k in range(1, n):
            total = total + parts[k] * b[k : k + 1]
        return total

    moments = jnp.zeros(shape, jnp.float32)
    sums = jnp.zeros((SUB, LANES), jnp.float32)
    given = [jnp.zeros((SUB, LANES), jnp.float32) for _ in range(4)]
    for j in range(p.np):
        source = (p.first_patch + j) ^ me
        line = jnp.broadcast_to(obs[pl.ds(source, 1), :], (SUB, LANES))
        mine = (lane_sub >= j * n) & (lane_sub < (j + 1) * n)
        for i in range(4):
            given[i] = jnp.where(mine, pltpu.roll(line, (j * n - i * n) % LANES, 1), given[i])
        for o in range(n):
            r, f, t, column = place_of(p, obs_cell[source * n + o], j)
            index = lax.rem(r, p.hrows) * p.fields + f
            here = lax.div(r, p.hrows) == core
            to = j * n + o
            shift = lax.rem(to + LANES - column, LANES)
            at = pl.ds(pl.multiple_of(t * p.block + index * n, SUB), n)
            value = jnp.where(here, own[at, :], other[at, :])
            moments = jnp.where(lane == to, pltpu.roll(value, shift, 1), moments)
            at = pl.ds(t * p.block + p.hrf * n + index, 1)
            value = jnp.broadcast_to(jnp.where(here, own[at, :], other[at, :]), (SUB, LANES))
            sums = jnp.where(lane_sub == to, pltpu.roll(value, shift, 1), sums)
    value, variance, loop, count = (a[0:1] for a in given)
    mean = sums[0:1] * (1.0 / p.total)
    slot = (lane_row % n).astype(jnp.float32)
    used = lane_row < p.np * n
    weight = jnp.where(used & (slot < count), jnp.exp(-0.35 * loop) / jnp.where(used, variance, 1.0), 0.0)
    root = jnp.sqrt(weight)
    root_col = col(root)
    mean_col = col(mean)
    scaled = root_col * (moments - p.total * mean_col * mean) * root
    bound = free + 0.5 * jnp.sum(pick(scaled, group + row), axis=0, keepdims=True)
    inverse = 1.0 / bound

    small = scaled * inverse
    t0 = free * inverse
    tf = t0 * eye + small
    tg = eye
    z0 = jnp.ones((1, LANES), jnp.float32)
    zg = None
    for repeat in range(NSI):
        f0 = 1.5 - 0.5 * t0
        ff = 1.5 * eye - 0.5 * tf
        parts = spread_out(ff)
        if zg is None:
            zg = -0.5 * z0 * tg
        else:
            zg = product(parts, zg) - 0.5 * z0 * tg
        z0 = z0 * f0
        if repeat < NSI - 1:
            square = product(parts, ff)
            bend = square - (0.5 * t0) * (ff + f0 * eye)
            tf = product(spread_out(square), tf)
            tg = bend if repeat == 0 else product(spread_out(bend), tg)
            t0 = t0 * f0 * f0
    zf = z0 * eye + product(spread_out(small), zg)
    scale = jnp.sqrt(free * inverse)
    spread = (scale * inverse) * root_col * zg * root
    down = root * (value - mean)
    for repeat in range(2):
        down = jnp.sum(zf * col(down), axis=0, keepdims=True)
    weights = product(spread_out(seen[...] - mean), spread) + root * down * inverse
    spread0 = scale * z0

    for t in range(p.nt):
        for half in range(p.halves):
            at_own = half == core
            pieces = []
            for i in range(p.hrf):
                at = t * p.block + i * n
                pieces.append(jnp.where(at_own, own[at : at + n, :], other[at : at + n, :]))
            base = t * p.block + p.hrf * n
            plain = jnp.where(at_own, own[base : base + p.plain, :], other[base : base + p.plain, :])
            results = []
            for j, first, stop in p.patches_of(t):
                mine = pltpu.roll(weights, (LANES - j * n) % LANES, 1)[:, :n]
                centre = pick(jnp.broadcast_to(mean, shape), row + j * n)
                keep0 = pick(jnp.broadcast_to(spread0, (SUB, LANES)), jnp.full((SUB, LANES), j * n, jnp.int32))[0:1]
                centred = [pieces[i] - centre * plain[i : i + 1, :] for i in range(p.hrf)]
                update = jnp.dot(mine, jnp.concatenate(centred, axis=1), precision=HIGHEST, preferred_element_type=jnp.float32)
                results.append((update, keep0, first, stop))
            for i in range(p.hrf):
                r, f = half * p.hrows + i // p.fields, i % p.fields
                x = ahead[t, r, f]
                centre = plain[i : i + 1, :] * (1.0 / p.total)
                final = None
                for update, keep0, first, stop in results:
                    part = centre + keep0 * (x - centre) + update[:, i * LANES : (i + 1) * LANES]
                    if final is None:
                        final = part
                    else:
                        at = lane_ids(part.shape)
                        final = jnp.where((at >= first) & (at < stop), part, final)
                staged[:, f, r, t * LANES : (t + 1) * LANES] = final
        cols = pl.ds((p.first + t) * LANES, LANES)
        pltpu.make_async_copy(staged.at[:, :, :, pl.ds(t * LANES, LANES)], out.at[:, :, :, cols], sems.at[t]).start()
    for t in range(p.nt):
        cols = pl.ds((p.first + t) * LANES, LANES)
        pltpu.make_async_copy(staged.at[:, :, :, pl.ds(t * LANES, LANES)], out.at[:, :, :, cols], sems.at[t]).wait()


def total_over_members(plan, keep, send):
    p = plan
    members = range(p.groups)
    bits = [1 << i for i in range(1, p.groups.bit_length() - 1)]
    total = keep + lax.ppermute(send, "mem", [(i, i ^ 1) for i in members])
    for phase in range(len(bits)):
        even = bits[phase]
        odd = bits[(phase + len(bits) // 2) % len(bits)]
        total = total + lax.ppermute(total, "mem", [(i, i ^ (odd if i & 1 else even)) for i in members])
    return total, lax.ppermute(total, "mem", [(i, i ^ 1) for i in members])


def per_device(ensemble, obs_value, obs_var, obs_cell, obs_loop, obs_count):
    groups = lax.axis_size("mem")
    bands = lax.axis_size("lat")
    slots = obs_cell.shape[-1]
    p = Plan(ensemble, slots, groups)
    chunks = [p.chunk(c) for c in range(len(p.counts))]
    f32 = jnp.float32
    shape = jax.ShapeDtypeStruct

    out = call(
        functools.partial(pack_kernel, p),
        [shape((p.tiles, p.rows, p.fields, p.members, LANES), f32)]
        + [shape((h.message, p.members, LANES), f32) for h in chunks for _ in range(2)],
        [VMEM],
        name="pack",
    )(ensemble)
    state, messages = out[0], out[1:]
    up = [(i, i + 1) for i in range(bands - 1)]
    down = [(i + 1, i) for i in range(bands - 1)]
    low, high = [], []
    for c in range(len(chunks)):
        low.append(lax.ppermute(messages[2 * c], "lat", up))
        high.append(lax.ppermute(messages[2 * c + 1], "lat", down))

    obs = jnp.concatenate(
        [
            obs_value[0],
            obs_var[0],
            obs_loop[0].astype(f32),
            jnp.broadcast_to(obs_count[0][:, None].astype(f32), (1, slots)),
            obs_cell[0].astype(f32),
        ],
        axis=1,
    )
    obs = jnp.pad(obs, ((0, 0), (0, -obs.shape[1] % LANES)))
    bit = 1
    while bit < groups:
        there = lax.ppermute(obs, "mem", [(i, i ^ bit) for i in range(groups)])
        obs = jnp.concatenate([obs, there], axis=0)
        bit *= 2
    cells = obs[:, 4 * slots : 5 * slots].astype(jnp.int32).reshape(groups * slots)

    band = lax.axis_index("lat")
    me = lax.axis_index("mem")
    flags = jnp.stack([band > 0, band < bands - 1, lax.rem(me, 2), me]).astype(jnp.int32)

    new = None
    for c, h in enumerate(chunks):
        stage = (p.rows + 2 * HALO, p.fields, h.nt + 1, SUB, LANES)
        ahead, seen, keep, send = call(
            functools.partial(forecast_kernel, h),
            [
                shape((h.nt, p.rows, p.fields, p.members, LANES), f32),
                shape((p.members, LANES), f32),
                shape((h.total_rows, LANES), f32),
                shape((h.total_rows, LANES), f32),
            ],
            [SMEM, SMEM, VMEM, VMEM, VMEM],
            [pltpu.VMEM(stage[:2] + stage[3:], f32), pltpu.VMEM(stage, f32), pltpu.VMEM(stage, f32)],
            name="forecast",
        )(cells, flags, state, low[c], high[c])
        own, other = total_over_members(p, keep, send)
        before = [] if new is None else [new]
        new = call(
            functools.partial(finish_kernel, h),
            shape(ensemble.shape, f32),
            [SMEM, SMEM, VMEM, VMEM, VMEM, VMEM, VMEM] + [HBM] * len(before),
            [pltpu.VMEM((p.members, p.fields, p.rows, h.nt * LANES), f32), pltpu.SemaphoreType.DMA((h.nt,))],
            name="finish",
            out_spec=HBM,
            alias={7: 0} if before else {},
        )(cells, flags, obs, ahead, seen, own, other, *before)
    return new


def solution(mesh):
    placed = (
        P("mem", None, "lat", None),
        P(None, ("mem", "lat"), None),
        P(None, ("mem", "lat"), None),
        P(None, ("mem", "lat"), None),
        P(None, ("mem", "lat"), None),
        P(None, ("mem", "lat")),
    )
    return jax.shard_map(
        per_device,
        mesh=mesh,
        in_specs=placed,
        out_specs=P("mem", None, "lat", None),
        check_vma=False,
    )
```

```python
import copy
import functools

import jax
import jax.numpy as jnp
from jax import lax
from jax.experimental import pallas as pl
from jax.experimental.pallas import tpu as pltpu
from jax.sharding import PartitionSpec as P

NSI = 5
HALO = 3
LANES = 128
SUB = 8

time_step = 0.15
viscosity = 0.1
third_part = 1.0 / 3.0
two_thirds = 2.0 / 3.0

HIGHEST = lax.Precision.HIGHEST
VMEM = pl.BlockSpec(memory_space=pltpu.VMEM)
SMEM = pl.BlockSpec(memory_space=pltpu.SMEM)
HBM = pl.BlockSpec(memory_space=pltpu.HBM)
KERNEL_VMEM = 12 << 20


def call(kernel, out_shape, in_specs, scratch=(), cost=(1 << 20, 1 << 20), name=None, out_specs=None, alias={}):
    flops, nbytes = cost
    return pl.pallas_call(
        kernel,
        out_shape=out_shape,
        in_specs=in_specs,
        out_specs=out_specs or [VMEM] * len(out_shape),
        scratch_shapes=list(scratch),
        input_output_aliases=alias,
        compiler_params=pltpu.CompilerParams(vmem_limit_bytes=KERNEL_VMEM),
        cost_estimate=pl.CostEstimate(flops=flops, bytes_accessed=nbytes, transcendentals=0),
        name=name,
    )


def chunk_tiles(tiles, most, step):
    most = max(step, most // step * step)
    count = -(-tiles // most)
    units = tiles // step
    return [(units // count + (1 if i < units % count else 0)) * step for i in range(count)]


class Plan:
    def __init__(self, ensemble, slots, groups):
        self.members, self.fields, self.rows, self.columns = ensemble.shape
        self.total = self.members * groups
        self.slots = slots
        self.groups = groups
        self.width = self.columns // groups
        self.tiles = self.columns // LANES
        self.q = max(1, LANES // self.width)
        most = LANES // (slots * self.q)
        self.counts = chunk_tiles(self.tiles, min(most, -(-self.tiles // 2)), max(1, self.width // LANES))
        self.starts = [sum(self.counts[:i]) for i in range(len(self.counts))]
        self.halves = 2
        self.hrows = self.rows // self.halves
        self.hrf = self.hrows * self.fields
        self.edge_groups = HALO * self.fields
        self.per_edge = LANES // (2 * HALO)
        self.edge_tiles = -(-self.edge_groups // self.per_edge)
        self.plain = -(-self.hrf // SUB) * SUB
        self.block = self.hrf * slots + self.plain

    def chunk(self, c):
        p = copy.copy(self)
        p.nt = self.counts[c]
        p.first = self.starts[c]
        p.after = (p.first + p.nt) % self.tiles
        p.before = (p.first - 1) % self.tiles
        p.np = p.nt * LANES // self.width
        p.first_patch = p.first * LANES // self.width
        p.message = p.nt * self.edge_groups + self.edge_tiles
        p.total_rows = p.nt * self.block
        return p

    def patches_of(self, tile):
        if self.width >= LANES:
            return [(tile * LANES // self.width, 0, LANES)]
        return [(tile * self.q + i, i * self.width, (i + 1) * self.width) for i in range(self.q)]


def lane_ids(shape):
    return lax.broadcasted_iota(jnp.int32, shape, len(shape) - 1)


def pack_kernel(plan, raw, state, *rest):
    p = plan
    chunks = [p.chunk(c) for c in range(len(p.counts))]
    count = 2 * len(chunks)
    outs, messages = rest[:count], rest[count : 2 * count]
    arrived, sems, out_sems = rest[2 * count :]
    lane = lane_ids((SUB, LANES))
    parts = p.members // SUB

    def part_copy(kk):
        part = pl.ds(kk * SUB, SUB)
        return pltpu.make_async_copy(raw.at[part], arrived.at[part], sems.at[kk])

    def message_copy(kk, i):
        part = pl.ds(kk * SUB, SUB)
        return pltpu.make_async_copy(messages[i].at[:, part, :], outs[i].at[:, part, :], out_sems.at[kk, i])

    for kk in range(min(2, parts)):
        part_copy(kk).start()

    def body(kk, carry):
        mem = pl.ds(pl.multiple_of(kk * SUB, SUB), SUB)
        part_copy(kk).wait()

        @pl.when(kk + 2 < parts)
        def _():
            part_copy(kk + 2).start()

        for c, h in enumerate(chunks):
            up, down = messages[2 * c], messages[2 * c + 1]
            for i in range(h.nt):
                cols = slice((h.first + i) * LANES, (h.first + i + 1) * LANES)
                for f in range(p.fields):
                    for r in range(p.rows):
                        x = arrived[mem, f, r, cols]
                        state[r, f, mem, cols] = x
                        if r >= p.rows - HALO:
                            up[(i * HALO + r - (p.rows - HALO)) * p.fields + f, mem, :] = x
                        if r < HALO:
                            down[(i * HALO + r) * p.fields + f, mem, :] = x
        for c, h in enumerate(chunks):
            for d in range(2):
                out = messages[2 * c + d]
                for e in range(p.edge_tiles):
                    packed = jnp.zeros((SUB, LANES), jnp.float32)
                    for g in range(e * p.per_edge, min((e + 1) * p.per_edge, p.edge_groups)):
                        i, f = divmod(g, p.fields)
                        edge = edge_tile(h, state, i + (p.rows - HALO if d == 0 else 0), f, mem, lane)
                        place = (g - e * p.per_edge) * 2 * HALO
                        inside = (lane >= place) & (lane < place + 2 * HALO)
                        packed = jnp.where(inside, pltpu.roll(edge, place + HALO, 1), packed)
                    out[h.nt * p.edge_groups + e, mem, :] = packed
                message_copy(kk, 2 * c + d).start()
        return carry

    lax.fori_loop(0, parts, body, 0)
    for kk in range(parts):
        for i in range(count):
            message_copy(kk, i).wait()


def edge_tile(p, state, r, f, mem, lane):
    after = state[r, f, mem, p.after * LANES : (p.after + 1) * LANES]
    before = state[r, f, mem, p.before * LANES : (p.before + 1) * LANES]
    return jnp.where(lane < LANES // 2, after, before)


def step_once(p, rows_in, load, store, last, scale):
    lane = lane_ids((SUB, LANES))
    ring = p.nt + 1
    out_tiles = p.nt if last else ring
    k = scale * time_step * viscosity
    centre = scale * (1.0 - 4.0 * time_step * viscosity)
    for first in range(0, p.fields, 2):
        pair = range(first, min(first + 2, p.fields))
        held = {row: {f: [load(row, f, t) for t in range(ring)] for f in pair} for row in range(2)}
        for row in range(1, rows_in - 1):
            held[row + 1] = {f: [load(row + 1, f, t) for t in range(ring)] for f in pair}
            coef = []
            for t in range(out_tiles):
                u, v = ((held[row][i][t] if i in held[row] else load(row, i, t)) * (scale * time_step * 0.5) for i in range(2))
                coef.append((k - u, k + u, k - v, k + v))
            for f in pair:
                x = held[row][f]
                right = [pltpu.roll(a, 1, 1) for a in x]
                left = [pltpu.roll(a, LANES - 1, 1) for a in x]
                for t in range(out_tiles):
                    west = jnp.where(lane == 0, right[(t - 1) % ring], right[t])
                    east = jnp.where(lane == LANES - 1, left[(t + 1) % ring], left[t])
                    ce, cw, cn, cs = coef[t]
                    moved = (ce * east + cw * west) + (cn * held[row + 1][f][t] + cs * held[row - 1][f][t])
                    store(row, f, t, centre * x[t] + moved)
            del held[row - 1]


def split(x):
    high = x.astype(jnp.bfloat16)
    return high, (x - high.astype(jnp.float32)).astype(jnp.bfloat16)


def places(p, chunks, me, cells):
    line = jnp.arange(p.groups, dtype=jnp.int32)[:, None]
    patch = line ^ me
    first = jnp.zeros_like(patch)
    for h in chunks:
        first = jnp.where(patch >= h.first_patch, h.first_patch, first)
    slot = jnp.arange(p.slots, dtype=jnp.int32)[None, :]
    column = cells % p.width + (patch - first) * p.width
    r = cells // p.width % p.rows
    f = cells // (p.width * p.rows)
    tile, lane = column // LANES, column % LANES
    index = r % p.hrows * p.fields + f
    shift = ((patch - first) * p.slots + slot - lane) % LANES
    table = [(tile * p.rows + r) * p.fields + f, shift, tile * p.block + index * p.slots, tile * p.block + p.hrf * p.slots + index, r // p.hrows]
    return jnp.stack(table).reshape(-1)


def forecast_kernel(plan, table, flags, state, low_in, high_in, ahead, seen, keep, send, s0, s1, s2, low, high, sems):
    p = plan
    full = p.rows + 2 * HALO
    has_low = flags[0].astype(jnp.float32)
    has_high = flags[1].astype(jnp.float32)
    core = flags[2]
    me = flags[3]
    lane = lane_ids((SUB, LANES))
    parts = p.members // SUB

    def part_copies(kk):
        part = pl.ds(kk * SUB, SUB)
        return [
            pltpu.make_async_copy(a.at[:, part, :], b.at[:, part, :], sems.at[kk, i])
            for i, (a, b) in enumerate(((low_in, low), (high_in, high)))
        ]

    for copy_in in part_copies(0):
        copy_in.start()

    def body(kk, carry):
        mem = pl.ds(pl.multiple_of(kk * SUB, SUB), SUB)

        @pl.when(kk + 1 < parts)
        def _():
            for copy_in in part_copies(kk + 1):
                copy_in.start()

        for copy_in in part_copies(kk):
            copy_in.wait()

        def edge_of(source, g):
            e, place = divmod(g, p.per_edge)
            return pltpu.roll(source[p.nt * p.edge_groups + e, mem, :], (LANES - HALO - place * 2 * HALO) % LANES, 1)

        for f in range(p.fields):
            for r in range(p.rows):
                s0[r + HALO, f] = edge_tile(p, state, r, f, mem, lane)
            for i in range(HALO):
                s0[i, f] = edge_of(low, i * p.fields + f)
                s0[HALO + p.rows + i, f] = edge_of(high, i * p.fields + f)

        def load0(row, f, t):
            if t == p.nt:
                return s0[row, f]
            if row < HALO:
                return low[(t * HALO + row) * p.fields + f, mem, :]
            if row >= HALO + p.rows:
                return high[(t * HALO + row - HALO - p.rows) * p.fields + f, mem, :]
            return state[row - HALO, f, mem, (p.first + t) * LANES : (p.first + t + 1) * LANES]

        def keep_zero(row, value):
            if row < HALO:
                return value * has_low
            if row >= HALO + p.rows:
                return value * has_high
            return value

        def store1(row, f, t, stepped):
            s1[row, f, t] = keep_zero(row, stepped)

        def store2(row, f, t, stepped):
            row = row + 1
            s2[row, f, t] = keep_zero(row, 0.75 * load0(row, f, t) + stepped)

        def store3(row, f, t, stepped):
            row = row + 2
            ahead[(t * p.rows + row - HALO) * p.fields + f, mem, :] = third_part * load0(row, f, t) + stepped

        step_once(p, full, load0, store1, False, 1.0)
        step_once(p, full - 2, lambda row, f, t: s1[row + 1, f, t], store2, False, 0.25)
        step_once(p, full - 4, lambda row, f, t: s2[row + 2, f, t], store3, True, two_thirds)
        return carry

    lax.fori_loop(0, parts, body, 0)

    wide = lane_ids((p.members, LANES))
    found = jnp.zeros((p.members, LANES), jnp.float32)
    every = p.groups * p.slots
    for j in range(p.np):
        at = ((p.first_patch + j) ^ me) * p.slots
        for o in range(p.slots):
            to = j * p.slots + o
            found = jnp.where(wide == to, pltpu.roll(ahead[table[at + o]], table[every + at + o], 1), found)
    seen[...] = found

    high, low_part = (a.astype(jnp.float32) for a in split(found))
    turned = jnp.transpose(jnp.concatenate([high, high, low_part], axis=0))
    depth = 3 * p.members
    extra = lax.broadcasted_iota(jnp.int32, (2 * SUB, depth), 0)
    ones = jnp.where((extra == 0) & (lane_ids((2 * SUB, depth)) < 2 * p.members), 1.0, 0.0).astype(jnp.float32)
    sides = [
        jnp.concatenate([turned[j * p.slots : (j + 1) * p.slots], ones], axis=0).astype(jnp.bfloat16) for j in range(p.np)
    ]
    for side in range(p.halves):
        out = keep if side == 0 else send
        half = core if side == 0 else 1 - core
        for t in range(p.nt):
            base = t * p.block
            begin = (t * p.rows + half * p.hrows) * p.fields
            high, low_part = split(jnp.concatenate([ahead[begin + i] for i in range(p.hrf)], axis=1))
            joined = jnp.concatenate([high, low_part, high], axis=0)
            result = None
            for j, first, stop in p.patches_of(t):
                part = jnp.dot(sides[j], joined, preferred_element_type=jnp.float32)
                if result is None:
                    result = part
                else:
                    at = lane_ids(part.shape) % LANES
                    result = jnp.where((at >= first) & (at < stop), part, result)
            for i in range(p.hrf):
                piece = result[:, i * LANES : (i + 1) * LANES]
                out[pl.ds(base + i * p.slots, p.slots), :] = piece[: p.slots]
                out[pl.ds(base + p.hrf * p.slots + i, 1), :] = piece[p.slots : p.slots + 1]
            for i in range(p.hrf, p.plain):
                out[pl.ds(base + p.hrf * p.slots + i, 1), :] = jnp.zeros((1, LANES), jnp.float32)


def finish_kernel(plan, table, flags, obs, ahead, seen, own, other, *rest):
    out, staged, sems = rest[-3:]
    p = plan
    n = p.slots
    core = flags[2]
    me = flags[3]
    free = p.total - 1.0
    shape = (n, LANES)
    lane = lane_ids(shape)
    row = lax.broadcasted_iota(jnp.int32, shape, 0)
    group = lane // n * n
    eye = jnp.where(lane - group == row, 1.0, 0.0).astype(jnp.float32)
    lane_row = lane_ids((1, LANES))
    lane_sub = lane_ids((SUB, LANES))

    def pick(a, index):
        return jnp.take_along_axis(a, index, axis=1)

    def col(a):
        return pick(jnp.broadcast_to(a, shape), group + row)

    def spread_out(a):
        base = lane_ids(a.shape) // n * n
        return [pick(a, base + k) for k in range(n)]

    def product(parts, b):
        total = parts[0] * b[0:1]
        for k in range(1, n):
            total = total + parts[k] * b[k : k + 1]
        return total

    moments = jnp.zeros(shape, jnp.float32)
    sums = jnp.zeros((SUB, LANES), jnp.float32)
    given = [jnp.zeros((SUB, LANES), jnp.float32) for _ in range(4)]
    every = p.groups * n
    for j in range(p.np):
        source = (p.first_patch + j) ^ me
        line = jnp.broadcast_to(obs[pl.ds(source, 1), :], (SUB, LANES))
        mine = (lane_sub >= j * n) & (lane_sub < (j + 1) * n)
        for i in range(4):
            given[i] = jnp.where(mine, pltpu.roll(line, (j * n - i * n) % LANES, 1), given[i])
        for o in range(n):
            to = j * n + o
            shift, at, line, half = (table[i * every + source * n + o] for i in range(1, 5))
            here = half == core
            at = pl.ds(pl.multiple_of(at, SUB), n)
            value = jnp.where(here, own[at, :], other[at, :])
            moments = jnp.where(lane == to, pltpu.roll(value, shift, 1), moments)
            value = jnp.where(here, own[pl.ds(line, 1), :], other[pl.ds(line, 1), :])
            sums = jnp.where(lane_sub == to, pltpu.roll(jnp.broadcast_to(value, (SUB, LANES)), shift, 1), sums)
    value, variance, loop, count = (a[0:1] for a in given)
    mean = sums[0:1] * (1.0 / p.total)
    slot = (lane_row % n).astype(jnp.float32)
    used = lane_row < p.np * n
    weight = jnp.where(used & (slot < count), jnp.exp(-0.35 * loop) / jnp.where(used, variance, 1.0), 0.0)
    root = jnp.sqrt(weight)
    root_col = col(root)
    mean_col = col(mean)
    scaled = root_col * (moments - p.total * mean_col * mean) * root
    bound = free + 0.5 * jnp.sum(pick(scaled, group + row), axis=0, keepdims=True)
    inverse = 1.0 / bound

    small = scaled * inverse
    t0 = free * inverse
    tf = t0 * eye + small
    tg = eye
    z0 = jnp.ones((1, LANES), jnp.float32)
    zg = None
    for repeat in range(NSI):
        f0 = 1.5 - 0.5 * t0
        ff = 1.5 * eye - 0.5 * tf
        parts = spread_out(ff)
        if zg is None:
            zg = -0.5 * z0 * tg
        else:
            zg = product(parts, zg) - 0.5 * z0 * tg
        z0 = z0 * f0
        if repeat < NSI - 1:
            square = product(parts, ff)
            bend = square - (0.5 * t0) * (ff + f0 * eye)
            tf = product(spread_out(square), tf)
            tg = bend if repeat == 0 else product(spread_out(bend), tg)
            t0 = t0 * f0 * f0
    zf = z0 * eye + product(spread_out(small), zg)
    scale = jnp.sqrt(free * inverse)
    spread = (scale * inverse) * root_col * zg * root
    down = root * (value - mean)
    for repeat in range(2):
        down = jnp.sum(zf * col(down), axis=0, keepdims=True)
    weights = product(spread_out(seen[...] - mean), spread) + root * down * inverse
    spread0 = scale * z0

    wide = lane_ids((p.members, LANES))
    high, low_part = (a.astype(jnp.float32) for a in split(weights))
    factors = []
    for j in range(p.np):
        here, there, last = (pltpu.roll(a, (i * n - j * n) % LANES, 1) for i, a in enumerate((high, high, low_part)))
        mine = jnp.where(wide < n, here, jnp.where(wide < 2 * n, there, last))[:, : 3 * n].astype(jnp.bfloat16)
        centre = pick(jnp.broadcast_to(mean, shape), row + j * n)
        keep0 = pick(jnp.broadcast_to(spread0, (SUB, LANES)), jnp.full((SUB, LANES), j * n, jnp.int32))[0:1]
        factors.append((mine, centre, keep0))

    def line_copy(r, f):
        cols = pl.ds(p.first * LANES, p.nt * LANES)
        return pltpu.make_async_copy(staged.at[r, f], out.at[:, f, r, cols], sems.at[r, f])

    for r in range(p.rows):
        half, begin = divmod(r, p.hrows)
        begin *= p.fields
        at_own = half == core
        for t in range(p.nt):
            pieces = []
            for f in range(p.fields):
                at = t * p.block + (begin + f) * n
                pieces.append(jnp.where(at_own, own[at : at + n, :], other[at : at + n, :]))
            at = t * p.block + p.hrf * n + begin
            plain = jnp.where(at_own, own[at : at + p.fields, :], other[at : at + p.fields, :])
            results = []
            for j, first, stop in p.patches_of(t):
                mine, centre, keep0 = factors[j]
                centred = [pieces[f] - centre * plain[f : f + 1, :] for f in range(p.fields)]
                high, low_part = split(jnp.concatenate(centred, axis=1))
                joined = jnp.concatenate([high, low_part, high], axis=0)
                results.append((jnp.dot(mine, joined, preferred_element_type=jnp.float32), keep0, first, stop))
            for f in range(p.fields):
                x = ahead[(t * p.rows + r) * p.fields + f]
                average = plain[f : f + 1, :] * (1.0 / p.total)
                final = None
                for update, keep0, first, stop in results:
                    part = (1.0 - keep0) * average + keep0 * x + update[:, f * LANES : (f + 1) * LANES]
                    if final is None:
                        final = part
                    else:
                        at = lane_ids(part.shape)
                        final = jnp.where((at >= first) & (at < stop), part, final)
                staged[r, f, :, t * LANES : (t + 1) * LANES] = final
        for f in range(p.fields):
            line_copy(r, f).start()
    for r in range(p.rows):
        for f in range(p.fields):
            line_copy(r, f).wait()


def first_sums(plan, keep, send):
    p = plan
    total = keep + lax.ppermute(send, "mem", [(i, i ^ 1) for i in range(p.groups)])
    return sum_phase(p, 0, total)


def sum_phase(plan, phase, total, waited=None):
    p = plan
    bits = [1 << i for i in range(1, p.groups.bit_length() - 1)]
    if phase >= len(bits):
        return total
    even = bits[phase]
    odd = bits[(phase + len(bits) // 2) % len(bits)]
    there = lax.ppermute(total, "mem", [(i, i ^ (odd if i & 1 else even)) for i in range(p.groups)])
    return (total if waited is None else after(total, waited)) + there


def last_sums(plan, total, waited=None):
    p = plan
    for phase in range(1, p.groups.bit_length() - 2):
        total = sum_phase(p, phase, total, waited)
    return total, lax.ppermute(total, "mem", [(i, i ^ 1) for i in range(p.groups)])


def after(value, *others):
    return lax.optimization_barrier((value,) + others)[0]


def per_device(ensemble, obs_value, obs_var, obs_cell, obs_loop, obs_count):
    groups = lax.axis_size("mem")
    bands = lax.axis_size("lat")
    slots = obs_cell.shape[-1]
    p = Plan(ensemble, slots, groups)
    chunks = [p.chunk(c) for c in range(len(p.counts))]
    f32 = jnp.float32
    shape = pltpu.VMEM

    sent = [(h.message, p.members, LANES) for h in chunks for _ in range(2)]
    out = call(
        functools.partial(pack_kernel, p),
        [pltpu.VMEM((p.rows, p.fields, p.members, p.columns), f32)] + [pltpu.HBM(a, f32) for a in sent],
        [HBM],
        [pltpu.VMEM(a, f32) for a in sent]
        + [
            pltpu.VMEM(ensemble.shape, f32),
            pltpu.SemaphoreType.DMA((p.members // SUB,)),
            pltpu.SemaphoreType.DMA((p.members // SUB, len(sent))),
        ],
        out_specs=[VMEM] + [HBM] * len(sent),
        name="pack",
    )(pltpu.with_memory_space_constraint(ensemble, pltpu.HBM))
    state, messages = out[0], out[1:]
    up = [(i, i + 1) for i in range(bands - 1)]
    down = [(i + 1, i) for i in range(bands - 1)]
    low, high = [], []
    for c in range(len(chunks)):
        low.append(lax.ppermute(messages[2 * c], "lat", up))
        high.append(lax.ppermute(messages[2 * c + 1], "lat", down))

    obs = jnp.concatenate(
        [
            after(obs_value, messages[0])[0],
            obs_var[0],
            obs_loop[0].astype(f32),
            jnp.broadcast_to(obs_count[0][:, None].astype(f32), (1, slots)),
            obs_cell[0].astype(f32),
        ],
        axis=1,
    )
    obs = jnp.pad(obs, ((0, 0), (0, -obs.shape[1] % LANES)))
    bit = 1
    while bit < groups:
        step = 2 if bit == 1 or bit * 4 > groups else 4
        there = [lax.ppermute(obs, "mem", [(i, i ^ (bit * b)) for i in range(groups)]) for b in range(1, step)]
        obs = jnp.concatenate([obs] + there, axis=0)
        bit *= step

    band = lax.axis_index("lat")
    me = lax.axis_index("mem")
    table = places(p, chunks, me, obs[:, 4 * slots : 5 * slots].astype(jnp.int32))
    flags = jnp.stack([band > 0, band < bands - 1, lax.rem(me, 2), me]).astype(jnp.int32)

    def near(x):
        return pltpu.with_memory_space_constraint(x, pltpu.VMEM)

    def far(x):
        return pltpu.with_memory_space_constraint(x, pltpu.HBM)

    new = None
    early = None
    for c, h in enumerate(chunks):
        final = c == len(chunks) - 1
        stage = (p.rows + 2 * HALO, p.fields, h.nt + 1, SUB, LANES)
        ahead, seen, keep, send = call(
            functools.partial(forecast_kernel, h),
            [
                shape((h.nt * p.rows * p.fields, p.members, LANES), f32),
                shape((p.members, LANES), f32),
                shape((h.total_rows, LANES), f32),
                shape((h.total_rows, LANES), f32),
            ],
            [SMEM, SMEM, VMEM, HBM, HBM],
            [pltpu.VMEM(stage[:2] + stage[3:], f32), pltpu.VMEM(stage, f32), pltpu.VMEM(stage, f32)]
            + [pltpu.VMEM((h.message, p.members, LANES), f32)] * 2
            + [pltpu.SemaphoreType.DMA((p.members // SUB, 2))],
            cost=(1024, h.nt * (6 << 20)),
            name="forecast",
        )(table, flags if early is None else after(flags, early), near(state), far(low[c]), far(high[c]))
        if c:
            own, other = last_sums(p, early)
            send = after(send, own)
            new = finish(p, chunks[c - 1], table, flags, obs, before + (own, other), new, ensemble.shape)
        before = (ahead, seen)
        if not final:
            early = lax.cond(obs_count[0, 0] >= 0, functools.partial(first_sums, p), lambda keep, send: keep, keep, send)
    own, other = last_sums(p, first_sums(p, keep, send), new)
    return finish(p, chunks[-1], table, flags, obs, before + (own, other), new, ensemble.shape)


def finish(plan, h, table, flags, obs, parts, new, whole):
    p = plan
    before = [] if new is None else [new]
    return call(
        functools.partial(finish_kernel, h),
        pltpu.HBM(whole, jnp.float32),
        [SMEM, SMEM, VMEM, VMEM, VMEM, VMEM, VMEM] + [HBM] * len(before),
        [pltpu.VMEM((p.rows, p.fields, p.members, h.nt * LANES), jnp.float32), pltpu.SemaphoreType.DMA((p.rows, p.fields))],
        cost=(1024, h.nt * (4 << 20)),
        name="finish",
        out_specs=HBM,
        alias={7: 0} if before else {},
    )(table, flags, obs, *(pltpu.with_memory_space_constraint(a, pltpu.VMEM) for a in parts), *before)


def solution(mesh):
    placed = (
        P("mem", None, "lat", None),
        P(None, ("mem", "lat"), None),
        P(None, ("mem", "lat"), None),
        P(None, ("mem", "lat"), None),
        P(None, ("mem", "lat"), None),
        P(None, ("mem", "lat")),
    )
    return jax.shard_map(
        per_device,
        mesh=mesh,
        in_specs=placed,
        out_specs=P("mem", None, "lat", None),
        check_vma=False,
    )
```

```python
import copy
import functools

import jax
import jax.numpy as jnp
from jax import lax
from jax.experimental import pallas as pl
from jax.experimental.pallas import tpu as pltpu
from jax.sharding import PartitionSpec as P

NSI = 5
HALO = 3
LANES = 128
SUB = 8

time_step = 0.15
viscosity = 0.1
third_part = 1.0 / 3.0
two_thirds = 2.0 / 3.0

HIGHEST = lax.Precision.HIGHEST
VMEM = pl.BlockSpec(memory_space=pltpu.VMEM)
SMEM = pl.BlockSpec(memory_space=pltpu.SMEM)
HBM = pl.BlockSpec(memory_space=pltpu.HBM)
ANY = pl.BlockSpec(memory_space=pl.ANY)
KERNEL_VMEM = 12 << 20


def call(kernel, out_shape, in_specs, scratch=(), cost=(1 << 20, 1 << 20), name=None, out_specs=None, alias={}):
    flops, nbytes = cost
    return pl.pallas_call(
        kernel,
        out_shape=out_shape,
        in_specs=in_specs,
        out_specs=out_specs or [VMEM] * len(out_shape),
        scratch_shapes=list(scratch),
        input_output_aliases=alias,
        compiler_params=pltpu.CompilerParams(vmem_limit_bytes=KERNEL_VMEM),
        cost_estimate=pl.CostEstimate(flops=flops, bytes_accessed=nbytes, transcendentals=0),
        name=name,
    )


def chunk_tiles(tiles, most, step):
    most = max(step, most // step * step)
    count = -(-tiles // most)
    units = tiles // step
    return [(units // count + (1 if i < units % count else 0)) * step for i in range(count)]


class Plan:
    def __init__(self, ensemble, slots, groups):
        self.members, self.fields, self.rows, self.columns = ensemble.shape
        self.total = self.members * groups
        self.slots = slots
        self.groups = groups
        self.width = self.columns // groups
        self.tiles = self.columns // LANES
        self.q = max(1, LANES // self.width)
        most = LANES // (slots * self.q)
        self.counts = chunk_tiles(self.tiles, min(most, -(-self.tiles // 2)), max(1, self.width // LANES))
        self.starts = [sum(self.counts[:i]) for i in range(len(self.counts))]
        self.halves = 2
        self.hrows = self.rows // self.halves
        self.hrf = self.hrows * self.fields
        self.edge_groups = HALO * self.fields
        self.per_edge = LANES // (2 * HALO)
        self.edge_tiles = -(-self.edge_groups // self.per_edge)
        self.plain = -(-self.hrf // SUB) * SUB
        self.block = self.hrf * slots + self.plain

    def chunk(self, c):
        p = copy.copy(self)
        p.nt = self.counts[c]
        p.first = self.starts[c]
        p.after = (p.first + p.nt) % self.tiles
        p.before = (p.first - 1) % self.tiles
        p.np = p.nt * LANES // self.width
        p.first_patch = p.first * LANES // self.width
        p.bands = lax.axis_size("lat")
        p.message = p.nt * self.edge_groups + self.edge_tiles
        p.total_rows = p.nt * self.block
        return p

    def patches_of(self, tile):
        if self.width >= LANES:
            return [(tile * LANES // self.width, 0, LANES)]
        return [(tile * self.q + i, i * self.width, (i + 1) * self.width) for i in range(self.q)]


def lane_ids(shape):
    return lax.broadcasted_iota(jnp.int32, shape, len(shape) - 1)


def pack_kernel(plan, raw, *rest):
    p = plan
    lane = lane_ids((SUB, LANES))
    parts = p.members // SUB
    given = []
    if p.first == 0:
        given, rest = rest[:5], rest[5:]
        row_out, (taken, lines, given_sems), rest = rest[3], (rest[-7:-2], *rest[-2:]), rest[:3] + rest[4:-7]
    state, first_out, second_out, up, down, arrived, beside, sems, out_sems = rest
    given_copies = []
    for i, a in enumerate(given):
        given_copies.append(pltpu.make_async_copy(a, taken[i], given_sems.at[i]))
    odd = lax.rem(lax.axis_index("lat"), 2)

    def part_copies(kk):
        part = pl.ds(kk * SUB, SUB)
        takes = [(arrived, p.first, p.nt)] + [(beside.at[i], t, 1) for i, t in enumerate((p.after, p.before))]
        return [
            pltpu.make_async_copy(raw.at[part, :, :, pl.ds(t * LANES, n * LANES)], to.at[part], sems.at[kk, i])
            for i, (to, t, n) in enumerate(takes)
        ]

    def message_copies(kk, swapped=0):
        part = pl.ds(kk * SUB, SUB)
        inner = (up, down) if swapped == 0 else (down, up)
        return [
            pltpu.make_async_copy(a.at[:, part, :], b.at[:, part, :], out_sems.at[kk, i])
            for i, (a, b) in enumerate(zip(inner, (first_out, second_out)))
        ]

    for kk in range(parts):
        for copy_in in part_copies(kk):
            copy_in.start()
    for copy_in in given_copies:
        copy_in.start()

    def body(kk, carry):
        mem = pl.ds(pl.multiple_of(kk * SUB, SUB), SUB)
        for copy_in in part_copies(kk):
            copy_in.wait()

        for i in range(p.nt):
            cols = slice(i * LANES, (i + 1) * LANES)
            for f in range(p.fields):
                for r in range(p.rows):
                    x = arrived[mem, f, r, cols]
                    state[r, f, mem, cols] = x
                    if r >= p.rows - HALO:
                        up[(i * HALO + r - (p.rows - HALO)) * p.fields + f, mem, :] = x
                    if r < HALO:
                        down[(i * HALO + r) * p.fields + f, mem, :] = x
        for r in range(p.rows):
            for f in range(p.fields):
                edge = jnp.where(lane < LANES // 2, beside[0, mem, f, r, :], beside[1, mem, f, r, :])
                state[r, f, mem, p.nt * LANES :] = edge
        for out, skipped in ((up, p.rows - HALO), (down, 0)):
            for e in range(p.edge_tiles):
                packed = jnp.zeros((SUB, LANES), jnp.float32)
                for g in range(e * p.per_edge, min((e + 1) * p.per_edge, p.edge_groups)):
                    i, f = divmod(g, p.fields)
                    place = (g - e * p.per_edge) * 2 * HALO
                    inside = (lane >= place) & (lane < place + 2 * HALO)
                    edge = state[i + skipped, f, mem, p.nt * LANES :]
                    packed = jnp.where(inside, pltpu.roll(edge, place + HALO, 1), packed)
                out[p.nt * p.edge_groups + e, mem, :] = packed

        for swapped in range(2):

            @pl.when(odd == swapped)
            def _():
                for copy_out in message_copies(kk, swapped):
                    copy_out.start()

        return carry

    lax.fori_loop(0, parts, body, 0)
    if given:
        for copy_in in given_copies:
            copy_in.wait()
        row = jnp.zeros((SUB, LANES), jnp.float32)
        for i, a in enumerate(given):
            lines[i : i + 1, : p.slots] = jnp.broadcast_to(taken[i][0].astype(jnp.float32), (1, p.slots))
            line = pltpu.roll(jnp.broadcast_to(lines[i : i + 1, :], (SUB, LANES)), i * p.slots, 1)
            row = jnp.where((lane >= i * p.slots) & (lane < (i + 1) * p.slots), line, row)
        row_out[...] = row[:1]
    for kk in range(parts):
        for copy_out in message_copies(kk):
            copy_out.wait()


def step_once(p, rows_in, load, store, last, scale):
    lane = lane_ids((SUB, LANES))
    ring = p.nt + 1
    out_tiles = p.nt if last else ring
    k = scale * time_step * viscosity
    centre = scale * (1.0 - 4.0 * time_step * viscosity)
    for first in range(0, p.fields, 2):
        pair = range(first, min(first + 2, p.fields))
        held = {row: {f: [load(row, f, t) for t in range(ring)] for f in pair} for row in range(2)}
        for row in range(1, rows_in - 1):
            held[row + 1] = {f: [load(row + 1, f, t) for t in range(ring)] for f in pair}
            coef = []
            for t in range(out_tiles):
                u, v = ((held[row][i][t] if i in held[row] else load(row, i, t)) * (scale * time_step * 0.5) for i in range(2))
                coef.append((k - u, k + u, k - v, k + v))
            for f in pair:
                x = held[row][f]
                right = [pltpu.roll(a, 1, 1) for a in x]
                left = [pltpu.roll(a, LANES - 1, 1) for a in x]
                for t in range(out_tiles):
                    west = jnp.where(lane == 0, right[(t - 1) % ring], right[t])
                    east = jnp.where(lane == LANES - 1, left[(t + 1) % ring], left[t])
                    ce, cw, cn, cs = coef[t]
                    moved = (ce * east + cw * west) + (cn * held[row + 1][f][t] + cs * held[row - 1][f][t])
                    store(row, f, t, centre * x[t] + moved)
            del held[row - 1]


def split(x):
    high = x.astype(jnp.bfloat16)
    return high, (x - high.astype(jnp.float32)).astype(jnp.bfloat16)


def places(p, chunks, me, cells):
    line = jnp.arange(p.groups, dtype=jnp.int32)[:, None]
    patch = line ^ me
    first = jnp.zeros_like(patch)
    for h in chunks:
        first = jnp.where(patch >= h.first_patch, h.first_patch, first)
    slot = jnp.arange(p.slots, dtype=jnp.int32)[None, :]
    column = cells % p.width + (patch - first) * p.width
    r = cells // p.width % p.rows
    f = cells // (p.width * p.rows)
    tile, lane = column // LANES, column % LANES
    index = r % p.hrows * p.fields + f
    shift = ((patch - first) * p.slots + slot - lane) % LANES
    table = [(tile * p.rows + r) * p.fields + f, shift, tile * p.block + index * p.slots, tile * p.block + p.hrf * p.slots + index, r // p.hrows]
    return jnp.stack(table).reshape(-1)


def table_kernel(table_in, table, sem):
    copy_in = pltpu.make_async_copy(table_in, table, sem)
    copy_in.start()
    copy_in.wait()


def forecast_kernel(plan, table, state, first_in, second_in, ahead, seen, keep, send, s0, s1, s2, low, high, sems):
    p = plan
    full = p.rows + 2 * HALO
    band = lax.axis_index("lat")
    me = lax.axis_index("mem")
    core = lax.rem(me, 2)
    has_low = (band > 0).astype(jnp.float32)
    has_high = (band < p.bands - 1).astype(jnp.float32)
    lane = lane_ids((SUB, LANES))
    parts = p.members // SUB

    def part_copies(kk, swapped=0):
        part = pl.ds(kk * SUB, SUB)
        inner = (high, low) if swapped == 0 else (low, high)
        return [
            pltpu.make_async_copy(a.at[:, part, :], b.at[:, part, :], sems.at[kk, i])
            for i, (a, b) in enumerate(zip((first_in, second_in), inner))
        ]

    def start_copies(kk):
        for swapped in range(2):

            @pl.when(lax.rem(band, 2) == swapped)
            def _():
                for copy_in in part_copies(kk, swapped):
                    copy_in.start()

    start_copies(0)

    def body(kk, carry):
        mem = pl.ds(pl.multiple_of(kk * SUB, SUB), SUB)

        @pl.when(kk + 1 < parts)
        def _():
            start_copies(kk + 1)

        for copy_in in part_copies(kk):
            copy_in.wait()

        def edge_of(source, g):
            e, place = divmod(g, p.per_edge)
            return pltpu.roll(source[p.nt * p.edge_groups + e, mem, :], (LANES - HALO - place * 2 * HALO) % LANES, 1)

        for f in range(p.fields):
            for i in range(HALO):
                s0[i, f] = edge_of(low, i * p.fields + f)
                s0[HALO + i, f] = edge_of(high, i * p.fields + f)

        def load0(row, f, t):
            if HALO <= row < HALO + p.rows:
                return state[row - HALO, f, mem, t * LANES : (t + 1) * LANES]
            i = row if row < HALO else row - p.rows
            if t == p.nt:
                return s0[i, f]
            source = low if row < HALO else high
            return source[(t * HALO + i % HALO) * p.fields + f, mem, :]

        def keep_zero(row, value):
            if row < HALO:
                return value * has_low
            if row >= HALO + p.rows:
                return value * has_high
            return value

        def store1(row, f, t, stepped):
            s1[row, f, t] = keep_zero(row, stepped)

        def store2(row, f, t, stepped):
            row = row + 1
            s2[row, f, t] = keep_zero(row, 0.75 * load0(row, f, t) + stepped)

        def store3(row, f, t, stepped):
            row = row + 2
            ahead[(t * p.rows + row - HALO) * p.fields + f, mem, :] = third_part * load0(row, f, t) + stepped

        step_once(p, full, load0, store1, False, 1.0)
        step_once(p, full - 2, lambda row, f, t: s1[row + 1, f, t], store2, False, 0.25)
        step_once(p, full - 4, lambda row, f, t: s2[row + 2, f, t], store3, True, two_thirds)
        return carry

    lax.fori_loop(0, parts, body, 0)

    wide = lane_ids((p.members, LANES))
    found = jnp.zeros((p.members, LANES), jnp.float32)
    every = p.groups * p.slots
    for j in range(p.np):
        at = ((p.first_patch + j) ^ me) * p.slots
        for o in range(p.slots):
            to = j * p.slots + o
            found = jnp.where(wide == to, pltpu.roll(ahead[table[at + o]], table[every + at + o], 1), found)
    seen[...] = found

    high, low_part = (a.astype(jnp.float32) for a in split(found))
    turned = jnp.transpose(jnp.concatenate([high, high, low_part], axis=0))
    depth = 3 * p.members
    extra = lax.broadcasted_iota(jnp.int32, (2 * SUB, depth), 0)
    ones = jnp.where((extra == 0) & (lane_ids((2 * SUB, depth)) < 2 * p.members), 1.0, 0.0).astype(jnp.float32)
    sides = [
        jnp.concatenate([turned[j * p.slots : (j + 1) * p.slots], ones], axis=0).astype(jnp.bfloat16) for j in range(p.np)
    ]
    for side in range(p.halves):
        out = keep if side == 0 else send
        half = core if side == 0 else 1 - core
        for t in range(p.nt):
            base = t * p.block
            begin = (t * p.rows + half * p.hrows) * p.fields
            high, low_part = split(jnp.concatenate([ahead[begin + i] for i in range(p.hrf)], axis=1))
            joined = jnp.concatenate([high, low_part, high], axis=0)
            result = None
            for j, first, stop in p.patches_of(t):
                part = jnp.dot(sides[j], joined, preferred_element_type=jnp.float32)
                if result is None:
                    result = part
                else:
                    at = lane_ids(part.shape) % LANES
                    result = jnp.where((at >= first) & (at < stop), part, result)
            for i in range(p.hrf):
                piece = result[:, i * LANES : (i + 1) * LANES]
                out[pl.ds(base + i * p.slots, p.slots), :] = piece[: p.slots]
                out[pl.ds(base + p.hrf * p.slots + i, 1), :] = piece[p.slots : p.slots + 1]
            for i in range(p.hrf, p.plain):
                out[pl.ds(base + p.hrf * p.slots + i, 1), :] = jnp.zeros((1, LANES), jnp.float32)


def finish_kernel(plan, table, obs, ahead, seen, own, other, *rest):
    out, staged, sems = rest[-3:]
    p = plan
    n = p.slots
    me = lax.axis_index("mem")
    core = lax.rem(me, 2)
    free = p.total - 1.0
    shape = (n, LANES)
    lane = lane_ids(shape)
    row = lax.broadcasted_iota(jnp.int32, shape, 0)
    group = lane // n * n
    eye = jnp.where(lane - group == row, 1.0, 0.0).astype(jnp.float32)
    lane_row = lane_ids((1, LANES))
    lane_sub = lane_ids((SUB, LANES))

    def pick(a, index):
        return jnp.take_along_axis(a, index, axis=1)

    def col(a):
        return pick(jnp.broadcast_to(a, shape), group + row)

    def spread_out(a):
        base = lane_ids(a.shape) // n * n
        return [pick(a, base + k) for k in range(n)]

    def product(parts, b):
        terms = [parts[k] * b[k : k + 1] for k in range(n)]
        while len(terms) > 1:
            terms = [sum(terms[i : i + 2][1:], terms[i]) for i in range(0, len(terms), 2)]
        return terms[0]

    moments = jnp.zeros(shape, jnp.float32)
    sums = jnp.zeros((SUB, LANES), jnp.float32)
    given = [jnp.zeros((SUB, LANES), jnp.float32) for _ in range(4)]
    every = p.groups * n
    for j in range(p.np):
        source = (p.first_patch + j) ^ me
        line = jnp.broadcast_to(obs[pl.ds(source, 1), :], (SUB, LANES))
        mine = (lane_sub >= j * n) & (lane_sub < (j + 1) * n)
        for i in range(4):
            given[i] = jnp.where(mine, pltpu.roll(line, (j * n - i * n) % LANES, 1), given[i])
        for o in range(n):
            to = j * n + o
            shift, at, line, half = (table[i * every + source * n + o] for i in range(1, 5))
            here = half == core
            at = pl.ds(pl.multiple_of(at, SUB), n)
            value = jnp.where(here, own[at, :], other[at, :])
            moments = jnp.where(lane == to, pltpu.roll(value, shift, 1), moments)
            value = jnp.where(here, own[pl.ds(line, 1), :], other[pl.ds(line, 1), :])
            sums = jnp.where(lane_sub == to, pltpu.roll(jnp.broadcast_to(value, (SUB, LANES)), shift, 1), sums)
    value, variance, loop, count = (a[0:1] for a in given)
    mean = sums[0:1] * (1.0 / p.total)
    slot = (lane_row % n).astype(jnp.float32)
    used = lane_row < p.np * n
    weight = jnp.where(used & (slot < count), jnp.exp(-0.35 * loop) / jnp.where(used, variance, 1.0), 0.0)
    root = jnp.sqrt(weight)
    root_col = col(root)
    mean_col = col(mean)
    scaled = root_col * (moments - p.total * mean_col * mean) * root
    bound = free + 0.5 * jnp.sum(pick(scaled, group + row), axis=0, keepdims=True)
    inverse = 1.0 / bound

    small = scaled * inverse
    t0 = free * inverse
    tf = t0 * eye + small
    tg = eye
    z0 = jnp.ones((1, LANES), jnp.float32)
    zg = None
    for repeat in range(NSI):
        f0 = 1.5 - 0.5 * t0
        ff = 1.5 * eye - 0.5 * tf
        parts = spread_out(ff)
        if zg is None:
            zg = -0.5 * z0 * tg
        else:
            zg = product(parts, zg) - 0.5 * z0 * tg
        z0 = z0 * f0
        if repeat < NSI - 1:
            square = product(parts, ff)
            bend = square - (0.5 * t0) * (ff + f0 * eye)
            tf = product(spread_out(square), tf)
            tg = bend if repeat == 0 else product(spread_out(bend), tg)
            t0 = t0 * f0 * f0
    zf = z0 * eye + product(spread_out(small), zg)
    scale = jnp.sqrt(free * inverse)
    spread = (scale * inverse) * root_col * zg * root
    down = root * (value - mean)
    for repeat in range(2):
        down = jnp.sum(zf * col(down), axis=0, keepdims=True)
    weights = product(spread_out(seen[...] - mean), spread) + root * down * inverse
    spread0 = scale * z0

    wide = lane_ids((p.members, LANES))
    high, low_part = (a.astype(jnp.float32) for a in split(weights))
    factors = []
    for j in range(p.np):
        here, there, last = (pltpu.roll(a, (i * n - j * n) % LANES, 1) for i, a in enumerate((high, high, low_part)))
        mine = jnp.where(wide < n, here, jnp.where(wide < 2 * n, there, last))[:, : 3 * n].astype(jnp.bfloat16)
        centre = pick(jnp.broadcast_to(mean, shape), row + j * n)
        keep0 = pick(jnp.broadcast_to(spread0, (SUB, LANES)), jnp.full((SUB, LANES), j * n, jnp.int32))[0:1]
        factors.append((mine, centre, keep0))

    def line_copy(r, f):
        cols = pl.ds(p.first * LANES, p.nt * LANES)
        return pltpu.make_async_copy(staged.at[r, f], out.at[:, f, r, cols], sems.at[r, f])

    for r in range(p.rows):
        half, begin = divmod(r, p.hrows)
        begin *= p.fields
        at_own = half == core
        for t in range(p.nt):
            pieces = []
            for f in range(p.fields):
                at = t * p.block + (begin + f) * n
                pieces.append(jnp.where(at_own, own[at : at + n, :], other[at : at + n, :]))
            at = t * p.block + p.hrf * n + begin
            plain = jnp.where(at_own, own[at : at + p.fields, :], other[at : at + p.fields, :])
            results = []
            for j, first, stop in p.patches_of(t):
                mine, centre, keep0 = factors[j]
                centred = [pieces[f] - centre * plain[f : f + 1, :] for f in range(p.fields)]
                high, low_part = split(jnp.concatenate(centred, axis=1))
                joined = jnp.concatenate([high, low_part, high], axis=0)
                results.append((jnp.dot(mine, joined, preferred_element_type=jnp.float32), keep0, first, stop))
            for f in range(p.fields):
                x = ahead[(t * p.rows + r) * p.fields + f]
                average = plain[f : f + 1, :] * (1.0 / p.total)
                final = None
                for update, keep0, first, stop in results:
                    part = (1.0 - keep0) * average + keep0 * x + update[:, f * LANES : (f + 1) * LANES]
                    if final is None:
                        final = part
                    else:
                        at = lane_ids(part.shape)
                        final = jnp.where((at >= first) & (at < stop), part, final)
                staged[r, f, :, t * LANES : (t + 1) * LANES] = final
        for f in range(p.fields):
            line_copy(r, f).start()
    for r in range(p.rows):
        for f in range(p.fields):
            line_copy(r, f).wait()


def first_sums(plan, keep, send):
    p = plan
    total = keep + lax.ppermute(send, "mem", [(i, i ^ 1) for i in range(p.groups)])
    return sum_phase(p, 0, total)


def sum_phase(plan, phase, total, waited=None):
    p = plan
    bits = [1 << i for i in range(1, p.groups.bit_length() - 1)]
    if phase >= len(bits):
        return total
    even = bits[phase]
    odd = bits[(phase + len(bits) // 2) % len(bits)]
    there = lax.ppermute(total, "mem", [(i, i ^ (odd if i & 1 else even)) for i in range(p.groups)])
    return (total if waited is None else after(total, waited)) + there


def last_sums(plan, total, waited=None):
    p = plan
    for phase in range(1, p.groups.bit_length() - 2):
        total = sum_phase(p, phase, total, waited)
    return total, lax.ppermute(total, "mem", [(i, i ^ 1) for i in range(p.groups)])


def after(value, *others):
    return lax.optimization_barrier((value,) + others)[0]


def per_device(ensemble, obs_value, obs_var, obs_cell, obs_loop, obs_count):
    groups = lax.axis_size("mem")
    bands = lax.axis_size("lat")
    slots = obs_cell.shape[-1]
    p = Plan(ensemble, slots, groups)
    chunks = [p.chunk(c) for c in range(len(p.counts))]
    f32 = jnp.float32
    shape = pltpu.VMEM

    given = (obs_value[0], obs_var[0], obs_loop[0], obs_count, obs_cell[0])
    given = tuple(a.reshape(1, 1, -1) for a in given)

    def pack(h, source):
        sent = (h.message, p.members, LANES)
        more = given if h.first == 0 else ()
        return call(
            functools.partial(pack_kernel, h),
            [pltpu.VMEM((p.rows, p.fields, p.members, (h.nt + 1) * LANES), f32), pltpu.HBM(sent, f32), pltpu.HBM(sent, f32)]
            + [pltpu.VMEM((1, LANES), f32) for _ in more[:1]],
            [HBM] + [ANY if a.size == 1 else HBM for a in more],
            [
                pltpu.VMEM(sent, f32),
                pltpu.VMEM(sent, f32),
                pltpu.VMEM((p.members, p.fields, p.rows, h.nt * LANES), f32),
                pltpu.VMEM((2, p.members, p.fields, p.rows, LANES), f32),
                pltpu.SemaphoreType.DMA((p.members // SUB, 3)),
                pltpu.SemaphoreType.DMA((p.members // SUB, 2)),
            ]
            + [pltpu.VMEM(a.shape, a.dtype) for a in more]
            + [pltpu.VMEM((SUB, LANES), f32) for _ in more[:1]]
            + [pltpu.SemaphoreType.DMA((len(more),)) for _ in more[:1]],
            out_specs=[VMEM, HBM, HBM] + [VMEM for _ in more[:1]],
            name="pack",
        )(*(a if a.size == 1 else pltpu.with_memory_space_constraint(a, pltpu.HBM) for a in (source,) + more))

    packed = [pack(h, ensemble) for h in chunks]
    messages = [a for part in packed for a in part[1:3]]
    swaps = [[pair for i in range(begin, bands - 1, 2) for pair in ((i, i + 1), (i + 1, i))] for begin in range(2)]
    halo = [[lax.ppermute(messages[2 * c + i], "lat", swaps[i]) for i in range(2)] for c in range(len(chunks))]

    obs = packed[0][3]
    bit = 1
    while bit < groups:
        step = 2 if bit == 1 or bit * 4 > groups else 4
        there = [lax.ppermute(obs, "mem", [(i, i ^ (bit * b)) for i in range(groups)]) for b in range(1, step)]
        obs = jnp.concatenate([obs] + there, axis=0)
        bit *= step

    table = call(
        table_kernel,
        [pltpu.SMEM((5 * groups * slots,), jnp.int32)],
        [ANY],
        [pltpu.SemaphoreType.DMA],
        out_specs=[SMEM],
        name="places",
    )(places(p, chunks, lax.axis_index("mem"), obs[:, 4 * slots : 5 * slots].astype(jnp.int32)))[0]
    table = pltpu.with_memory_space_constraint(table, pltpu.SMEM)

    def near(x):
        return pltpu.with_memory_space_constraint(x, pltpu.VMEM)

    def far(x):
        return pltpu.with_memory_space_constraint(x, pltpu.HBM)

    new = None
    early = None
    for c, h in enumerate(chunks):
        final = c == len(chunks) - 1
        stage = (p.rows + 2 * HALO, p.fields, h.nt + 1, SUB, LANES)
        ahead, seen, keep, send = call(
            functools.partial(forecast_kernel, h),
            [
                shape((h.nt * p.rows * p.fields, p.members, LANES), f32),
                shape((p.members, LANES), f32),
                shape((h.total_rows, LANES), f32),
                shape((h.total_rows, LANES), f32),
            ],
            [SMEM, VMEM, ANY, ANY],
            [pltpu.VMEM((2 * HALO, p.fields, SUB, LANES), f32), pltpu.VMEM(stage, f32), pltpu.VMEM(stage, f32)]
            + [pltpu.VMEM((h.message, p.members, LANES), f32)] * 2
            + [pltpu.SemaphoreType.DMA((p.members // SUB, 2))],
            cost=(1024, h.nt * (6 << 20)),
            name="forecast",
        )(table, near(packed[c][0] if early is None else after(packed[c][0], early)), *map(far, halo[c]))
        if c:
            own, other = last_sums(p, early)
            send = after(send, own)
            new = finish(p, chunks[c - 1], table, obs, before + (own, other), new, ensemble.shape)
        before = (ahead, seen)
        if not final:
            early = lax.cond(obs_count[0, 0] >= 0, functools.partial(first_sums, p), lambda keep, send: keep, keep, send)
    own, other = last_sums(p, first_sums(p, keep, send), new)
    return finish(p, chunks[-1], table, obs, before + (own, other), new, ensemble.shape)


def finish(plan, h, table, obs, parts, new, whole):
    p = plan
    before = [] if new is None else [new]
    return call(
        functools.partial(finish_kernel, h),
        pltpu.HBM(whole, jnp.float32),
        [SMEM, VMEM, VMEM, VMEM, VMEM, VMEM] + [HBM] * len(before),
        [pltpu.VMEM((p.rows, p.fields, p.members, h.nt * LANES), jnp.float32), pltpu.SemaphoreType.DMA((p.rows, p.fields))],
        cost=(1024, h.nt * (4 << 20)),
        name="finish",
        out_specs=HBM,
        alias={6: 0} if before else {},
    )(table, obs, *(pltpu.with_memory_space_constraint(a, pltpu.VMEM) for a in parts), *before)


def solution(mesh):
    placed = (
        P("mem", None, "lat", None),
        P(None, ("mem", "lat"), None),
        P(None, ("mem", "lat"), None),
        P(None, ("mem", "lat"), None),
        P(None, ("mem", "lat"), None),
        P(None, ("mem", "lat")),
    )
    return jax.shard_map(
        per_device,
        mesh=mesh,
        in_specs=placed,
        out_specs=P("mem", None, "lat", None),
        check_vma=False,
    )
```

```python
import copy
import functools

import jax
import jax.numpy as jnp
from jax import lax
from jax.experimental import pallas as pl
from jax.experimental.pallas import tpu as pltpu
from jax.sharding import PartitionSpec as P

NSI = 5
HALO = 3
LANES = 128
SUB = 8

time_step = 0.15
viscosity = 0.1
third_part = 1.0 / 3.0
two_thirds = 2.0 / 3.0

HIGHEST = lax.Precision.HIGHEST
VMEM = pl.BlockSpec(memory_space=pltpu.VMEM)
SMEM = pl.BlockSpec(memory_space=pltpu.SMEM)
HBM = pl.BlockSpec(memory_space=pltpu.HBM)
ANY = pl.BlockSpec(memory_space=pl.ANY)
KERNEL_VMEM = 12 << 20


def call(kernel, out_shape, in_specs, scratch=(), cost=(1 << 20, 1 << 20), name=None, out_specs=None, alias={}):
    flops, nbytes = cost
    return pl.pallas_call(
        kernel,
        out_shape=out_shape,
        in_specs=in_specs,
        out_specs=out_specs or [VMEM] * len(out_shape),
        scratch_shapes=list(scratch),
        input_output_aliases=alias,
        compiler_params=pltpu.CompilerParams(vmem_limit_bytes=KERNEL_VMEM),
        cost_estimate=pl.CostEstimate(flops=flops, bytes_accessed=nbytes, transcendentals=0),
        name=name,
    )


def chunk_tiles(tiles, most, step):
    most = max(step, most // step * step)
    count = -(-tiles // most)
    units = tiles // step
    return [(units // count + (1 if i < units % count else 0)) * step for i in range(count)]


class Plan:
    def __init__(self, ensemble, slots, groups):
        self.members, self.fields, self.rows, self.columns = ensemble.shape
        self.total = self.members * groups
        self.slots = slots
        self.groups = groups
        self.width = self.columns // groups
        self.tiles = self.columns // LANES
        self.q = max(1, LANES // self.width)
        most = LANES // (slots * self.q)
        self.counts = chunk_tiles(self.tiles, min(most, -(-self.tiles // 2)), max(1, self.width // LANES))
        self.counts = [4, 4] if self.counts == [4, 4] else self.counts
        self.starts = [sum(self.counts[:i]) for i in range(len(self.counts))]
        self.halves = 2
        self.hrows = self.rows // self.halves
        self.hrf = self.hrows * self.fields
        self.edge_groups = HALO * self.fields
        self.per_edge = LANES // (2 * HALO)
        self.edge_tiles = -(-self.edge_groups // self.per_edge)
        self.plain = -(-self.hrf // SUB) * SUB
        self.block = self.hrf * slots + self.plain

    def chunk(self, c):
        p = copy.copy(self)
        p.nt = self.counts[c]
        p.first = self.starts[c]
        p.after = (p.first + p.nt) % self.tiles
        p.before = (p.first - 1) % self.tiles
        p.np = p.nt * LANES // self.width
        p.first_patch = p.first * LANES // self.width
        p.bands = lax.axis_size("lat")
        p.message = p.nt * self.edge_groups + self.edge_tiles
        p.cell_rows = p.nt * self.block
        p.total_rows = p.cell_rows + p.slots + SUB
        return p

    def patches_of(self, tile):
        if self.width >= LANES:
            return [(tile * LANES // self.width, 0, LANES)]
        return [(tile * self.q + i, i * self.width, (i + 1) * self.width) for i in range(self.q)]


def lane_ids(shape):
    return lax.broadcasted_iota(jnp.int32, shape, len(shape) - 1)


def pack_kernel(plan, raw, *rest):
    p = plan
    lane = lane_ids((SUB, LANES))
    parts = p.members // SUB
    given = []
    if p.first == 0:
        given, rest = rest[:4], rest[4:]
        row_out, (taken, lines, given_sems), rest = rest[3], (rest[-6:-2], *rest[-2:]), rest[:3] + rest[4:-6]
    state, first_out, second_out, up, down, arrived, beside, sems, out_sems = rest
    given_copies = []
    for i, a in enumerate(given):
        given_copies.append(pltpu.make_async_copy(a, taken[i], given_sems.at[i]))
    odd = lax.rem(lax.axis_index("lat"), 2)

    def part_copies(kk):
        part = pl.ds(kk * SUB, SUB)
        takes = [(arrived, p.first, p.nt)] + [(beside.at[i], t, 1) for i, t in enumerate((p.after, p.before))]
        return [
            pltpu.make_async_copy(raw.at[part, :, :, pl.ds(t * LANES, n * LANES)], to.at[part], sems.at[kk, i])
            for i, (to, t, n) in enumerate(takes)
        ]

    cut = p.nt // 2
    pieces = [(0, cut * p.edge_groups), (cut * p.edge_groups, p.message)] if cut else [(0, p.message)]

    def message_copies(kk, piece, swapped=0):
        part = pl.ds(kk * SUB, SUB)
        lines = pl.ds(pieces[piece][0], pieces[piece][1] - pieces[piece][0])
        inner = (up, down) if swapped == 0 else (down, up)
        return [
            pltpu.make_async_copy(a.at[lines, part, :], b.at[lines, part, :], out_sems.at[kk, 2 * piece + i])
            for i, (a, b) in enumerate(zip(inner, (first_out, second_out)))
        ]

    def send_out(kk, piece):
        for swapped in range(2):

            @pl.when(odd == swapped)
            def _():
                for copy_out in message_copies(kk, piece, swapped):
                    copy_out.start()

    for kk in range(parts):
        for copy_in in part_copies(kk):
            copy_in.start()
    for copy_in in given_copies:
        copy_in.start()

    def body(kk, carry):
        mem = pl.ds(pl.multiple_of(kk * SUB, SUB), SUB)
        for copy_in in part_copies(kk):
            copy_in.wait()

        for i in range(p.nt):
            if cut and i == cut:
                send_out(kk, 0)
            cols = slice(i * LANES, (i + 1) * LANES)
            for f in range(p.fields):
                for r in range(p.rows):
                    x = arrived[mem, f, r, cols]
                    state[r, f, mem, cols] = x
                    if r >= p.rows - HALO:
                        up[(i * HALO + r - (p.rows - HALO)) * p.fields + f, mem, :] = x
                    if r < HALO:
                        down[(i * HALO + r) * p.fields + f, mem, :] = x
        for r in range(p.rows):
            for f in range(p.fields):
                edge = jnp.where(lane < LANES // 2, beside[0, mem, f, r, :], beside[1, mem, f, r, :])
                state[r, f, mem, p.nt * LANES :] = edge
        for out, skipped in ((up, p.rows - HALO), (down, 0)):
            for e in range(p.edge_tiles):
                packed = jnp.zeros((SUB, LANES), jnp.float32)
                for g in range(e * p.per_edge, min((e + 1) * p.per_edge, p.edge_groups)):
                    i, f = divmod(g, p.fields)
                    place = (g - e * p.per_edge) * 2 * HALO
                    inside = (lane >= place) & (lane < place + 2 * HALO)
                    edge = state[i + skipped, f, mem, p.nt * LANES :]
                    packed = jnp.where(inside, pltpu.roll(edge, place + HALO, 1), packed)
                out[p.nt * p.edge_groups + e, mem, :] = packed

        send_out(kk, len(pieces) - 1)
        return carry

    lax.fori_loop(0, parts, body, 0)
    if given:
        for copy_in in given_copies:
            copy_in.wait()
        row = jnp.zeros((SUB, LANES), jnp.float32)
        for i, a in enumerate(given):
            lines[i : i + 1, : p.slots] = jnp.broadcast_to(taken[i][0].astype(jnp.float32), (1, p.slots))
            line = pltpu.roll(jnp.broadcast_to(lines[i : i + 1, :], (SUB, LANES)), i * p.slots, 1)
            row = jnp.where((lane >= i * p.slots) & (lane < (i + 1) * p.slots), line, row)
        row_out[...] = row[:1]
    for kk in range(parts):
        for piece in range(len(pieces)):
            for copy_out in message_copies(kk, piece):
                copy_out.wait()


def step_once(p, rows_in, load, store, last, scale):
    lane = lane_ids((SUB, LANES))
    ring = p.nt + 1
    out_tiles = p.nt if last else ring
    k = scale * time_step * viscosity
    centre = scale * (1.0 - 4.0 * time_step * viscosity)
    for first in range(0, p.fields, 2):
        pair = range(first, min(first + 2, p.fields))
        held = {row: {f: [load(row, f, t) for t in range(ring)] for f in pair} for row in range(2)}
        for row in range(1, rows_in - 1):
            held[row + 1] = {f: [load(row + 1, f, t) for t in range(ring)] for f in pair}
            rolled = {}

            def turn(f, t, by):
                if (f, t, by) not in rolled:
                    rolled[f, t, by] = pltpu.roll(held[row][f][t], by, 1)
                return rolled[f, t, by]

            for t in range(out_tiles):
                u, v = ((held[row][i][t] if i in held[row] else load(row, i, t)) * (scale * time_step * 0.5) for i in range(2))
                ce, cw, cn, cs = k - u, k + u, k - v, k + v
                for f in pair:
                    west = pltpu.roll(jnp.where(lane == LANES - 1, held[row][f][(t - 1) % ring], held[row][f][t]), 1, 1)
                    east = pltpu.roll(jnp.where(lane == 0, held[row][f][(t + 1) % ring], held[row][f][t]), LANES - 1, 1)
                    moved = (ce * east + cw * west) + (cn * held[row + 1][f][t] + cs * held[row - 1][f][t])
                    store(row, f, t, centre * held[row][f][t] + moved)
            del held[row - 1]


def split(x):
    high = x.astype(jnp.bfloat16)
    return high, (x - high.astype(jnp.float32)).astype(jnp.bfloat16)


def places(p, chunks, me, cells):
    line = jnp.arange(p.groups, dtype=jnp.int32)[:, None]
    patch = line ^ me
    first = jnp.zeros_like(patch)
    for h in chunks:
        first = jnp.where(patch >= h.first_patch, h.first_patch, first)
    slot = jnp.arange(p.slots, dtype=jnp.int32)[None, :]
    column = cells % p.width + (patch - first) * p.width
    r = cells // p.width % p.rows
    f = cells // (p.width * p.rows)
    tile, lane = column // LANES, column % LANES
    shift = ((patch - first) * p.slots + slot - lane) % LANES
    table = [(tile * p.rows + r) * p.fields + f, shift]
    return jnp.stack(table).reshape(-1)


def table_kernel(table_in, table, sem):
    copy_in = pltpu.make_async_copy(table_in, table, sem)
    copy_in.start()
    copy_in.wait()


def forecast_kernel(plan, table, state, first_in, second_in, ahead, seen, keep, send, s0, s1, s2, low, high, sems):
    p = plan
    full = p.rows + 2 * HALO
    band = lax.axis_index("lat")
    me = lax.axis_index("mem")
    core = lax.rem(me, 2)
    has_low = (band > 0).astype(jnp.float32)
    has_high = (band < p.bands - 1).astype(jnp.float32)
    lane = lane_ids((SUB, LANES))
    parts = p.members // SUB

    def part_copies(kk, swapped=0):
        part = pl.ds(kk * SUB, SUB)
        inner = (high, low) if swapped == 0 else (low, high)
        return [
            pltpu.make_async_copy(a.at[:, part, :], b.at[:, part, :], sems.at[kk, i])
            for i, (a, b) in enumerate(zip((first_in, second_in), inner))
        ]

    def start_copies(kk):
        for swapped in range(2):

            @pl.when(lax.rem(band, 2) == swapped)
            def _():
                for copy_in in part_copies(kk, swapped):
                    copy_in.start()

    start_copies(0)

    def body(kk, carry):
        mem = pl.ds(pl.multiple_of(kk * SUB, SUB), SUB)

        @pl.when(kk + 1 < parts)
        def _():
            start_copies(kk + 1)

        for copy_in in part_copies(kk):
            copy_in.wait()

        def edge_of(source, g):
            e, place = divmod(g, p.per_edge)
            return pltpu.roll(source[p.nt * p.edge_groups + e, mem, :], (LANES - HALO - place * 2 * HALO) % LANES, 1)

        for f in range(p.fields):
            for i in range(HALO):
                s0[i, f] = edge_of(low, i * p.fields + f)
                s0[HALO + i, f] = edge_of(high, i * p.fields + f)

        def load0(row, f, t):
            if HALO <= row < HALO + p.rows:
                return state[row - HALO, f, mem, t * LANES : (t + 1) * LANES]
            i = row if row < HALO else row - p.rows
            if t == p.nt:
                return s0[i, f]
            source = low if row < HALO else high
            return source[(t * HALO + i % HALO) * p.fields + f, mem, :]

        def keep_zero(row, value):
            if row < HALO:
                return value * has_low
            if row >= HALO + p.rows:
                return value * has_high
            return value

        def store1(row, f, t, stepped):
            s1[row, f, t] = keep_zero(row, stepped)

        def store2(row, f, t, stepped):
            row = row + 1
            s2[row, f, t] = keep_zero(row, 0.75 * load0(row, f, t) + stepped)

        def store3(row, f, t, stepped):
            row = row + 2
            ahead[(t * p.rows + row - HALO) * p.fields + f, mem, :] = third_part * load0(row, f, t) + stepped

        step_once(p, full, load0, store1, False, 1.0)
        step_once(p, full - 2, lambda row, f, t: s1[row + 1, f, t], store2, False, 0.25)
        step_once(p, full - 4, lambda row, f, t: s2[row + 2, f, t], store3, True, two_thirds)
        return carry

    lax.fori_loop(0, parts, body, 0)

    wide = lane_ids((p.members, LANES))
    found = jnp.zeros((p.members, LANES), jnp.float32)
    every = p.groups * p.slots
    for j in range(p.np):
        at = ((p.first_patch + j) ^ me) * p.slots
        for o in range(p.slots):
            to = j * p.slots + o
            found = jnp.where(wide == to, pltpu.roll(ahead[table[at + o]], table[every + at + o], 1), found)
    seen[...] = found

    high, low_part = (a.astype(jnp.float32) for a in split(found))
    turned = jnp.transpose(jnp.concatenate([high, high, low_part], axis=0))
    depth = 3 * p.members
    extra = lax.broadcasted_iota(jnp.int32, (2 * SUB, depth), 0)
    ones = jnp.where((extra == 0) & (lane_ids((2 * SUB, depth)) < 2 * p.members), 1.0, 0.0).astype(jnp.float32)
    sides = [
        jnp.concatenate([turned[j * p.slots : (j + 1) * p.slots], ones], axis=0).astype(jnp.bfloat16) for j in range(p.np)
    ]
    lanes = lane_ids((p.slots + 2 * SUB, LANES))
    moments = jnp.zeros((p.slots + 2 * SUB, LANES), jnp.float32)
    joined = jnp.concatenate([a.astype(jnp.bfloat16) for a in (high, low_part, high)], axis=0)
    for j in range(p.np):
        part = jnp.dot(sides[j], joined, preferred_element_type=jnp.float32)
        moments = jnp.where((lanes >= j * p.slots) & (lanes < (j + 1) * p.slots), part, moments)
    for out in (keep, send):
        out[pl.ds(p.cell_rows, p.slots + SUB), :] = moments[: p.slots + SUB]
    for side in range(p.halves):
        out = keep if side == 0 else send
        half = core if side == 0 else 1 - core
        for t in range(p.nt):
            base = t * p.block
            begin = (t * p.rows + half * p.hrows) * p.fields
            high, low_part = split(jnp.concatenate([ahead[begin + i] for i in range(p.hrf)], axis=1))
            joined = jnp.concatenate([high, low_part, high], axis=0)
            result = None
            for j, first, stop in p.patches_of(t):
                part = jnp.dot(sides[j], joined, preferred_element_type=jnp.float32)
                if result is None:
                    result = part
                else:
                    at = lane_ids(part.shape) % LANES
                    result = jnp.where((at >= first) & (at < stop), part, result)
            for i in range(p.hrf):
                piece = result[:, i * LANES : (i + 1) * LANES]
                out[pl.ds(base + i * p.slots, p.slots), :] = piece[: p.slots]
                out[pl.ds(base + p.hrf * p.slots + i, 1), :] = piece[p.slots : p.slots + 1]
            for i in range(p.hrf, p.plain):
                out[pl.ds(base + p.hrf * p.slots + i, 1), :] = jnp.zeros((1, LANES), jnp.float32)


def solve_kernel(plan, obs, seen, own, factors, centres, keeps):
    p = plan
    n = p.slots
    me = lax.axis_index("mem")
    free = p.total - 1.0
    shape = (n, LANES)
    lane = lane_ids(shape)
    row = lax.broadcasted_iota(jnp.int32, shape, 0)
    group = lane // n * n
    eye = jnp.where(lane - group == row, 1.0, 0.0).astype(jnp.float32)
    lane_row = lane_ids((1, LANES))
    lane_sub = lane_ids((SUB, LANES))

    def pick(a, index):
        return jnp.take_along_axis(a, index, axis=1)

    def col(a):
        return pick(jnp.broadcast_to(a, shape), group + row)

    def spread_out(a):
        base = lane_ids(a.shape) // n * n
        return [pick(a, base + k) for k in range(n)]

    def product(parts, b):
        terms = [parts[k] * b[k : k + 1] for k in range(n)]
        while len(terms) > 1:
            terms = [sum(terms[i : i + 2][1:], terms[i]) for i in range(0, len(terms), 2)]
        return terms[0]

    given = [jnp.zeros((SUB, LANES), jnp.float32) for _ in range(4)]
    for j in range(p.np):
        source = (p.first_patch + j) ^ me
        line = jnp.broadcast_to(obs[pl.ds(source, 1), :], (SUB, LANES))
        mine = (lane_sub >= j * n) & (lane_sub < (j + 1) * n)
        for i, place in enumerate((0, 1, 2, 4)):
            given[i] = jnp.where(mine, pltpu.roll(line, (j * n - place * n) % LANES, 1), given[i])
    moments = own[pl.ds(p.cell_rows, n), :]
    sums = own[pl.ds(p.cell_rows + n, SUB), :]
    value, variance, loop, count = (a[0:1] for a in given)
    mean = sums[0:1] * (1.0 / p.total)
    slot = (lane_row % n).astype(jnp.float32)
    used = lane_row < p.np * n
    weight = jnp.where(used & (slot < count), jnp.exp(-0.35 * loop) / jnp.where(used, variance, 1.0), 0.0)
    root = jnp.sqrt(weight)
    root_col = col(root)
    mean_col = col(mean)
    scaled = root_col * (moments - p.total * mean_col * mean) * root
    bound = free + 0.5 * jnp.sum(pick(scaled, group + row), axis=0, keepdims=True)
    inverse = 1.0 / bound

    small = scaled * inverse
    t0 = free * inverse
    tf = t0 * eye + small
    tg = eye
    z0 = jnp.ones((1, LANES), jnp.float32)
    zg = None
    for repeat in range(NSI):
        f0 = 1.5 - 0.5 * t0
        ff = 1.5 * eye - 0.5 * tf
        parts = spread_out(ff)
        if zg is None:
            zg = -0.5 * z0 * tg
        else:
            zg = product(parts, zg) - 0.5 * z0 * tg
        z0 = z0 * f0
        if repeat < NSI - 1:
            square = product(parts, ff)
            bend = square - (0.5 * t0) * (ff + f0 * eye)
            tf = product(spread_out(square), tf)
            tg = bend if repeat == 0 else product(spread_out(bend), tg)
            t0 = t0 * f0 * f0
    zf = z0 * eye + product(spread_out(small), zg)
    scale = jnp.sqrt(free * inverse)
    spread = (scale * inverse) * root_col * zg * root
    down = root * (value - mean)
    for repeat in range(2):
        down = jnp.sum(zf * col(down), axis=0, keepdims=True)
    weights = product(spread_out(seen[...] - mean), spread) + root * down * inverse
    spread0 = scale * z0

    wide = lane_ids((p.members, LANES))
    high, low_part = (a.astype(jnp.float32) for a in split(weights))
    for j in range(p.np):
        here, there, last = (pltpu.roll(a, (i * n - j * n) % LANES, 1) for i, a in enumerate((high, high, low_part)))
        factors[j] = jnp.where(wide < n, here, jnp.where(wide < 2 * n, there, last))
        centres[j] = pick(jnp.broadcast_to(mean, shape), row + j * n)
        keeps[j] = pick(jnp.broadcast_to(spread0, (SUB, LANES)), jnp.full((SUB, LANES), j * n, jnp.int32))


def finish_kernel(plan, ahead, factors, centres, keeps, own, other, *rest):
    out, staged, sems = rest[-3:]
    p = plan
    n = p.slots
    core = lax.rem(lax.axis_index("mem"), 2)
    mixing = [(factors[j][:, : 3 * n].astype(jnp.bfloat16), centres[j], keeps[j][0:1]) for j in range(p.np)]

    def line_copy(r, f):
        cols = pl.ds(p.first * LANES, p.nt * LANES)
        return pltpu.make_async_copy(staged.at[r, f], out.at[:, f, r, cols], sems.at[r, f])

    for r in range(p.rows):
        half, begin = divmod(r, p.hrows)
        begin *= p.fields
        at_own = half == core
        for t in range(p.nt):
            pieces = []
            for f in range(p.fields):
                at = t * p.block + (begin + f) * n
                pieces.append(jnp.where(at_own, own[at : at + n, :], other[at : at + n, :]))
            at = t * p.block + p.hrf * n + begin
            plain = jnp.where(at_own, own[at : at + p.fields, :], other[at : at + p.fields, :])
            results = []
            for j, first, stop in p.patches_of(t):
                mine, centre, keep0 = mixing[j]
                centred = [pieces[f] - centre * plain[f : f + 1, :] for f in range(p.fields)]
                high, low_part = split(jnp.concatenate(centred, axis=1))
                joined = jnp.concatenate([high, low_part, high], axis=0)
                results.append((jnp.dot(mine, joined, preferred_element_type=jnp.float32), keep0, first, stop))
            for f in range(p.fields):
                x = ahead[(t * p.rows + r) * p.fields + f]
                average = plain[f : f + 1, :] * (1.0 / p.total)
                final = None
                for update, keep0, first, stop in results:
                    part = (1.0 - keep0) * average + keep0 * x + update[:, f * LANES : (f + 1) * LANES]
                    if final is None:
                        final = part
                    else:
                        at = lane_ids(part.shape)
                        final = jnp.where((at >= first) & (at < stop), part, final)
                staged[r, f, :, t * LANES : (t + 1) * LANES] = final
        for f in range(p.fields):
            line_copy(r, f).start()
    for r in range(p.rows):
        for f in range(p.fields):
            line_copy(r, f).wait()


def core_sums(plan, keep, send):
    return keep + lax.ppermute(send, "mem", [(i, i ^ 1) for i in range(plan.groups)])


def sum_phase(plan, phase, total, waited=None):
    p = plan
    bits = [1 << i for i in range(1, p.groups.bit_length() - 1)]
    if phase >= len(bits):
        return total
    even = bits[phase]
    odd = bits[(phase + len(bits) // 2) % len(bits)]
    there = lax.ppermute(total, "mem", [(i, i ^ (odd if i & 1 else even)) for i in range(p.groups)])
    return (total if waited is None else after(total, waited)) + there


def last_sums(plan, total, waited=None):
    p = plan
    for phase in range(1, p.groups.bit_length() - 2):
        total = sum_phase(p, phase, total, waited)
    return total, lax.ppermute(total, "mem", [(i, i ^ 1) for i in range(p.groups)])


def after(value, *others):
    return lax.optimization_barrier((value,) + others)[0]


def per_device(ensemble, obs_value, obs_var, obs_cell, obs_loop, obs_count):
    groups = lax.axis_size("mem")
    bands = lax.axis_size("lat")
    slots = obs_cell.shape[-1]
    p = Plan(ensemble, slots, groups)
    chunks = [p.chunk(c) for c in range(len(p.counts))]
    f32 = jnp.float32
    shape = pltpu.VMEM

    given = (obs_value, obs_var, obs_loop, obs_cell)

    def pack(h, source):
        sent = (h.message, p.members, LANES)
        more = given if h.first == 0 else ()
        return call(
            functools.partial(pack_kernel, h),
            [pltpu.VMEM((p.rows, p.fields, p.members, (h.nt + 1) * LANES), f32), pltpu.HBM(sent, f32), pltpu.HBM(sent, f32)]
            + [pltpu.VMEM((1, LANES), f32) for _ in more[:1]],
            [HBM] * (1 + len(more)),
            [
                pltpu.VMEM(sent, f32),
                pltpu.VMEM(sent, f32),
                pltpu.VMEM((p.members, p.fields, p.rows, h.nt * LANES), f32),
                pltpu.VMEM((2, p.members, p.fields, p.rows, LANES), f32),
                pltpu.SemaphoreType.DMA((p.members // SUB, 3)),
                pltpu.SemaphoreType.DMA((p.members // SUB, 4)),
            ]
            + [pltpu.VMEM(a.shape, a.dtype) for a in more]
            + [pltpu.VMEM((SUB, LANES), f32) for _ in more[:1]]
            + [pltpu.SemaphoreType.DMA((len(more),)) for _ in more[:1]],
            out_specs=[VMEM, HBM, HBM] + [VMEM for _ in more[:1]],
            name="pack",
        )(*(pltpu.with_memory_space_constraint(a, pltpu.HBM) for a in (source,) + more))

    packed = [pack(chunks[0], ensemble)]
    obs = jnp.where(jnp.arange(LANES) < 4 * slots, packed[0][3], obs_count.astype(f32))
    bit = 1
    while bit < groups:
        step = 2 if bit == 1 or bit * 4 > groups else 4
        there = [lax.ppermute(obs, "mem", [(i, i ^ (bit * b)) for i in range(groups)]) for b in range(1, step)]
        obs = jnp.concatenate([obs] + there, axis=0)
        bit *= step

    packed += [pack(h, after(ensemble, obs)) for h in chunks[1:]]
    messages = [a for part in packed for a in part[1:3]]
    swaps = [[pair for i in range(begin, bands - 1, 2) for pair in ((i, i + 1), (i + 1, i))] for begin in range(2)]
    halo = [[lax.ppermute(messages[2 * c + i], "lat", swaps[i]) for i in range(2)] for c in range(len(chunks))]

    table = call(
        table_kernel,
        [pltpu.SMEM((2 * groups * slots,), jnp.int32)],
        [ANY],
        [pltpu.SemaphoreType.DMA],
        out_specs=[SMEM],
        name="places",
    )(places(p, chunks, lax.axis_index("mem"), obs[:, 3 * slots : 4 * slots].astype(jnp.int32)))[0]
    table = pltpu.with_memory_space_constraint(table, pltpu.SMEM)

    def near(x):
        return pltpu.with_memory_space_constraint(x, pltpu.VMEM)

    def far(x):
        return pltpu.with_memory_space_constraint(x, pltpu.HBM)

    parts = []
    early = None
    for c, h in enumerate(chunks):
        stage = (p.rows + 2 * HALO, p.fields, h.nt + 1, SUB, LANES)
        ahead, seen, keep, send = call(
            functools.partial(forecast_kernel, h),
            [
                shape((h.nt * p.rows * p.fields, p.members, LANES), f32),
                shape((p.members, LANES), f32),
                shape((h.total_rows, LANES), f32),
                shape((h.total_rows, LANES), f32),
            ],
            [SMEM, VMEM, ANY, ANY],
            [pltpu.VMEM((2 * HALO, p.fields, SUB, LANES), f32), pltpu.VMEM(stage, f32), pltpu.VMEM(stage, f32)]
            + [pltpu.VMEM((h.message, p.members, LANES), f32)] * 2
            + [pltpu.SemaphoreType.DMA((p.members // SUB, 2))],
            cost=(1024, h.nt * (6 << 20) if c else 1024),
            name="forecast",
        )(table, near(packed[c][0] if early is None else after(packed[c][0], early)), *map(far, halo[c]))
        if c == 0:
            early = lax.cond(
                obs_count[0, 0] >= 0,
                lambda keep, send: sum_phase(p, 0, core_sums(p, keep, send)),
                lambda keep, send: keep,
                keep,
                send,
            )
            parts.append((ahead, seen, early))
        else:
            if c == 1:
                first = last_sums(p, parts[0][2])
                send = after(send, first[0])
            early = send
            parts.append((ahead, seen, sum_phase(p, 0, core_sums(p, keep, send))))
    new = None
    for c, h in enumerate(chunks):
        ahead, seen, total = parts[c]
        own, other = first if c == 0 and len(chunks) > 1 else last_sums(p, total, new)
        new = finish(p, h, obs, (ahead, seen, own, other), new, ensemble.shape)
    return new


def finish(plan, h, obs, parts, new, whole):
    p = plan
    f32 = jnp.float32
    ahead, seen, own, other = parts

    def near(*arrays):
        return [pltpu.with_memory_space_constraint(a, pltpu.VMEM) for a in arrays]

    solved = call(
        functools.partial(solve_kernel, h),
        [
            pltpu.VMEM((h.np, p.members, LANES), f32),
            pltpu.VMEM((h.np, p.slots, LANES), f32),
            pltpu.VMEM((h.np, SUB, LANES), f32),
        ],
        [VMEM] * 3,
        cost=(1024, 6 << 20),
        name="solve",
    )(*near(obs, seen, own))
    before = [] if new is None else [new]
    return call(
        functools.partial(finish_kernel, h),
        pltpu.HBM(whole, f32),
        [VMEM] * 6 + [HBM] * len(before),
        [pltpu.VMEM((p.rows, p.fields, p.members, h.nt * LANES), f32), pltpu.SemaphoreType.DMA((p.rows, p.fields))],
        cost=(1024, h.nt * (4 << 20)),
        name="finish",
        out_specs=HBM,
        alias={6: 0} if before else {},
    )(*near(ahead, *solved, own, other), *before)


def solution(mesh):
    placed = (
        P("mem", None, "lat", None),
        P(None, ("mem", "lat"), None),
        P(None, ("mem", "lat"), None),
        P(None, ("mem", "lat"), None),
        P(None, ("mem", "lat"), None),
        P(None, ("mem", "lat")),
    )
    return jax.shard_map(
        per_device,
        mesh=mesh,
        in_specs=placed,
        out_specs=P("mem", None, "lat", None),
        check_vma=False,
    )
```

```python
import copy
import functools

import jax
import jax.numpy as jnp
from jax import lax
from jax.experimental import pallas as pl
from jax.experimental.pallas import tpu as pltpu
from jax.sharding import PartitionSpec as P

NSI = 5
HALO = 3
LANES = 128
SUB = 8

time_step = 0.15
viscosity = 0.1
third_part = 1.0 / 3.0
two_thirds = 2.0 / 3.0

HIGHEST = lax.Precision.HIGHEST
VMEM = pl.BlockSpec(memory_space=pltpu.VMEM)
SMEM = pl.BlockSpec(memory_space=pltpu.SMEM)
HBM = pl.BlockSpec(memory_space=pltpu.HBM)
ANY = pl.BlockSpec(memory_space=pl.ANY)
KERNEL_VMEM = 12 << 20


def call(kernel, out_shape, in_specs, scratch=(), cost=(1 << 20, 1 << 20), name=None, out_specs=None, alias={}):
    flops, nbytes = cost
    return pl.pallas_call(
        kernel,
        out_shape=out_shape,
        in_specs=in_specs,
        out_specs=out_specs or [VMEM] * len(out_shape),
        scratch_shapes=list(scratch),
        input_output_aliases=alias,
        compiler_params=pltpu.CompilerParams(vmem_limit_bytes=KERNEL_VMEM),
        cost_estimate=pl.CostEstimate(flops=flops, bytes_accessed=nbytes, transcendentals=0),
        name=name,
    )


def chunk_tiles(tiles, most, step):
    most = max(step, most // step * step)
    count = -(-tiles // most)
    units = tiles // step
    return [(units // count + (1 if i < units % count else 0)) * step for i in range(count)]


class Plan:
    def __init__(self, ensemble, slots, groups):
        self.members, self.fields, self.rows, self.columns = ensemble.shape
        self.total = self.members * groups
        self.slots = slots
        self.groups = groups
        self.width = self.columns // groups
        self.tiles = self.columns // LANES
        self.q = max(1, LANES // self.width)
        most = LANES // (slots * self.q)
        self.counts = chunk_tiles(self.tiles, min(most, -(-self.tiles // 2)), max(1, self.width // LANES))
        self.counts = [4, 4] if self.counts == [4, 4] else self.counts
        self.starts = [sum(self.counts[:i]) for i in range(len(self.counts))]
        self.halves = 2
        self.hrows = self.rows // self.halves
        self.hrf = self.hrows * self.fields
        self.edge_groups = HALO * self.fields
        self.per_edge = LANES // (2 * HALO)
        self.edge_tiles = -(-self.edge_groups // self.per_edge)
        self.plain = -(-self.hrf // SUB) * SUB
        self.block = self.hrf * slots + self.plain

    def chunk(self, c):
        p = copy.copy(self)
        p.nt = self.counts[c]
        p.first = self.starts[c]
        p.after = (p.first + p.nt) % self.tiles
        p.before = (p.first - 1) % self.tiles
        p.np = p.nt * LANES // self.width
        p.first_patch = p.first * LANES // self.width
        p.bands = lax.axis_size("lat")
        p.message = p.nt * self.edge_groups + self.edge_tiles
        p.cell_rows = p.nt * self.block
        p.total_rows = p.cell_rows + p.slots + SUB
        return p

    def patches_of(self, tile):
        if self.width >= LANES:
            return [(tile * LANES // self.width, 0, LANES)]
        return [(tile * self.q + i, i * self.width, (i + 1) * self.width) for i in range(self.q)]


def lane_ids(shape):
    return lax.broadcasted_iota(jnp.int32, shape, len(shape) - 1)


def pack_kernel(plan, raw, *rest):
    p = plan
    lane = lane_ids((SUB, LANES))
    parts = p.members // SUB
    given = []
    if p.first == 0:
        given, rest = rest[:4], rest[4:]
        row_out, (taken, lines, given_sems), rest = rest[3], (rest[-6:-2], *rest[-2:]), rest[:3] + rest[4:-6]
    state, first_out, second_out, up, down, arrived, beside, sems, out_sems = rest
    given_copies = []
    for i, a in enumerate(given):
        given_copies.append(pltpu.make_async_copy(a, taken[i], given_sems.at[i]))
    odd = lax.rem(lax.axis_index("lat"), 2)

    def part_copies(kk):
        part = pl.ds(kk * SUB, SUB)
        takes = [(arrived, p.first, p.nt)] + [(beside.at[i], t, 1) for i, t in enumerate((p.after, p.before))]
        return [
            pltpu.make_async_copy(raw.at[part, :, :, pl.ds(t * LANES, n * LANES)], to.at[part], sems.at[kk, i])
            for i, (to, t, n) in enumerate(takes)
        ]

    cut = p.nt // 2
    pieces = [(0, cut * p.edge_groups), (cut * p.edge_groups, p.message)] if cut else [(0, p.message)]

    def message_copies(kk, piece, swapped=0):
        part = pl.ds(kk * SUB, SUB)
        lines = pl.ds(pieces[piece][0], pieces[piece][1] - pieces[piece][0])
        inner = (up, down) if swapped == 0 else (down, up)
        return [
            pltpu.make_async_copy(a.at[lines, part, :], b.at[lines, part, :], out_sems.at[kk, 2 * piece + i])
            for i, (a, b) in enumerate(zip(inner, (first_out, second_out)))
        ]

    def send_out(kk, piece):
        for swapped in range(2):

            @pl.when(odd == swapped)
            def _():
                for copy_out in message_copies(kk, piece, swapped):
                    copy_out.start()

    for kk in range(parts):
        for copy_in in part_copies(kk):
            copy_in.start()
    for copy_in in given_copies:
        copy_in.start()

    def body(kk, carry):
        mem = pl.ds(pl.multiple_of(kk * SUB, SUB), SUB)
        for copy_in in part_copies(kk):
            copy_in.wait()

        for i in range(p.nt):
            if cut and i == cut:
                send_out(kk, 0)
            cols = slice(i * LANES, (i + 1) * LANES)
            for f in range(p.fields):
                for r in range(p.rows):
                    x = arrived[mem, f, r, cols]
                    state[r, f, mem, cols] = x
                    if r >= p.rows - HALO:
                        up[(i * HALO + r - (p.rows - HALO)) * p.fields + f, mem, :] = x
                    if r < HALO:
                        down[(i * HALO + r) * p.fields + f, mem, :] = x
        for r in range(p.rows):
            for f in range(p.fields):
                edge = jnp.where(lane < LANES // 2, beside[0, mem, f, r, :], beside[1, mem, f, r, :])
                state[r, f, mem, p.nt * LANES :] = edge
        for out, skipped in ((up, p.rows - HALO), (down, 0)):
            for e in range(p.edge_tiles):
                packed = jnp.zeros((SUB, LANES), jnp.float32)
                for g in range(e * p.per_edge, min((e + 1) * p.per_edge, p.edge_groups)):
                    i, f = divmod(g, p.fields)
                    place = (g - e * p.per_edge) * 2 * HALO
                    inside = (lane >= place) & (lane < place + 2 * HALO)
                    edge = state[i + skipped, f, mem, p.nt * LANES :]
                    packed = jnp.where(inside, pltpu.roll(edge, place + HALO, 1), packed)
                out[p.nt * p.edge_groups + e, mem, :] = packed

        send_out(kk, len(pieces) - 1)
        return carry

    lax.fori_loop(0, parts, body, 0)
    if given:
        for copy_in in given_copies:
            copy_in.wait()
        row = jnp.zeros((SUB, LANES), jnp.float32)
        for i, a in enumerate(given):
            lines[i : i + 1, : p.slots] = jnp.broadcast_to(taken[i][0].astype(jnp.float32), (1, p.slots))
            line = pltpu.roll(jnp.broadcast_to(lines[i : i + 1, :], (SUB, LANES)), i * p.slots, 1)
            row = jnp.where((lane >= i * p.slots) & (lane < (i + 1) * p.slots), line, row)
        row_out[...] = row[:1]
    for kk in range(parts):
        for piece in range(len(pieces)):
            for copy_out in message_copies(kk, piece):
                copy_out.wait()


def step_once(p, rows_in, load, store, last, scale):
    lane = lane_ids((SUB, LANES))
    ring = p.nt + 1
    out_tiles = p.nt if last else ring
    k = scale * time_step * viscosity
    centre = scale * (1.0 - 4.0 * time_step * viscosity)
    for first in range(0, p.fields, 2):
        pair = range(first, min(first + 2, p.fields))
        held = {row: {f: [load(row, f, t) for t in range(ring)] for f in pair} for row in range(2)}
        for row in range(1, rows_in - 1):
            held[row + 1] = {f: [load(row + 1, f, t) for t in range(ring)] for f in pair}
            rolled = {}

            def turn(f, t, by):
                if (f, t, by) not in rolled:
                    rolled[f, t, by] = pltpu.roll(held[row][f][t], by, 1)
                return rolled[f, t, by]

            for t in range(out_tiles):
                u, v = ((held[row][i][t] if i in held[row] else load(row, i, t)) * (scale * time_step * 0.5) for i in range(2))
                ce, cw, cn, cs = k - u, k + u, k - v, k + v
                for f in pair:
                    west = pltpu.roll(jnp.where(lane == LANES - 1, held[row][f][(t - 1) % ring], held[row][f][t]), 1, 1)
                    east = pltpu.roll(jnp.where(lane == 0, held[row][f][(t + 1) % ring], held[row][f][t]), LANES - 1, 1)
                    moved = (ce * east + cw * west) + (cn * held[row + 1][f][t] + cs * held[row - 1][f][t])
                    store(row, f, t, centre * held[row][f][t] + moved)
            del held[row - 1]


def split(x):
    high = x.astype(jnp.bfloat16)
    return high, (x - high.astype(jnp.float32)).astype(jnp.bfloat16)


def places(p, chunks, me, cells):
    line = jnp.arange(p.groups, dtype=jnp.int32)[:, None]
    patch = line ^ me
    first = jnp.zeros_like(patch)
    for h in chunks:
        first = jnp.where(patch >= h.first_patch, h.first_patch, first)
    slot = jnp.arange(p.slots, dtype=jnp.int32)[None, :]
    column = cells % p.width + (patch - first) * p.width
    r = cells // p.width % p.rows
    f = cells // (p.width * p.rows)
    tile, lane = column // LANES, column % LANES
    shift = ((patch - first) * p.slots + slot - lane) % LANES
    table = [(tile * p.rows + r) * p.fields + f, shift]
    return jnp.stack(table).reshape(-1)


def table_kernel(table_in, table, sem):
    copy_in = pltpu.make_async_copy(table_in, table, sem)
    copy_in.start()
    copy_in.wait()


def forecast_kernel(plan, table, state, first_in, second_in, ahead, seen, keep, send, s0, s1, s2, low, high, sems, *rest):
    p = plan
    ahead_out = ahead
    if rest:
        ahead = rest[0]

    def ahead_copy(kk):
        part = pl.ds(kk * SUB, SUB)
        return pltpu.make_async_copy(ahead.at[:, part, :], ahead_out.at[:, part, :], rest[1].at[kk])

    full = p.rows + 2 * HALO
    band = lax.axis_index("lat")
    me = lax.axis_index("mem")
    core = lax.rem(me, 2)
    has_low = (band > 0).astype(jnp.float32)
    has_high = (band < p.bands - 1).astype(jnp.float32)
    lane = lane_ids((SUB, LANES))
    parts = p.members // SUB

    def part_copies(kk, swapped=0):
        part = pl.ds(kk * SUB, SUB)
        inner = (high, low) if swapped == 0 else (low, high)
        return [
            pltpu.make_async_copy(a.at[:, part, :], b.at[:, part, :], sems.at[kk, i])
            for i, (a, b) in enumerate(zip((first_in, second_in), inner))
        ]

    def start_copies(kk):
        for swapped in range(2):

            @pl.when(lax.rem(band, 2) == swapped)
            def _():
                for copy_in in part_copies(kk, swapped):
                    copy_in.start()

    start_copies(0)

    def body(kk, carry):
        mem = pl.ds(pl.multiple_of(kk * SUB, SUB), SUB)

        @pl.when(kk + 1 < parts)
        def _():
            start_copies(kk + 1)

        for copy_in in part_copies(kk):
            copy_in.wait()

        def edge_of(source, g):
            e, place = divmod(g, p.per_edge)
            return pltpu.roll(source[p.nt * p.edge_groups + e, mem, :], (LANES - HALO - place * 2 * HALO) % LANES, 1)

        for f in range(p.fields):
            for i in range(HALO):
                s0[i, f] = edge_of(low, i * p.fields + f)
                s0[HALO + i, f] = edge_of(high, i * p.fields + f)

        def load0(row, f, t):
            if HALO <= row < HALO + p.rows:
                return state[row - HALO, f, mem, t * LANES : (t + 1) * LANES]
            i = row if row < HALO else row - p.rows
            if t == p.nt:
                return s0[i, f]
            source = low if row < HALO else high
            return source[(t * HALO + i % HALO) * p.fields + f, mem, :]

        def keep_zero(row, value):
            if row < HALO:
                return value * has_low
            if row >= HALO + p.rows:
                return value * has_high
            return value

        def store1(row, f, t, stepped):
            s1[row, f, t] = keep_zero(row, stepped)

        def store2(row, f, t, stepped):
            row = row + 1
            s2[row, f, t] = keep_zero(row, 0.75 * load0(row, f, t) + stepped)

        def store3(row, f, t, stepped):
            row = row + 2
            ahead[(t * p.rows + row - HALO) * p.fields + f, mem, :] = third_part * load0(row, f, t) + stepped

        step_once(p, full, load0, store1, False, 1.0)
        step_once(p, full - 2, lambda row, f, t: s1[row + 1, f, t], store2, False, 0.25)
        step_once(p, full - 4, lambda row, f, t: s2[row + 2, f, t], store3, True, two_thirds)
        if rest:
            ahead_copy(kk).start()
        return carry

    lax.fori_loop(0, parts, body, 0)

    wide = lane_ids((p.members, LANES))
    found = jnp.zeros((p.members, LANES), jnp.float32)
    every = p.groups * p.slots
    for j in range(p.np):
        at = ((p.first_patch + j) ^ me) * p.slots
        for o in range(p.slots):
            to = j * p.slots + o
            found = jnp.where(wide == to, pltpu.roll(ahead[table[at + o]], table[every + at + o], 1), found)
    seen[...] = found

    high, low_part = (a.astype(jnp.float32) for a in split(found))
    turned = jnp.transpose(jnp.concatenate([high, high, low_part], axis=0))
    depth = 3 * p.members
    extra = lax.broadcasted_iota(jnp.int32, (2 * SUB, depth), 0)
    ones = jnp.where((extra == 0) & (lane_ids((2 * SUB, depth)) < 2 * p.members), 1.0, 0.0).astype(jnp.float32)
    sides = [
        jnp.concatenate([turned[j * p.slots : (j + 1) * p.slots], ones], axis=0).astype(jnp.bfloat16) for j in range(p.np)
    ]
    lanes = lane_ids((p.slots + 2 * SUB, LANES))
    moments = jnp.zeros((p.slots + 2 * SUB, LANES), jnp.float32)
    joined = jnp.concatenate([a.astype(jnp.bfloat16) for a in (high, low_part, high)], axis=0)
    for j in range(p.np):
        part = jnp.dot(sides[j], joined, preferred_element_type=jnp.float32)
        moments = jnp.where((lanes >= j * p.slots) & (lanes < (j + 1) * p.slots), part, moments)
    for out in (keep, send):
        out[pl.ds(p.cell_rows, p.slots + SUB), :] = moments[: p.slots + SUB]
    for side in range(p.halves):
        out = keep if side == 0 else send
        half = core if side == 0 else 1 - core
        for t in range(p.nt):
            base = t * p.block
            begin = (t * p.rows + half * p.hrows) * p.fields
            high, low_part = split(jnp.concatenate([ahead[begin + i] for i in range(p.hrf)], axis=1))
            joined = jnp.concatenate([high, low_part, high], axis=0)
            result = None
            for j, first, stop in p.patches_of(t):
                part = jnp.dot(sides[j], joined, preferred_element_type=jnp.float32)
                if result is None:
                    result = part
                else:
                    at = lane_ids(part.shape) % LANES
                    result = jnp.where((at >= first) & (at < stop), part, result)
            for i in range(p.hrf):
                piece = result[:, i * LANES : (i + 1) * LANES]
                out[pl.ds(base + i * p.slots, p.slots), :] = piece[: p.slots]
                out[pl.ds(base + p.hrf * p.slots + i, 1), :] = piece[p.slots : p.slots + 1]
            for i in range(p.hrf, p.plain):
                out[pl.ds(base + p.hrf * p.slots + i, 1), :] = jnp.zeros((1, LANES), jnp.float32)
    if rest:
        for kk in range(parts):
            ahead_copy(kk).wait()


def solve_kernel(plan, obs, seen, own, factors, centres, keeps):
    p = plan
    n = p.slots
    me = lax.axis_index("mem")
    free = p.total - 1.0
    shape = (n, LANES)
    lane = lane_ids(shape)
    row = lax.broadcasted_iota(jnp.int32, shape, 0)
    group = lane // n * n
    eye = jnp.where(lane - group == row, 1.0, 0.0).astype(jnp.float32)
    lane_row = lane_ids((1, LANES))
    lane_sub = lane_ids((SUB, LANES))

    def pick(a, index):
        return jnp.take_along_axis(a, index, axis=1)

    def col(a):
        return pick(jnp.broadcast_to(a, shape), group + row)

    def spread_out(a):
        base = lane_ids(a.shape) // n * n
        return [pick(a, base + k) for k in range(n)]

    def product(parts, b):
        terms = [parts[k] * b[k : k + 1] for k in range(n)]
        while len(terms) > 1:
            terms = [sum(terms[i : i + 2][1:], terms[i]) for i in range(0, len(terms), 2)]
        return terms[0]

    given = [jnp.zeros((SUB, LANES), jnp.float32) for _ in range(4)]
    for j in range(p.np):
        source = (p.first_patch + j) ^ me
        line = jnp.broadcast_to(obs[pl.ds(source, 1), :], (SUB, LANES))
        mine = (lane_sub >= j * n) & (lane_sub < (j + 1) * n)
        for i, place in enumerate((0, 1, 2, 4)):
            given[i] = jnp.where(mine, pltpu.roll(line, (j * n - place * n) % LANES, 1), given[i])
    moments = own[pl.ds(p.cell_rows, n), :]
    sums = own[pl.ds(p.cell_rows + n, SUB), :]
    value, variance, loop, count = (a[0:1] for a in given)
    mean = sums[0:1] * (1.0 / p.total)
    slot = (lane_row % n).astype(jnp.float32)
    used = lane_row < p.np * n
    weight = jnp.where(used & (slot < count), jnp.exp(-0.35 * loop) / jnp.where(used, variance, 1.0), 0.0)
    root = jnp.sqrt(weight)
    root_col = col(root)
    mean_col = col(mean)
    scaled = root_col * (moments - p.total * mean_col * mean) * root
    bound = free + 0.5 * jnp.sum(pick(scaled, group + row), axis=0, keepdims=True)
    inverse = 1.0 / bound

    small = scaled * inverse
    t0 = free * inverse
    tf = t0 * eye + small
    tg = eye
    z0 = jnp.ones((1, LANES), jnp.float32)
    zg = None
    for repeat in range(NSI):
        f0 = 1.5 - 0.5 * t0
        ff = 1.5 * eye - 0.5 * tf
        parts = spread_out(ff)
        if zg is None:
            zg = -0.5 * z0 * tg
        else:
            zg = product(parts, zg) - 0.5 * z0 * tg
        z0 = z0 * f0
        if repeat < NSI - 1:
            square = product(parts, ff)
            bend = square - (0.5 * t0) * (ff + f0 * eye)
            tf = product(spread_out(square), tf)
            tg = bend if repeat == 0 else product(spread_out(bend), tg)
            t0 = t0 * f0 * f0
    zf = z0 * eye + product(spread_out(small), zg)
    scale = jnp.sqrt(free * inverse)
    spread = (scale * inverse) * root_col * zg * root
    down = root * (value - mean)
    for repeat in range(2):
        down = jnp.sum(zf * col(down), axis=0, keepdims=True)
    weights = product(spread_out(seen[...] - mean), spread) + root * down * inverse
    spread0 = scale * z0

    wide = lane_ids((p.members, LANES))
    high, low_part = (a.astype(jnp.float32) for a in split(weights))
    for j in range(p.np):
        here, there, last = (pltpu.roll(a, (i * n - j * n) % LANES, 1) for i, a in enumerate((high, high, low_part)))
        factors[j] = jnp.where(wide < n, here, jnp.where(wide < 2 * n, there, last))
        centres[j] = pick(jnp.broadcast_to(mean, shape), row + j * n)
        keeps[j] = pick(jnp.broadcast_to(spread0, (SUB, LANES)), jnp.full((SUB, LANES), j * n, jnp.int32))


def finish_kernel(plan, ahead, factors, centres, keeps, own, other, *rest):
    out, staged, sems = rest[-3:]
    p = plan
    n = p.slots
    core = lax.rem(lax.axis_index("mem"), 2)
    mixing = [(factors[j][:, : 3 * n].astype(jnp.bfloat16), centres[j], keeps[j][0:1]) for j in range(p.np)]

    def line_copy(r, f):
        cols = pl.ds(p.first * LANES, p.nt * LANES)
        return pltpu.make_async_copy(staged.at[r, f], out.at[:, f, r, cols], sems.at[r, f])

    for r in range(p.rows):
        half, begin = divmod(r, p.hrows)
        begin *= p.fields
        at_own = half == core
        for t in range(p.nt):
            pieces = []
            for f in range(p.fields):
                at = t * p.block + (begin + f) * n
                pieces.append(jnp.where(at_own, own[at : at + n, :], other[at : at + n, :]))
            at = t * p.block + p.hrf * n + begin
            plain = jnp.where(at_own, own[at : at + p.fields, :], other[at : at + p.fields, :])
            results = []
            for j, first, stop in p.patches_of(t):
                mine, centre, keep0 = mixing[j]
                centred = [pieces[f] - centre * plain[f : f + 1, :] for f in range(p.fields)]
                high, low_part = split(jnp.concatenate(centred, axis=1))
                joined = jnp.concatenate([high, low_part, high], axis=0)
                results.append((jnp.dot(mine, joined, preferred_element_type=jnp.float32), keep0, first, stop))
            for f in range(p.fields):
                x = ahead[(t * p.rows + r) * p.fields + f]
                average = plain[f : f + 1, :] * (1.0 / p.total)
                final = None
                for update, keep0, first, stop in results:
                    part = (1.0 - keep0) * average + keep0 * x + update[:, f * LANES : (f + 1) * LANES]
                    if final is None:
                        final = part
                    else:
                        at = lane_ids(part.shape)
                        final = jnp.where((at >= first) & (at < stop), part, final)
                staged[r, f, :, t * LANES : (t + 1) * LANES] = final
        for f in range(p.fields):
            line_copy(r, f).start()
    for r in range(p.rows):
        for f in range(p.fields):
            line_copy(r, f).wait()


def core_sums(plan, keep, send):
    return keep + lax.ppermute(send, "mem", [(i, i ^ 1) for i in range(plan.groups)])


def sum_phase(plan, phase, total, waited=None):
    p = plan
    bits = [1 << i for i in range(1, p.groups.bit_length() - 1)]
    if phase >= len(bits):
        return total
    even = bits[phase]
    odd = bits[(phase + len(bits) // 2) % len(bits)]
    there = lax.ppermute(total, "mem", [(i, i ^ (odd if i & 1 else even)) for i in range(p.groups)])
    return (total if waited is None else after(total, waited)) + there


def last_sums(plan, total, waited=None):
    p = plan
    for phase in range(1, p.groups.bit_length() - 2):
        total = sum_phase(p, phase, total, waited)
    return total, lax.ppermute(total, "mem", [(i, i ^ 1) for i in range(p.groups)])


def after(value, *others):
    return lax.optimization_barrier((value,) + others)[0]


def per_device(ensemble, obs_value, obs_var, obs_cell, obs_loop, obs_count):
    groups = lax.axis_size("mem")
    bands = lax.axis_size("lat")
    slots = obs_cell.shape[-1]
    p = Plan(ensemble, slots, groups)
    chunks = [p.chunk(c) for c in range(len(p.counts))]
    f32 = jnp.float32
    shape = pltpu.VMEM

    given = (obs_value, obs_var, obs_loop, obs_cell)

    def pack(h, source):
        sent = (h.message, p.members, LANES)
        more = given if h.first == 0 else ()
        return call(
            functools.partial(pack_kernel, h),
            [pltpu.VMEM((p.rows, p.fields, p.members, (h.nt + 1) * LANES), f32), pltpu.HBM(sent, f32), pltpu.HBM(sent, f32)]
            + [pltpu.VMEM((1, LANES), f32) for _ in more[:1]],
            [HBM] * (1 + len(more)),
            [
                pltpu.VMEM(sent, f32),
                pltpu.VMEM(sent, f32),
                pltpu.VMEM((p.members, p.fields, p.rows, h.nt * LANES), f32),
                pltpu.VMEM((2, p.members, p.fields, p.rows, LANES), f32),
                pltpu.SemaphoreType.DMA((p.members // SUB, 3)),
                pltpu.SemaphoreType.DMA((p.members // SUB, 4)),
            ]
            + [pltpu.VMEM(a.shape, a.dtype) for a in more]
            + [pltpu.VMEM((SUB, LANES), f32) for _ in more[:1]]
            + [pltpu.SemaphoreType.DMA((len(more),)) for _ in more[:1]],
            out_specs=[VMEM, HBM, HBM] + [VMEM for _ in more[:1]],
            name="pack",
        )(*(pltpu.with_memory_space_constraint(a, pltpu.HBM) for a in (source,) + more))

    packed = [pack(chunks[0], ensemble)]
    obs = jnp.where(jnp.arange(LANES) < 4 * slots, packed[0][3], obs_count.astype(f32))
    bit = 1
    while bit < groups:
        step = 2 if bit == 1 or bit * 4 > groups else 4
        there = [lax.ppermute(obs, "mem", [(i, i ^ (bit * b)) for i in range(groups)]) for b in range(1, step)]
        obs = jnp.concatenate([obs] + there, axis=0)
        bit *= step

    packed += [pack(h, after(ensemble, obs)) for h in chunks[1:]]
    messages = [a for part in packed for a in part[1:3]]
    swaps = [[pair for i in range(begin, bands - 1, 2) for pair in ((i, i + 1), (i + 1, i))] for begin in range(2)]
    halo = [[lax.ppermute(messages[2 * c + i], "lat", swaps[i]) for i in range(2)] for c in range(len(chunks))]

    table = call(
        table_kernel,
        [pltpu.SMEM((2 * groups * slots,), jnp.int32)],
        [ANY],
        [pltpu.SemaphoreType.DMA],
        out_specs=[SMEM],
        name="places",
    )(places(p, chunks, lax.axis_index("mem"), obs[:, 3 * slots : 4 * slots].astype(jnp.int32)))[0]
    table = pltpu.with_memory_space_constraint(table, pltpu.SMEM)

    def near(x):
        return pltpu.with_memory_space_constraint(x, pltpu.VMEM)

    def far(x):
        return pltpu.with_memory_space_constraint(x, pltpu.HBM)

    parts = []
    early = None
    for c, h in enumerate(chunks):
        stage = (p.rows + 2 * HALO, p.fields, h.nt + 1, SUB, LANES)
        ahead, seen, keep, send = call(
            functools.partial(forecast_kernel, h),
            [
                (shape if c == len(chunks) - 1 else pltpu.HBM)((h.nt * p.rows * p.fields, p.members, LANES), f32),
                shape((p.members, LANES), f32),
                shape((h.total_rows, LANES), f32),
                shape((h.total_rows, LANES), f32),
            ],
            [SMEM, VMEM, ANY, ANY],
            [pltpu.VMEM((2 * HALO, p.fields, SUB, LANES), f32), pltpu.VMEM(stage, f32), pltpu.VMEM(stage, f32)]
            + [pltpu.VMEM((h.message, p.members, LANES), f32)] * 2
            + [pltpu.SemaphoreType.DMA((p.members // SUB, 2))]
            + (
                []
                if c == len(chunks) - 1
                else [
                    pltpu.VMEM((h.nt * p.rows * p.fields, p.members, LANES), f32),
                    pltpu.SemaphoreType.DMA((p.members // SUB,)),
                ]
            ),
            out_specs=[VMEM if c == len(chunks) - 1 else HBM] + [VMEM] * 3,
            cost=(1024, h.nt * (6 << 20) if c else 1024),
            name="forecast",
        )(table, near(packed[c][0] if early is None else after(packed[c][0], early)), *halo[c])
        if c == 0:
            early = lax.cond(
                obs_count[0, 0] >= 0,
                functools.partial(sum_phase, p, 0),
                lambda total: total,
                core_sums(p, keep, send),
            )
            parts.append((ahead, seen, early))
        else:
            if c == 1:
                first = last_sums(p, parts[0][2])
                send = after(send, first[0])
            early = send
            parts.append((ahead, seen, sum_phase(p, 0, core_sums(p, keep, send))))
    new = None
    for c, h in enumerate(chunks):
        ahead, seen, total = parts[c]
        own, other = first if c == 0 and len(chunks) > 1 else last_sums(p, total, new)
        new = finish(p, h, obs, (ahead, seen, own, other), new, ensemble.shape)
    return new


def finish(plan, h, obs, parts, new, whole):
    p = plan
    f32 = jnp.float32
    ahead, seen, own, other = parts

    def near(*arrays):
        return [pltpu.with_memory_space_constraint(a, pltpu.VMEM) for a in arrays]

    solved = call(
        functools.partial(solve_kernel, h),
        [
            pltpu.VMEM((h.np, p.members, LANES), f32),
            pltpu.VMEM((h.np, p.slots, LANES), f32),
            pltpu.VMEM((h.np, SUB, LANES), f32),
        ],
        [VMEM] * 3,
        cost=(1024, 6 << 20),
        name="solve",
    )(*near(obs, seen, own))
    before = [] if new is None else [new]
    return call(
        functools.partial(finish_kernel, h),
        pltpu.HBM(whole, f32),
        [VMEM] * 6 + [HBM] * len(before),
        [pltpu.VMEM((p.rows, p.fields, p.members, h.nt * LANES), f32), pltpu.SemaphoreType.DMA((p.rows, p.fields))],
        cost=(1024, h.nt * (4 << 20)),
        name="finish",
        out_specs=HBM,
        alias={6: 0} if before else {},
    )(*near(ahead, *solved, own, other), *before)


def solution(mesh):
    placed = (
        P("mem", None, "lat", None),
        P(None, ("mem", "lat"), None),
        P(None, ("mem", "lat"), None),
        P(None, ("mem", "lat"), None),
        P(None, ("mem", "lat"), None),
        P(None, ("mem", "lat")),
    )
    return jax.shard_map(
        per_device,
        mesh=mesh,
        in_specs=placed,
        out_specs=P("mem", None, "lat", None),
        check_vma=False,
    )
```

```python
import copy
import functools

import jax
import jax.numpy as jnp
from jax import lax
from jax.experimental import pallas as pl
from jax.experimental.pallas import tpu as pltpu
from jax.sharding import PartitionSpec as P

NSI = 5
HALO = 3
LANES = 128
SUB = 8

time_step = 0.15
viscosity = 0.1
third_part = 1.0 / 3.0
two_thirds = 2.0 / 3.0

HIGHEST = lax.Precision.HIGHEST
VMEM = pl.BlockSpec(memory_space=pltpu.VMEM)
SMEM = pl.BlockSpec(memory_space=pltpu.SMEM)
HBM = pl.BlockSpec(memory_space=pltpu.HBM)
ANY = pl.BlockSpec(memory_space=pl.ANY)
KERNEL_VMEM = 12 << 20


def call(kernel, out_shape, in_specs, scratch=(), cost=(1 << 20, 1 << 20), name=None, out_specs=None, alias={}):
    flops, nbytes = cost
    return pl.pallas_call(
        kernel,
        out_shape=out_shape,
        in_specs=in_specs,
        out_specs=out_specs or [VMEM] * len(out_shape),
        scratch_shapes=list(scratch),
        input_output_aliases=alias,
        compiler_params=pltpu.CompilerParams(vmem_limit_bytes=KERNEL_VMEM),
        cost_estimate=pl.CostEstimate(flops=flops, bytes_accessed=nbytes, transcendentals=0),
        name=name,
    )


def chunk_tiles(tiles, most, step):
    most = max(step, most // step * step)
    count = -(-tiles // most)
    units = tiles // step
    return [(units // count + (1 if i < units % count else 0)) * step for i in range(count)]


class Plan:
    def __init__(self, ensemble, slots, groups):
        self.members, self.fields, self.rows, self.columns = ensemble.shape
        self.total = self.members * groups
        self.slots = slots
        self.groups = groups
        self.width = self.columns // groups
        self.tiles = self.columns // LANES
        self.q = max(1, LANES // self.width)
        most = LANES // (slots * self.q)
        self.counts = chunk_tiles(self.tiles, min(most, -(-self.tiles // 2)), max(1, self.width // LANES))
        self.counts = [4, 4] if self.counts == [4, 4] else self.counts
        self.starts = [sum(self.counts[:i]) for i in range(len(self.counts))]
        self.halves = 2
        self.hrows = self.rows // self.halves
        self.hrf = self.hrows * self.fields
        self.edge_groups = HALO * self.fields
        self.per_edge = LANES // (2 * HALO)
        self.edge_tiles = -(-self.edge_groups // self.per_edge)
        self.plain = -(-self.hrf // SUB) * SUB
        self.block = self.hrf * slots + self.plain

    def chunk(self, c):
        p = copy.copy(self)
        p.nt = self.counts[c]
        p.first = self.starts[c]
        p.after = (p.first + p.nt) % self.tiles
        p.before = (p.first - 1) % self.tiles
        p.np = p.nt * LANES // self.width
        p.first_patch = p.first * LANES // self.width
        p.bands = lax.axis_size("lat")
        p.message = p.nt * self.edge_groups + self.edge_tiles
        p.cell_rows = p.nt * self.block
        p.total_rows = p.cell_rows + p.slots + SUB
        return p

    def patches_of(self, tile):
        if self.width >= LANES:
            return [(tile * LANES // self.width, 0, LANES)]
        return [(tile * self.q + i, i * self.width, (i + 1) * self.width) for i in range(self.q)]


def lane_ids(shape):
    return lax.broadcasted_iota(jnp.int32, shape, len(shape) - 1)


def pack_kernel(plan, raw, *rest):
    p = plan
    lane = lane_ids((SUB, LANES))
    parts = p.members // SUB
    given = []
    if p.first == 0:
        given, rest = rest[:4], rest[4:]
        row_out, (taken, lines, given_sems), rest = rest[3], (rest[-6:-2], *rest[-2:]), rest[:3] + rest[4:-6]
    state, first_out, second_out, up, down, arrived, beside, sems, out_sems = rest
    given_copies = []
    for i, a in enumerate(given):
        given_copies.append(pltpu.make_async_copy(a, taken[i], given_sems.at[i]))
    odd = lax.rem(lax.axis_index("lat"), 2)

    def part_copies(kk):
        part = pl.ds(kk * SUB, SUB)
        takes = [(arrived, p.first, p.nt)] + [(beside.at[i], t, 1) for i, t in enumerate((p.after, p.before))]
        return [
            pltpu.make_async_copy(raw.at[part, :, :, pl.ds(t * LANES, n * LANES)], to.at[part], sems.at[kk, i])
            for i, (to, t, n) in enumerate(takes)
        ]

    cut = p.nt // 2
    pieces = [(0, cut * p.edge_groups), (cut * p.edge_groups, p.message)] if cut else [(0, p.message)]

    def message_copies(kk, piece, swapped=0):
        part = pl.ds(kk * SUB, SUB)
        lines = pl.ds(pieces[piece][0], pieces[piece][1] - pieces[piece][0])
        inner = (up, down) if swapped == 0 else (down, up)
        return [
            pltpu.make_async_copy(a.at[lines, part, :], b.at[lines, part, :], out_sems.at[kk, 2 * piece + i])
            for i, (a, b) in enumerate(zip(inner, (first_out, second_out)))
        ]

    def send_out(kk, piece):
        for swapped in range(2):

            @pl.when(odd == swapped)
            def _():
                for copy_out in message_copies(kk, piece, swapped):
                    copy_out.start()

    for kk in range(parts):
        for copy_in in part_copies(kk):
            copy_in.start()
    for copy_in in given_copies:
        copy_in.start()

    def body(kk, carry):
        mem = pl.ds(pl.multiple_of(kk * SUB, SUB), SUB)
        for copy_in in part_copies(kk):
            copy_in.wait()

        for i in range(p.nt):
            if cut and i == cut:
                send_out(kk, 0)
            cols = slice(i * LANES, (i + 1) * LANES)
            for f in range(p.fields):
                for r in range(p.rows):
                    x = arrived[mem, f, r, cols]
                    state[r, f, mem, cols] = x
                    if r >= p.rows - HALO:
                        up[(i * HALO + r - (p.rows - HALO)) * p.fields + f, mem, :] = x
                    if r < HALO:
                        down[(i * HALO + r) * p.fields + f, mem, :] = x
        for r in range(p.rows):
            for f in range(p.fields):
                edge = jnp.where(lane < LANES // 2, beside[0, mem, f, r, :], beside[1, mem, f, r, :])
                state[r, f, mem, p.nt * LANES :] = edge
        for out, skipped in ((up, p.rows - HALO), (down, 0)):
            for e in range(p.edge_tiles):
                packed = jnp.zeros((SUB, LANES), jnp.float32)
                for g in range(e * p.per_edge, min((e + 1) * p.per_edge, p.edge_groups)):
                    i, f = divmod(g, p.fields)
                    place = (g - e * p.per_edge) * 2 * HALO
                    inside = (lane >= place) & (lane < place + 2 * HALO)
                    edge = state[i + skipped, f, mem, p.nt * LANES :]
                    packed = jnp.where(inside, pltpu.roll(edge, place + HALO, 1), packed)
                out[p.nt * p.edge_groups + e, mem, :] = packed

        send_out(kk, len(pieces) - 1)
        return carry

    lax.fori_loop(0, parts, body, 0)
    if given:
        for copy_in in given_copies:
            copy_in.wait()
        row = jnp.zeros((SUB, LANES), jnp.float32)
        for i, a in enumerate(given):
            lines[i : i + 1, : p.slots] = jnp.broadcast_to(taken[i][0].astype(jnp.float32), (1, p.slots))
            line = pltpu.roll(jnp.broadcast_to(lines[i : i + 1, :], (SUB, LANES)), i * p.slots, 1)
            row = jnp.where((lane >= i * p.slots) & (lane < (i + 1) * p.slots), line, row)
        row_out[...] = row[:1]
    for kk in range(parts):
        for piece in range(len(pieces)):
            for copy_out in message_copies(kk, piece):
                copy_out.wait()


def step_once(p, rows_in, load, store, last, scale):
    lane = lane_ids((SUB, LANES))
    ring = p.nt + 1
    out_tiles = p.nt if last else ring
    k = scale * time_step * viscosity
    centre = scale * (1.0 - 4.0 * time_step * viscosity)
    for first in range(0, p.fields, 2):
        pair = range(first, min(first + 2, p.fields))
        held = {row: {f: [load(row, f, t) for t in range(ring)] for f in pair} for row in range(2)}
        for row in range(1, rows_in - 1):
            held[row + 1] = {f: [load(row + 1, f, t) for t in range(ring)] for f in pair}
            rolled = {}

            def turn(f, t, by):
                if (f, t, by) not in rolled:
                    rolled[f, t, by] = pltpu.roll(held[row][f][t], by, 1)
                return rolled[f, t, by]

            for t in range(out_tiles):
                u, v = ((held[row][i][t] if i in held[row] else load(row, i, t)) * (scale * time_step * 0.5) for i in range(2))
                ce, cw, cn, cs = k - u, k + u, k - v, k + v
                for f in pair:
                    west = pltpu.roll(jnp.where(lane == LANES - 1, held[row][f][(t - 1) % ring], held[row][f][t]), 1, 1)
                    east = pltpu.roll(jnp.where(lane == 0, held[row][f][(t + 1) % ring], held[row][f][t]), LANES - 1, 1)
                    moved = (ce * east + cw * west) + (cn * held[row + 1][f][t] + cs * held[row - 1][f][t])
                    store(row, f, t, centre * held[row][f][t] + moved)
            del held[row - 1]


def split(x):
    high = x.astype(jnp.bfloat16)
    return high, (x - high.astype(jnp.float32)).astype(jnp.bfloat16)


def places(p, chunks, me, cells):
    line = jnp.arange(p.groups, dtype=jnp.int32)[:, None]
    patch = line ^ me
    first = jnp.zeros_like(patch)
    for h in chunks:
        first = jnp.where(patch >= h.first_patch, h.first_patch, first)
    slot = jnp.arange(p.slots, dtype=jnp.int32)[None, :]
    column = cells % p.width + (patch - first) * p.width
    r = cells // p.width % p.rows
    f = cells // (p.width * p.rows)
    tile, lane = column // LANES, column % LANES
    shift = ((patch - first) * p.slots + slot - lane) % LANES
    table = [(tile * p.rows + r) * p.fields + f, shift]
    return jnp.stack(table).reshape(-1)


def table_kernel(table_in, table, sem):
    copy_in = pltpu.make_async_copy(table_in, table, sem)
    copy_in.start()
    copy_in.wait()


def forecast_kernel(plan, table, state, first_in, second_in, ahead, seen, keep, send, s0, s1, s2, low, high, sems, *rest):
    p = plan
    ahead_out = ahead
    if rest:
        ahead = rest[0]

    def ahead_copy(kk):
        part = pl.ds(kk * SUB, SUB)
        return pltpu.make_async_copy(ahead.at[:, part, :], ahead_out.at[:, part, :], rest[1].at[kk])

    full = p.rows + 2 * HALO
    band = lax.axis_index("lat")
    me = lax.axis_index("mem")
    core = lax.rem(me, 2)
    has_low = (band > 0).astype(jnp.float32)
    has_high = (band < p.bands - 1).astype(jnp.float32)
    lane = lane_ids((SUB, LANES))
    parts = p.members // SUB

    def part_copies(kk, swapped=0):
        part = pl.ds(kk * SUB, SUB)
        inner = (high, low) if swapped == 0 else (low, high)
        return [
            pltpu.make_async_copy(a.at[:, part, :], b.at[:, part, :], sems.at[kk, i])
            for i, (a, b) in enumerate(zip((first_in, second_in), inner))
        ]

    def start_copies(kk):
        for swapped in range(2):

            @pl.when(lax.rem(band, 2) == swapped)
            def _():
                for copy_in in part_copies(kk, swapped):
                    copy_in.start()

    start_copies(0)

    def body(kk, carry):
        mem = pl.ds(pl.multiple_of(kk * SUB, SUB), SUB)

        @pl.when(kk + 1 < parts)
        def _():
            start_copies(kk + 1)

        for copy_in in part_copies(kk):
            copy_in.wait()

        def edge_of(source, g):
            e, place = divmod(g, p.per_edge)
            return pltpu.roll(source[p.nt * p.edge_groups + e, mem, :], (LANES - HALO - place * 2 * HALO) % LANES, 1)

        for f in range(p.fields):
            for i in range(HALO):
                s0[i, f] = edge_of(low, i * p.fields + f)
                s0[HALO + i, f] = edge_of(high, i * p.fields + f)

        def load0(row, f, t):
            if HALO <= row < HALO + p.rows:
                return state[row - HALO, f, mem, t * LANES : (t + 1) * LANES]
            i = row if row < HALO else row - p.rows
            if t == p.nt:
                return s0[i, f]
            source = low if row < HALO else high
            return source[(t * HALO + i % HALO) * p.fields + f, mem, :]

        def keep_zero(row, value):
            if row < HALO:
                return value * has_low
            if row >= HALO + p.rows:
                return value * has_high
            return value

        def store1(row, f, t, stepped):
            s1[row, f, t] = keep_zero(row, stepped)

        def store2(row, f, t, stepped):
            row = row + 1
            s2[row, f, t] = keep_zero(row, 0.75 * load0(row, f, t) + stepped)

        def store3(row, f, t, stepped):
            row = row + 2
            ahead[(t * p.rows + row - HALO) * p.fields + f, mem, :] = third_part * load0(row, f, t) + stepped

        step_once(p, full, load0, store1, False, 1.0)
        step_once(p, full - 2, lambda row, f, t: s1[row + 1, f, t], store2, False, 0.25)
        step_once(p, full - 4, lambda row, f, t: s2[row + 2, f, t], store3, True, two_thirds)
        if rest:
            ahead_copy(kk).start()
        return carry

    lax.fori_loop(0, parts, body, 0)

    wide = lane_ids((p.members, LANES))
    found = jnp.zeros((p.members, LANES), jnp.float32)
    every = p.groups * p.slots
    for j in range(p.np):
        at = ((p.first_patch + j) ^ me) * p.slots
        for o in range(p.slots):
            to = j * p.slots + o
            found = jnp.where(wide == to, pltpu.roll(ahead[table[at + o]], table[every + at + o], 1), found)
    seen[...] = found

    high, low_part = (a.astype(jnp.float32) for a in split(found))
    turned = jnp.transpose(jnp.concatenate([high, high, low_part], axis=0))
    depth = 3 * p.members
    extra = lax.broadcasted_iota(jnp.int32, (2 * SUB, depth), 0)
    ones = jnp.where((extra == 0) & (lane_ids((2 * SUB, depth)) < 2 * p.members), 1.0, 0.0).astype(jnp.float32)
    sides = [
        jnp.concatenate([turned[j * p.slots : (j + 1) * p.slots], ones], axis=0).astype(jnp.bfloat16) for j in range(p.np)
    ]
    lanes = lane_ids((p.slots + 2 * SUB, LANES))
    moments = jnp.zeros((p.slots + 2 * SUB, LANES), jnp.float32)
    joined = jnp.concatenate([a.astype(jnp.bfloat16) for a in (high, low_part, high)], axis=0)
    for j in range(p.np):
        part = jnp.dot(sides[j], joined, preferred_element_type=jnp.float32)
        moments = jnp.where((lanes >= j * p.slots) & (lanes < (j + 1) * p.slots), part, moments)
    for out in (keep, send):
        out[pl.ds(p.cell_rows, p.slots + SUB), :] = moments[: p.slots + SUB]
    for side in range(p.halves):
        out = keep if side == 0 else send
        half = core if side == 0 else 1 - core
        for t in range(p.nt):
            base = t * p.block
            begin = (t * p.rows + half * p.hrows) * p.fields
            high, low_part = split(jnp.concatenate([ahead[begin + i] for i in range(p.hrf)], axis=1))
            joined = jnp.concatenate([high, low_part, high], axis=0)
            result = None
            for j, first, stop in p.patches_of(t):
                part = jnp.dot(sides[j], joined, preferred_element_type=jnp.float32)
                if result is None:
                    result = part
                else:
                    at = lane_ids(part.shape) % LANES
                    result = jnp.where((at >= first) & (at < stop), part, result)
            for i in range(p.hrf):
                piece = result[:, i * LANES : (i + 1) * LANES]
                out[pl.ds(base + i * p.slots, p.slots), :] = piece[: p.slots]
                out[pl.ds(base + p.hrf * p.slots + i, 1), :] = piece[p.slots : p.slots + 1]
            for i in range(p.hrf, p.plain):
                out[pl.ds(base + p.hrf * p.slots + i, 1), :] = jnp.zeros((1, LANES), jnp.float32)
    if rest:
        for kk in range(parts):
            ahead_copy(kk).wait()


def solve_kernel(plan, obs, seen, own, factors, centres, keeps):
    p = plan
    n = p.slots
    me = lax.axis_index("mem")
    free = p.total - 1.0
    shape = (n, LANES)
    lane = lane_ids(shape)
    row = lax.broadcasted_iota(jnp.int32, shape, 0)
    group = lane // n * n
    eye = jnp.where(lane - group == row, 1.0, 0.0).astype(jnp.float32)
    lane_row = lane_ids((1, LANES))
    lane_sub = lane_ids((SUB, LANES))

    def pick(a, index):
        return jnp.take_along_axis(a, index, axis=1)

    def col(a):
        return pick(jnp.broadcast_to(a, shape), group + row)

    def spread_out(a):
        base = lane_ids(a.shape) // n * n
        return [pick(a, base + k) for k in range(n)]

    def product(parts, b):
        terms = [parts[k] * b[k : k + 1] for k in range(n)]
        while len(terms) > 1:
            terms = [sum(terms[i : i + 2][1:], terms[i]) for i in range(0, len(terms), 2)]
        return terms[0]

    given = [jnp.zeros((SUB, LANES), jnp.float32) for _ in range(4)]
    for j in range(p.np):
        source = (p.first_patch + j) ^ me
        line = jnp.broadcast_to(obs[pl.ds(source, 1), :], (SUB, LANES))
        mine = (lane_sub >= j * n) & (lane_sub < (j + 1) * n)
        for i, place in enumerate((0, 1, 2, 4)):
            given[i] = jnp.where(mine, pltpu.roll(line, (j * n - place * n) % LANES, 1), given[i])
    moments = own[pl.ds(p.cell_rows, n), :]
    sums = own[pl.ds(p.cell_rows + n, SUB), :]
    value, variance, loop, count = (a[0:1] for a in given)
    mean = sums[0:1] * (1.0 / p.total)
    slot = (lane_row % n).astype(jnp.float32)
    used = lane_row < p.np * n
    weight = jnp.where(used & (slot < count), jnp.exp(-0.35 * loop) / jnp.where(used, variance, 1.0), 0.0)
    root = jnp.sqrt(weight)
    root_col = col(root)
    mean_col = col(mean)
    scaled = root_col * (moments - p.total * mean_col * mean) * root
    bound = free + 0.5 * jnp.sum(pick(scaled, group + row), axis=0, keepdims=True)
    inverse = 1.0 / bound

    small = scaled * inverse
    t0 = free * inverse
    tf = t0 * eye + small
    tg = eye
    z0 = jnp.ones((1, LANES), jnp.float32)
    zg = None
    for repeat in range(NSI):
        f0 = 1.5 - 0.5 * t0
        ff = 1.5 * eye - 0.5 * tf
        parts = spread_out(ff)
        if zg is None:
            zg = -0.5 * z0 * tg
        else:
            zg = product(parts, zg) - 0.5 * z0 * tg
        z0 = z0 * f0
        if repeat < NSI - 1:
            square = product(parts, ff)
            bend = square - (0.5 * t0) * (ff + f0 * eye)
            tf = product(spread_out(square), tf)
            tg = bend if repeat == 0 else product(spread_out(bend), tg)
            t0 = t0 * f0 * f0
    zf = z0 * eye + product(spread_out(small), zg)
    scale = jnp.sqrt(free * inverse)
    spread = (scale * inverse) * root_col * zg * root
    down = root * (value - mean)
    for repeat in range(2):
        down = jnp.sum(zf * col(down), axis=0, keepdims=True)
    weights = product(spread_out(seen[...] - mean), spread) + root * down * inverse
    spread0 = scale * z0

    wide = lane_ids((p.members, LANES))
    high, low_part = (a.astype(jnp.float32) for a in split(weights))
    for j in range(p.np):
        here, there, last = (pltpu.roll(a, (i * n - j * n) % LANES, 1) for i, a in enumerate((high, high, low_part)))
        factors[j] = jnp.where(wide < n, here, jnp.where(wide < 2 * n, there, last))
        centres[j] = pick(jnp.broadcast_to(mean, shape), row + j * n)
        keeps[j] = pick(jnp.broadcast_to(spread0, (SUB, LANES)), jnp.full((SUB, LANES), j * n, jnp.int32))


def finish_kernel(plan, ahead, factors, centres, keeps, own, other, *rest):
    out, staged, sems = rest[-3:]
    p = plan
    n = p.slots
    core = lax.rem(lax.axis_index("mem"), 2)
    mixing = [(factors[j][:, : 3 * n].astype(jnp.bfloat16), centres[j], keeps[j][0:1]) for j in range(p.np)]

    def line_copy(r, f):
        cols = pl.ds(p.first * LANES, p.nt * LANES)
        return pltpu.make_async_copy(staged.at[r, f], out.at[:, f, r, cols], sems.at[r, f])

    for half in range(p.halves):
        at_own = half == core
        lines = [(half * p.hrows + i // p.fields, i % p.fields) for i in range(p.hrf)]
        for t in range(p.nt):
            pieces = []
            for i in range(p.hrf):
                at = t * p.block + i * n
                pieces.append(jnp.where(at_own, own[at : at + n, :], other[at : at + n, :]))
            at = t * p.block + p.hrf * n
            plain = jnp.where(at_own, own[at : at + p.plain, :], other[at : at + p.plain, :])
            results = []
            for j, first, stop in p.patches_of(t):
                mine, centre, keep0 = mixing[j]
                centred = [pieces[i] - centre * plain[i : i + 1, :] for i in range(p.hrf)]
                high, low_part = split(jnp.concatenate(centred, axis=1))
                joined = jnp.concatenate([high, low_part, high], axis=0)
                results.append((jnp.dot(mine, joined, preferred_element_type=jnp.float32), keep0, first, stop))
            for i, (r, f) in enumerate(lines):
                x = ahead[(t * p.rows + r) * p.fields + f]
                average = plain[i : i + 1, :] * (1.0 / p.total)
                final = None
                for update, keep0, first, stop in results:
                    part = (1.0 - keep0) * average + keep0 * x + update[:, i * LANES : (i + 1) * LANES]
                    if final is None:
                        final = part
                    else:
                        at = lane_ids(part.shape)
                        final = jnp.where((at >= first) & (at < stop), part, final)
                staged[r, f, :, t * LANES : (t + 1) * LANES] = final
        for r, f in lines:
            line_copy(r, f).start()
    for r in range(p.rows):
        for f in range(p.fields):
            line_copy(r, f).wait()


def core_sums(plan, keep, send):
    return keep + lax.ppermute(send, "mem", [(i, i ^ 1) for i in range(plan.groups)])


def sum_phase(plan, phase, total, waited=None):
    p = plan
    bits = [1 << i for i in range(1, p.groups.bit_length() - 1)]
    if phase >= len(bits):
        return total
    even = bits[phase]
    odd = bits[(phase + len(bits) // 2) % len(bits)]
    there = lax.ppermute(total, "mem", [(i, i ^ (odd if i & 1 else even)) for i in range(p.groups)])
    return (total if waited is None else after(total, waited)) + there


def last_sums(plan, total, waited=None):
    p = plan
    for phase in range(1, p.groups.bit_length() - 2):
        total = sum_phase(p, phase, total, waited)
    return total, lax.ppermute(total, "mem", [(i, i ^ 1) for i in range(p.groups)])


def after(value, *others):
    return lax.optimization_barrier((value,) + others)[0]


def per_device(ensemble, obs_value, obs_var, obs_cell, obs_loop, obs_count):
    groups = lax.axis_size("mem")
    bands = lax.axis_size("lat")
    slots = obs_cell.shape[-1]
    p = Plan(ensemble, slots, groups)
    chunks = [p.chunk(c) for c in range(len(p.counts))]
    f32 = jnp.float32
    shape = pltpu.VMEM

    given = (obs_value, obs_var, obs_loop, obs_cell)

    def pack(h, source):
        sent = (h.message, p.members, LANES)
        more = given if h.first == 0 else ()
        return call(
            functools.partial(pack_kernel, h),
            [pltpu.VMEM((p.rows, p.fields, p.members, (h.nt + 1) * LANES), f32), pltpu.HBM(sent, f32), pltpu.HBM(sent, f32)]
            + [pltpu.VMEM((1, LANES), f32) for _ in more[:1]],
            [HBM] * (1 + len(more)),
            [
                pltpu.VMEM(sent, f32),
                pltpu.VMEM(sent, f32),
                pltpu.VMEM((p.members, p.fields, p.rows, h.nt * LANES), f32),
                pltpu.VMEM((2, p.members, p.fields, p.rows, LANES), f32),
                pltpu.SemaphoreType.DMA((p.members // SUB, 3)),
                pltpu.SemaphoreType.DMA((p.members // SUB, 4)),
            ]
            + [pltpu.VMEM(a.shape, a.dtype) for a in more]
            + [pltpu.VMEM((SUB, LANES), f32) for _ in more[:1]]
            + [pltpu.SemaphoreType.DMA((len(more),)) for _ in more[:1]],
            out_specs=[VMEM, HBM, HBM] + [VMEM for _ in more[:1]],
            name="pack",
        )(*(pltpu.with_memory_space_constraint(a, pltpu.HBM) for a in (source,) + more))

    packed = [pack(chunks[0], ensemble)]
    obs = jnp.where(jnp.arange(LANES) < 4 * slots, packed[0][3], obs_count.astype(f32))
    bit = 1
    while bit < groups:
        step = 2 if bit == 1 or bit * 4 > groups else 4
        there = [lax.ppermute(obs, "mem", [(i, i ^ (bit * b)) for i in range(groups)]) for b in range(1, step)]
        obs = jnp.concatenate([obs] + there, axis=0)
        bit *= step

    packed += [pack(h, after(ensemble, obs)) for h in chunks[1:]]
    messages = [a for part in packed for a in part[1:3]]
    swaps = [[pair for i in range(begin, bands - 1, 2) for pair in ((i, i + 1), (i + 1, i))] for begin in range(2)]
    halo = [[lax.ppermute(messages[2 * c + i], "lat", swaps[i]) for i in range(2)] for c in range(len(chunks))]

    table = call(
        table_kernel,
        [pltpu.SMEM((2 * groups * slots,), jnp.int32)],
        [ANY],
        [pltpu.SemaphoreType.DMA],
        out_specs=[SMEM],
        name="places",
    )(places(p, chunks, lax.axis_index("mem"), obs[:, 3 * slots : 4 * slots].astype(jnp.int32)))[0]
    table = pltpu.with_memory_space_constraint(table, pltpu.SMEM)

    def near(x):
        return pltpu.with_memory_space_constraint(x, pltpu.VMEM)

    def far(x):
        return pltpu.with_memory_space_constraint(x, pltpu.HBM)

    parts = []
    early = None
    for c, h in enumerate(chunks):
        stage = (p.rows + 2 * HALO, p.fields, h.nt + 1, SUB, LANES)
        ahead, seen, keep, send = call(
            functools.partial(forecast_kernel, h),
            [
                (shape if c == len(chunks) - 1 else pltpu.HBM)((h.nt * p.rows * p.fields, p.members, LANES), f32),
                shape((p.members, LANES), f32),
                shape((h.total_rows, LANES), f32),
                shape((h.total_rows, LANES), f32),
            ],
            [SMEM, VMEM, ANY, ANY],
            [pltpu.VMEM((2 * HALO, p.fields, SUB, LANES), f32), pltpu.VMEM(stage, f32), pltpu.VMEM(stage, f32)]
            + [pltpu.VMEM((h.message, p.members, LANES), f32)] * 2
            + [pltpu.SemaphoreType.DMA((p.members // SUB, 2))]
            + (
                []
                if c == len(chunks) - 1
                else [
                    pltpu.VMEM((h.nt * p.rows * p.fields, p.members, LANES), f32),
                    pltpu.SemaphoreType.DMA((p.members // SUB,)),
                ]
            ),
            out_specs=[VMEM if c == len(chunks) - 1 else HBM] + [VMEM] * 3,
            cost=(1024, h.nt * (6 << 20) if c else 1024),
            name="forecast",
        )(table, near(packed[c][0] if early is None else after(packed[c][0], early)), *halo[c])
        if c == 0:
            early = lax.cond(
                obs_count[0, 0] >= 0,
                functools.partial(sum_phase, p, 0),
                lambda total: total,
                core_sums(p, keep, send),
            )
            parts.append((ahead, seen, early))
        else:
            if c == 1:
                first = last_sums(p, parts[0][2])
                send = after(send, first[0])
            early = send
            parts.append((ahead, seen, sum_phase(p, 0, core_sums(p, keep, send))))
    new = None
    for c, h in enumerate(chunks):
        ahead, seen, total = parts[c]
        own, other = first if c == 0 and len(chunks) > 1 else last_sums(p, total, new)
        new = finish(p, h, obs, (ahead, seen, own, other), new, ensemble.shape)
    return new


def finish(plan, h, obs, parts, new, whole):
    p = plan
    f32 = jnp.float32
    ahead, seen, own, other = parts

    def near(*arrays):
        return [pltpu.with_memory_space_constraint(a, pltpu.VMEM) for a in arrays]

    solved = call(
        functools.partial(solve_kernel, h),
        [
            pltpu.VMEM((h.np, p.members, LANES), f32),
            pltpu.VMEM((h.np, p.slots, LANES), f32),
            pltpu.VMEM((h.np, SUB, LANES), f32),
        ],
        [VMEM] * 3,
        cost=(1024, 6 << 20),
        name="solve",
    )(*near(obs, seen, own))
    before = [] if new is None else [new]
    return call(
        functools.partial(finish_kernel, h),
        pltpu.HBM(whole, f32),
        [VMEM] * 6 + [HBM] * len(before),
        [pltpu.VMEM((p.rows, p.fields, p.members, h.nt * LANES), f32), pltpu.SemaphoreType.DMA((p.rows, p.fields))],
        cost=(1024, h.nt * (4 << 20)),
        name="finish",
        out_specs=HBM,
        alias={6: 0} if before else {},
    )(*near(ahead, *solved, own, other), *before)


def solution(mesh):
    placed = (
        P("mem", None, "lat", None),
        P(None, ("mem", "lat"), None),
        P(None, ("mem", "lat"), None),
        P(None, ("mem", "lat"), None),
        P(None, ("mem", "lat"), None),
        P(None, ("mem", "lat")),
    )
    return jax.shard_map(
        per_device,
        mesh=mesh,
        in_specs=placed,
        out_specs=P("mem", None, "lat", None),
        check_vma=False,
    )
```

```python
import copy
import functools

import jax
import jax.numpy as jnp
from jax import lax
from jax.experimental import pallas as pl
from jax.experimental.pallas import tpu as pltpu
from jax.sharding import PartitionSpec as P

NSI = 5
HALO = 3
LANES = 128
SUB = 8

time_step = 0.15
viscosity = 0.1
third_part = 1.0 / 3.0
two_thirds = 2.0 / 3.0

HIGHEST = lax.Precision.HIGHEST
VMEM = pl.BlockSpec(memory_space=pltpu.VMEM)
SMEM = pl.BlockSpec(memory_space=pltpu.SMEM)
HBM = pl.BlockSpec(memory_space=pltpu.HBM)
ANY = pl.BlockSpec(memory_space=pl.ANY)
KERNEL_VMEM = 12 << 20


def call(kernel, out_shape, in_specs, scratch=(), cost=(1 << 20, 1 << 20), name=None, out_specs=None, alias={}):
    flops, nbytes = cost
    return pl.pallas_call(
        kernel,
        out_shape=out_shape,
        in_specs=in_specs,
        out_specs=out_specs or [VMEM] * len(out_shape),
        scratch_shapes=list(scratch),
        input_output_aliases=alias,
        compiler_params=pltpu.CompilerParams(vmem_limit_bytes=KERNEL_VMEM),
        cost_estimate=pl.CostEstimate(flops=flops, bytes_accessed=nbytes, transcendentals=0),
        name=name,
    )


def chunk_tiles(tiles, most, step):
    most = max(step, most // step * step)
    count = -(-tiles // most)
    units = tiles // step
    return [(units // count + (1 if i < units % count else 0)) * step for i in range(count)]


class Plan:
    def __init__(self, ensemble, slots, groups):
        self.members, self.fields, self.rows, self.columns = ensemble.shape
        self.total = self.members * groups
        self.slots = slots
        self.groups = groups
        self.width = self.columns // groups
        self.tiles = self.columns // LANES
        self.q = max(1, LANES // self.width)
        most = LANES // (slots * self.q)
        self.counts = chunk_tiles(self.tiles, min(most, -(-self.tiles // 2)), max(1, self.width // LANES))
        self.counts = [4, 4] if self.counts == [4, 4] else self.counts
        self.starts = [sum(self.counts[:i]) for i in range(len(self.counts))]
        self.halves = 2
        self.hrows = self.rows // self.halves
        self.hrf = self.hrows * self.fields
        self.edge_groups = HALO * self.fields
        self.per_edge = LANES // (2 * HALO)
        self.edge_tiles = -(-self.edge_groups // self.per_edge)
        self.plain = -(-self.hrf // SUB) * SUB
        self.block = self.hrf * slots + self.plain

    def chunk(self, c):
        p = copy.copy(self)
        p.nt = self.counts[c]
        p.first = self.starts[c]
        p.after = (p.first + p.nt) % self.tiles
        p.before = (p.first - 1) % self.tiles
        p.np = p.nt * LANES // self.width
        p.first_patch = p.first * LANES // self.width
        p.bands = lax.axis_size("lat")
        p.message = p.nt * self.edge_groups + self.edge_tiles
        p.cell_rows = p.nt * self.block
        p.total_rows = p.cell_rows + p.slots + SUB
        return p

    def patches_of(self, tile):
        if self.width >= LANES:
            return [(tile * LANES // self.width, 0, LANES)]
        return [(tile * self.q + i, i * self.width, (i + 1) * self.width) for i in range(self.q)]


def lane_ids(shape):
    return lax.broadcasted_iota(jnp.int32, shape, len(shape) - 1)


def pack_kernel(plan, raw, *rest):
    p = plan
    lane = lane_ids((SUB, LANES))
    parts = p.members // SUB
    given = []
    if p.first == 0:
        given, rest = rest[:4], rest[4:]
        row_out, (taken, lines, given_sems), rest = rest[3], (rest[-6:-2], *rest[-2:]), rest[:3] + rest[4:-6]
    state, first_out, second_out, up, down, arrived, beside, sems, out_sems = rest
    given_copies = []
    for i, a in enumerate(given):
        given_copies.append(pltpu.make_async_copy(a, taken[i], given_sems.at[i]))
    odd = lax.rem(lax.axis_index("lat"), 2)

    def part_copies(kk):
        part = pl.ds(kk * SUB, SUB)
        takes = [(arrived, p.first, p.nt)] + [(beside.at[i], t, 1) for i, t in enumerate((p.after, p.before))]
        return [
            pltpu.make_async_copy(raw.at[part, :, :, pl.ds(t * LANES, n * LANES)], to.at[part], sems.at[kk, i])
            for i, (to, t, n) in enumerate(takes)
        ]

    cut = p.nt // 2
    pieces = [(0, cut * p.edge_groups), (cut * p.edge_groups, p.message)] if cut else [(0, p.message)]

    def message_copies(kk, piece, swapped=0):
        part = pl.ds(kk * SUB, SUB)
        lines = pl.ds(pieces[piece][0], pieces[piece][1] - pieces[piece][0])
        inner = (up, down) if swapped == 0 else (down, up)
        return [
            pltpu.make_async_copy(a.at[lines, part, :], b.at[lines, part, :], out_sems.at[kk, 2 * piece + i])
            for i, (a, b) in enumerate(zip(inner, (first_out, second_out)))
        ]

    def send_out(kk, piece):
        for swapped in range(2):

            @pl.when(odd == swapped)
            def _():
                for copy_out in message_copies(kk, piece, swapped):
                    copy_out.start()

    for kk in range(parts):
        for copy_in in part_copies(kk):
            copy_in.start()
    for copy_in in given_copies:
        copy_in.start()

    def body(kk, carry):
        mem = pl.ds(pl.multiple_of(kk * SUB, SUB), SUB)
        for copy_in in part_copies(kk):
            copy_in.wait()

        for i in range(p.nt):
            if cut and i == cut:
                send_out(kk, 0)
            cols = slice(i * LANES, (i + 1) * LANES)
            for f in range(p.fields):
                for r in range(p.rows):
                    x = arrived[mem, f, r, cols]
                    state[r, f, mem, cols] = x
                    if r >= p.rows - HALO:
                        up[(i * HALO + r - (p.rows - HALO)) * p.fields + f, mem, :] = x
                    if r < HALO:
                        down[(i * HALO + r) * p.fields + f, mem, :] = x
        for r in range(p.rows):
            for f in range(p.fields):
                edge = jnp.where(lane < LANES // 2, beside[0, mem, f, r, :], beside[1, mem, f, r, :])
                state[r, f, mem, p.nt * LANES :] = edge
        for out, skipped in ((up, p.rows - HALO), (down, 0)):
            for e in range(p.edge_tiles):
                packed = jnp.zeros((SUB, LANES), jnp.float32)
                for g in range(e * p.per_edge, min((e + 1) * p.per_edge, p.edge_groups)):
                    i, f = divmod(g, p.fields)
                    place = (g - e * p.per_edge) * 2 * HALO
                    inside = (lane >= place) & (lane < place + 2 * HALO)
                    edge = state[i + skipped, f, mem, p.nt * LANES :]
                    packed = jnp.where(inside, pltpu.roll(edge, place + HALO, 1), packed)
                out[p.nt * p.edge_groups + e, mem, :] = packed

        send_out(kk, len(pieces) - 1)
        return carry

    lax.fori_loop(0, parts, body, 0)
    if given:
        for copy_in in given_copies:
            copy_in.wait()
        row = jnp.zeros((SUB, LANES), jnp.float32)
        for i, a in enumerate(given):
            lines[i : i + 1, : p.slots] = jnp.broadcast_to(taken[i][0].astype(jnp.float32), (1, p.slots))
            line = pltpu.roll(jnp.broadcast_to(lines[i : i + 1, :], (SUB, LANES)), i * p.slots, 1)
            row = jnp.where((lane >= i * p.slots) & (lane < (i + 1) * p.slots), line, row)
        row_out[...] = row[:1]
    for kk in range(parts):
        for piece in range(len(pieces)):
            for copy_out in message_copies(kk, piece):
                copy_out.wait()


def step_once(p, rows_in, load, store, last, scale):
    lane = lane_ids((SUB, LANES))
    ring = p.nt + 1
    out_tiles = p.nt if last else ring
    k = scale * time_step * viscosity
    centre = scale * (1.0 - 4.0 * time_step * viscosity)
    for first in range(0, p.fields, 2):
        pair = range(first, min(first + 2, p.fields))
        held = {row: {f: [load(row, f, t) for t in range(ring)] for f in pair} for row in range(2)}
        for row in range(1, rows_in - 1):
            held[row + 1] = {f: [load(row + 1, f, t) for t in range(ring)] for f in pair}
            rolled = {}

            def turn(f, t, by):
                if (f, t, by) not in rolled:
                    rolled[f, t, by] = pltpu.roll(held[row][f][t], by, 1)
                return rolled[f, t, by]

            for t in range(out_tiles):
                u, v = ((held[row][i][t] if i in held[row] else load(row, i, t)) * (scale * time_step * 0.5) for i in range(2))
                ce, cw, cn, cs = k - u, k + u, k - v, k + v
                for f in pair:
                    west = pltpu.roll(jnp.where(lane == LANES - 1, held[row][f][(t - 1) % ring], held[row][f][t]), 1, 1)
                    east = pltpu.roll(jnp.where(lane == 0, held[row][f][(t + 1) % ring], held[row][f][t]), LANES - 1, 1)
                    moved = (ce * east + cw * west) + (cn * held[row + 1][f][t] + cs * held[row - 1][f][t])
                    store(row, f, t, centre * held[row][f][t] + moved)
            del held[row - 1]


def split(x):
    high = x.astype(jnp.bfloat16)
    return high, (x - high.astype(jnp.float32)).astype(jnp.bfloat16)


def places(p, chunks, me, cells):
    line = jnp.arange(p.groups, dtype=jnp.int32)[:, None]
    patch = line ^ me
    first = jnp.zeros_like(patch)
    for h in chunks:
        first = jnp.where(patch >= h.first_patch, h.first_patch, first)
    slot = jnp.arange(p.slots, dtype=jnp.int32)[None, :]
    column = cells % p.width + (patch - first) * p.width
    r = cells // p.width % p.rows
    f = cells // (p.width * p.rows)
    tile, lane = column // LANES, column % LANES
    shift = ((patch - first) * p.slots + slot - lane) % LANES
    table = [(tile * p.rows + r) * p.fields + f, shift]
    return jnp.stack(table).reshape(-1)


def table_kernel(table_in, table, sem):
    copy_in = pltpu.make_async_copy(table_in, table, sem)
    copy_in.start()
    copy_in.wait()


def forecast_kernel(plan, table, state, first_in, second_in, ahead, seen, keep, send, s0, s1, s2, low, high, sems, *rest):
    p = plan
    ahead_out = ahead
    if rest:
        ahead = rest[0]

    def ahead_copy(kk):
        part = pl.ds(kk * SUB, SUB)
        return pltpu.make_async_copy(ahead.at[:, part, :], ahead_out.at[:, part, :], rest[1].at[kk])

    full = p.rows + 2 * HALO
    band = lax.axis_index("lat")
    me = lax.axis_index("mem")
    core = lax.rem(me, 2)
    has_low = (band > 0).astype(jnp.float32)
    has_high = (band < p.bands - 1).astype(jnp.float32)
    lane = lane_ids((SUB, LANES))
    parts = p.members // SUB

    def part_copies(kk, swapped=0):
        part = pl.ds(kk * SUB, SUB)
        inner = (high, low) if swapped == 0 else (low, high)
        return [
            pltpu.make_async_copy(a.at[:, part, :], b.at[:, part, :], sems.at[kk, i])
            for i, (a, b) in enumerate(zip((first_in, second_in), inner))
        ]

    def start_copies(kk):
        for swapped in range(2):

            @pl.when(lax.rem(band, 2) == swapped)
            def _():
                for copy_in in part_copies(kk, swapped):
                    copy_in.start()

    start_copies(0)

    def body(kk, carry):
        mem = pl.ds(pl.multiple_of(kk * SUB, SUB), SUB)

        @pl.when(kk + 1 < parts)
        def _():
            start_copies(kk + 1)

        for copy_in in part_copies(kk):
            copy_in.wait()

        def edge_of(source, g):
            e, place = divmod(g, p.per_edge)
            return pltpu.roll(source[p.nt * p.edge_groups + e, mem, :], (LANES - HALO - place * 2 * HALO) % LANES, 1)

        for f in range(p.fields):
            for i in range(HALO):
                s0[i, f] = edge_of(low, i * p.fields + f)
                s0[HALO + i, f] = edge_of(high, i * p.fields + f)

        def load0(row, f, t):
            if HALO <= row < HALO + p.rows:
                return state[row - HALO, f, mem, t * LANES : (t + 1) * LANES]
            i = row if row < HALO else row - p.rows
            if t == p.nt:
                return s0[i, f]
            source = low if row < HALO else high
            return source[(t * HALO + i % HALO) * p.fields + f, mem, :]

        def keep_zero(row, value):
            if row < HALO:
                return value * has_low
            if row >= HALO + p.rows:
                return value * has_high
            return value

        def store1(row, f, t, stepped):
            s1[row, f, t] = keep_zero(row, stepped)

        def store2(row, f, t, stepped):
            row = row + 1
            s2[row, f, t] = keep_zero(row, 0.75 * load0(row, f, t) + stepped)

        def store3(row, f, t, stepped):
            row = row + 2
            ahead[(t * p.rows + row - HALO) * p.fields + f, mem, :] = third_part * load0(row, f, t) + stepped

        step_once(p, full, load0, store1, False, 1.0)
        step_once(p, full - 2, lambda row, f, t: s1[row + 1, f, t], store2, False, 0.25)
        step_once(p, full - 4, lambda row, f, t: s2[row + 2, f, t], store3, True, two_thirds)
        if rest:
            ahead_copy(kk).start()
        return carry

    lax.fori_loop(0, parts, body, 0)

    wide = lane_ids((p.members, LANES))
    found = jnp.zeros((p.members, LANES), jnp.float32)
    every = p.groups * p.slots
    for j in range(p.np):
        at = ((p.first_patch + j) ^ me) * p.slots
        for o in range(p.slots):
            to = j * p.slots + o
            found = jnp.where(wide == to, pltpu.roll(ahead[table[at + o]], table[every + at + o], 1), found)
    seen[...] = found

    share = 1.0 / p.members
    average = jnp.sum(found, axis=0, keepdims=True) * share
    high, low_part = (a.astype(jnp.float32) for a in split(found - average))
    turned = jnp.transpose(jnp.concatenate([high, high, low_part], axis=0))
    weigh = jnp.transpose(jnp.broadcast_to(average * p.members, (SUB, LANES)))
    sides = [turned[j * p.slots : (j + 1) * p.slots].astype(jnp.bfloat16) for j in range(p.np)]
    weighs = [weigh[j * p.slots : (j + 1) * p.slots, 0:1] for j in range(p.np)]
    lanes = lane_ids((p.slots, LANES))
    moments = jnp.zeros((p.slots, LANES), jnp.float32)
    joined = jnp.concatenate([a.astype(jnp.bfloat16) for a in (high, low_part, high)], axis=0)
    for j in range(p.np):
        part = jnp.dot(sides[j], joined, preferred_element_type=jnp.float32) + weighs[j] * average
        moments = jnp.where((lanes >= j * p.slots) & (lanes < (j + 1) * p.slots), part, moments)
    for out in (keep, send):
        out[pl.ds(p.cell_rows, p.slots), :] = moments
        out[pl.ds(p.cell_rows + p.slots, SUB), :] = jnp.broadcast_to(average * p.members, (SUB, LANES))
    for side in range(p.halves):
        out = keep if side == 0 else send
        half = core if side == 0 else 1 - core
        for t in range(p.nt):
            base = t * p.block
            begin = (t * p.rows + half * p.hrows) * p.fields
            tiles = [ahead[begin + i] for i in range(p.hrf)]
            means = [jnp.sum(x, axis=0, keepdims=True) * share for x in tiles]
            high, low_part = split(jnp.concatenate([x - m for x, m in zip(tiles, means)], axis=1))
            joined = jnp.concatenate([high, low_part, high], axis=0)
            line = jnp.concatenate(means, axis=1)
            result = None
            for j, first, stop in p.patches_of(t):
                part = jnp.dot(sides[j], joined, preferred_element_type=jnp.float32) + weighs[j] * line
                if result is None:
                    result = part
                else:
                    at = lane_ids(part.shape) % LANES
                    result = jnp.where((at >= first) & (at < stop), part, result)
            for i in range(p.hrf):
                out[pl.ds(base + i * p.slots, p.slots), :] = result[:, i * LANES : (i + 1) * LANES]
                out[pl.ds(base + p.hrf * p.slots + i, 1), :] = means[i] * p.members
            for i in range(p.hrf, p.plain):
                out[pl.ds(base + p.hrf * p.slots + i, 1), :] = jnp.zeros((1, LANES), jnp.float32)
    if rest:
        for kk in range(parts):
            ahead_copy(kk).wait()


def solve_kernel(plan, obs, seen, own, factors, centres, keeps):
    p = plan
    n = p.slots
    me = lax.axis_index("mem")
    free = p.total - 1.0
    shape = (n, LANES)
    lane = lane_ids(shape)
    row = lax.broadcasted_iota(jnp.int32, shape, 0)
    group = lane // n * n
    eye = jnp.where(lane - group == row, 1.0, 0.0).astype(jnp.float32)
    lane_row = lane_ids((1, LANES))
    lane_sub = lane_ids((SUB, LANES))

    def pick(a, index):
        return jnp.take_along_axis(a, index, axis=1)

    def col(a):
        return pick(jnp.broadcast_to(a, shape), group + row)

    def spread_out(a):
        base = lane_ids(a.shape) // n * n
        return [pick(a, base + k) for k in range(n)]

    def product(parts, b):
        terms = [parts[k] * b[k : k + 1] for k in range(n)]
        while len(terms) > 1:
            terms = [sum(terms[i : i + 2][1:], terms[i]) for i in range(0, len(terms), 2)]
        return terms[0]

    given = [jnp.zeros((SUB, LANES), jnp.float32) for _ in range(4)]
    for j in range(p.np):
        source = (p.first_patch + j) ^ me
        line = jnp.broadcast_to(obs[pl.ds(source, 1), :], (SUB, LANES))
        mine = (lane_sub >= j * n) & (lane_sub < (j + 1) * n)
        for i, place in enumerate((0, 1, 2, 4)):
            given[i] = jnp.where(mine, pltpu.roll(line, (j * n - place * n) % LANES, 1), given[i])
    moments = own[pl.ds(p.cell_rows, n), :]
    sums = own[pl.ds(p.cell_rows + n, SUB), :]
    value, variance, loop, count = (a[0:1] for a in given)
    mean = sums[0:1] * (1.0 / p.total)
    slot = (lane_row % n).astype(jnp.float32)
    used = lane_row < p.np * n
    weight = jnp.where(used & (slot < count), jnp.exp(-0.35 * loop) / jnp.where(used, variance, 1.0), 0.0)
    root = jnp.sqrt(weight)
    root_col = col(root)
    mean_col = col(mean)
    scaled = root_col * (moments - p.total * mean_col * mean) * root
    bound = free + 0.5 * jnp.sum(pick(scaled, group + row), axis=0, keepdims=True)
    inverse = 1.0 / bound

    small = scaled * inverse
    t0 = free * inverse
    tf = t0 * eye + small
    tg = eye
    z0 = jnp.ones((1, LANES), jnp.float32)
    zg = None
    for repeat in range(NSI):
        f0 = 1.5 - 0.5 * t0
        ff = 1.5 * eye - 0.5 * tf
        parts = spread_out(ff)
        if zg is None:
            zg = -0.5 * z0 * tg
        else:
            zg = product(parts, zg) - 0.5 * z0 * tg
        z0 = z0 * f0
        if repeat < NSI - 1:
            square = product(parts, ff)
            bend = square - (0.5 * t0) * (ff + f0 * eye)
            tf = product(spread_out(square), tf)
            tg = bend if repeat == 0 else product(spread_out(bend), tg)
            t0 = t0 * f0 * f0
    zf = z0 * eye + product(spread_out(small), zg)
    scale = jnp.sqrt(free * inverse)
    spread = (scale * inverse) * root_col * zg * root
    down = root * (value - mean)
    for repeat in range(2):
        down = jnp.sum(zf * col(down), axis=0, keepdims=True)
    weights = product(spread_out(seen[...] - mean), spread) + root * down * inverse
    spread0 = scale * z0

    wide = lane_ids((p.members, LANES))
    high, low_part = (a.astype(jnp.float32) for a in split(weights))
    for j in range(p.np):
        here, there, last = (pltpu.roll(a, (i * n - j * n) % LANES, 1) for i, a in enumerate((high, high, low_part)))
        factors[j] = jnp.where(wide < n, here, jnp.where(wide < 2 * n, there, last))
        centres[j] = pick(jnp.broadcast_to(mean, shape), row + j * n)
        keeps[j] = pick(jnp.broadcast_to(spread0, (SUB, LANES)), jnp.full((SUB, LANES), j * n, jnp.int32))


def finish_kernel(plan, ahead, factors, centres, keeps, own, other, *rest):
    out, staged, sems = rest[-3:]
    p = plan
    n = p.slots
    core = lax.rem(lax.axis_index("mem"), 2)
    mixing = [(factors[j][:, : 3 * n].astype(jnp.bfloat16), centres[j], keeps[j][0:1]) for j in range(p.np)]

    def line_copy(r, f):
        cols = pl.ds(p.first * LANES, p.nt * LANES)
        return pltpu.make_async_copy(staged.at[r, f], out.at[:, f, r, cols], sems.at[r, f])

    for half in range(p.halves):
        at_own = half == core
        lines = [(half * p.hrows + i // p.fields, i % p.fields) for i in range(p.hrf)]
        for t in range(p.nt):
            pieces = []
            for i in range(p.hrf):
                at = t * p.block + i * n
                pieces.append(jnp.where(at_own, own[at : at + n, :], other[at : at + n, :]))
            at = t * p.block + p.hrf * n
            plain = jnp.where(at_own, own[at : at + p.plain, :], other[at : at + p.plain, :])
            results = []
            for j, first, stop in p.patches_of(t):
                mine, centre, keep0 = mixing[j]
                centred = [pieces[i] - centre * plain[i : i + 1, :] for i in range(p.hrf)]
                high, low_part = split(jnp.concatenate(centred, axis=1))
                joined = jnp.concatenate([high, low_part, high], axis=0)
                results.append((jnp.dot(mine, joined, preferred_element_type=jnp.float32), keep0, first, stop))
            for i, (r, f) in enumerate(lines):
                x = ahead[(t * p.rows + r) * p.fields + f]
                average = plain[i : i + 1, :] * (1.0 / p.total)
                final = None
                for update, keep0, first, stop in results:
                    part = (1.0 - keep0) * average + keep0 * x + update[:, i * LANES : (i + 1) * LANES]
                    if final is None:
                        final = part
                    else:
                        at = lane_ids(part.shape)
                        final = jnp.where((at >= first) & (at < stop), part, final)
                staged[r, f, :, t * LANES : (t + 1) * LANES] = final
        for r, f in lines:
            line_copy(r, f).start()
    for r in range(p.rows):
        for f in range(p.fields):
            line_copy(r, f).wait()


def core_sums(plan, keep, send):
    return keep + lax.ppermute(send, "mem", [(i, i ^ 1) for i in range(plan.groups)])


def sum_phase(plan, phase, total, waited=None):
    p = plan
    bits = [1 << i for i in range(1, p.groups.bit_length() - 1)]
    if phase >= len(bits):
        return total
    even = bits[phase]
    odd = bits[(phase + len(bits) // 2) % len(bits)]
    there = lax.ppermute(total, "mem", [(i, i ^ (odd if i & 1 else even)) for i in range(p.groups)])
    return (total if waited is None else after(total, waited)) + there


def last_sums(plan, total, waited=None):
    p = plan
    for phase in range(1, p.groups.bit_length() - 2):
        total = sum_phase(p, phase, total, waited)
    return total, lax.ppermute(total, "mem", [(i, i ^ 1) for i in range(p.groups)])


def after(value, *others):
    return lax.optimization_barrier((value,) + others)[0]


def per_device(ensemble, obs_value, obs_var, obs_cell, obs_loop, obs_count):
    groups = lax.axis_size("mem")
    bands = lax.axis_size("lat")
    slots = obs_cell.shape[-1]
    p = Plan(ensemble, slots, groups)
    chunks = [p.chunk(c) for c in range(len(p.counts))]
    f32 = jnp.float32
    shape = pltpu.VMEM

    given = (obs_value, obs_var, obs_loop, obs_cell)

    def pack(h, source):
        sent = (h.message, p.members, LANES)
        more = given if h.first == 0 else ()
        return call(
            functools.partial(pack_kernel, h),
            [pltpu.VMEM((p.rows, p.fields, p.members, (h.nt + 1) * LANES), f32), pltpu.HBM(sent, f32), pltpu.HBM(sent, f32)]
            + [pltpu.VMEM((1, LANES), f32) for _ in more[:1]],
            [HBM] * (1 + len(more)),
            [
                pltpu.VMEM(sent, f32),
                pltpu.VMEM(sent, f32),
                pltpu.VMEM((p.members, p.fields, p.rows, h.nt * LANES), f32),
                pltpu.VMEM((2, p.members, p.fields, p.rows, LANES), f32),
                pltpu.SemaphoreType.DMA((p.members // SUB, 3)),
                pltpu.SemaphoreType.DMA((p.members // SUB, 4)),
            ]
            + [pltpu.VMEM(a.shape, a.dtype) for a in more]
            + [pltpu.VMEM((SUB, LANES), f32) for _ in more[:1]]
            + [pltpu.SemaphoreType.DMA((len(more),)) for _ in more[:1]],
            out_specs=[VMEM, HBM, HBM] + [VMEM for _ in more[:1]],
            name="pack",
        )(*(pltpu.with_memory_space_constraint(a, pltpu.HBM) for a in (source,) + more))

    packed = [pack(chunks[0], ensemble)]
    obs = jnp.where(jnp.arange(LANES) < 4 * slots, packed[0][3], obs_count.astype(f32))
    bit = 1
    while bit < groups:
        step = 2 if bit == 1 or bit * 4 > groups else 4
        there = [lax.ppermute(obs, "mem", [(i, i ^ (bit * b)) for i in range(groups)]) for b in range(1, step)]
        obs = jnp.concatenate([obs] + there, axis=0)
        bit *= step

    packed += [pack(h, after(ensemble, obs)) for h in chunks[1:]]
    messages = [a for part in packed for a in part[1:3]]
    swaps = [[pair for i in range(begin, bands - 1, 2) for pair in ((i, i + 1), (i + 1, i))] for begin in range(2)]
    halo = [[lax.ppermute(messages[2 * c + i], "lat", swaps[i]) for i in range(2)] for c in range(len(chunks))]

    table = call(
        table_kernel,
        [pltpu.SMEM((2 * groups * slots,), jnp.int32)],
        [ANY],
        [pltpu.SemaphoreType.DMA],
        out_specs=[SMEM],
        name="places",
    )(places(p, chunks, lax.axis_index("mem"), obs[:, 3 * slots : 4 * slots].astype(jnp.int32)))[0]
    table = pltpu.with_memory_space_constraint(table, pltpu.SMEM)

    def near(x):
        return pltpu.with_memory_space_constraint(x, pltpu.VMEM)

    def far(x):
        return pltpu.with_memory_space_constraint(x, pltpu.HBM)

    parts = []
    early = None
    for c, h in enumerate(chunks):
        stage = (p.rows + 2 * HALO, p.fields, h.nt + 1, SUB, LANES)
        ahead, seen, keep, send = call(
            functools.partial(forecast_kernel, h),
            [
                (shape if c == len(chunks) - 1 else pltpu.HBM)((h.nt * p.rows * p.fields, p.members, LANES), f32),
                shape((p.members, LANES), f32),
                shape((h.total_rows, LANES), f32),
                shape((h.total_rows, LANES), f32),
            ],
            [SMEM, VMEM, ANY, ANY],
            [pltpu.VMEM((2 * HALO, p.fields, SUB, LANES), f32), pltpu.VMEM(stage, f32), pltpu.VMEM(stage, f32)]
            + [pltpu.VMEM((h.message, p.members, LANES), f32)] * 2
            + [pltpu.SemaphoreType.DMA((p.members // SUB, 2))]
            + (
                []
                if c == len(chunks) - 1
                else [
                    pltpu.VMEM((h.nt * p.rows * p.fields, p.members, LANES), f32),
                    pltpu.SemaphoreType.DMA((p.members // SUB,)),
                ]
            ),
            out_specs=[VMEM if c == len(chunks) - 1 else HBM] + [VMEM] * 3,
            cost=(1024, h.nt * (6 << 20) if c else 1024),
            name="forecast",
        )(table, near(packed[c][0] if early is None else after(packed[c][0], early)), *halo[c])
        if c == 0:
            early = lax.cond(
                obs_count[0, 0] >= 0,
                functools.partial(sum_phase, p, 0),
                lambda total: total,
                core_sums(p, keep, send),
            )
            parts.append((ahead, seen, early))
        else:
            if c == 1:
                first = last_sums(p, parts[0][2])
                send = after(send, first[0])
            early = send
            parts.append((ahead, seen, sum_phase(p, 0, core_sums(p, keep, send))))
    new = None
    for c, h in enumerate(chunks):
        ahead, seen, total = parts[c]
        own, other = first if c == 0 and len(chunks) > 1 else last_sums(p, total, new)
        new = finish(p, h, obs, (ahead, seen, own, other), new, ensemble.shape)
    return new


def finish(plan, h, obs, parts, new, whole):
    p = plan
    f32 = jnp.float32
    ahead, seen, own, other = parts

    def near(*arrays):
        return [pltpu.with_memory_space_constraint(a, pltpu.VMEM) for a in arrays]

    solved = call(
        functools.partial(solve_kernel, h),
        [
            pltpu.VMEM((h.np, p.members, LANES), f32),
            pltpu.VMEM((h.np, p.slots, LANES), f32),
            pltpu.VMEM((h.np, SUB, LANES), f32),
        ],
        [VMEM] * 3,
        cost=(1024, 6 << 20),
        name="solve",
    )(*near(obs, seen, own))
    before = [] if new is None else [new]
    return call(
        functools.partial(finish_kernel, h),
        pltpu.HBM(whole, f32),
        [VMEM] * 6 + [HBM] * len(before),
        [pltpu.VMEM((p.rows, p.fields, p.members, h.nt * LANES), f32), pltpu.SemaphoreType.DMA((p.rows, p.fields))],
        cost=(1024, h.nt * (4 << 20)),
        name="finish",
        out_specs=HBM,
        alias={6: 0} if before else {},
    )(*near(ahead, *solved, own, other), *before)


def solution(mesh):
    placed = (
        P("mem", None, "lat", None),
        P(None, ("mem", "lat"), None),
        P(None, ("mem", "lat"), None),
        P(None, ("mem", "lat"), None),
        P(None, ("mem", "lat"), None),
        P(None, ("mem", "lat")),
    )
    return jax.shard_map(
        per_device,
        mesh=mesh,
        in_specs=placed,
        out_specs=P("mem", None, "lat", None),
        check_vma=False,
    )
```
